256 devices in a mesh: context: 64 (over y_hi, z, x), tensor: 4 (over y_lo, core).
Axes of the slice: x: 4, y: 4 (y_hi: 2, y_lo: 2; y = y_hi * 2 + y_lo), z: 8, core: 2. Of those that a mesh axis runs over, the one named last changes fastest.
Arguments:
- mixer_values: bfloat16 [8192, 8192], P('context', 'tensor'), may hold values from -6 to 6
- gate_values: bfloat16 [8192, 8192], P('context', 'tensor'), may hold values from -6 to 6
- input_coefs: bfloat16 [8192, 512], P('context', 'tensor'), may hold values from -6 to 6
- output_coefs: bfloat16 [8192, 512], P('context', 'tensor'), may hold values from -0.5 to 0.5
- step_raw: bfloat16 [8192, 128], P('context', 'tensor')
- step_bias: float32 [128], P('tensor')
- decay_log: float32 [128], P('tensor'), as said below
- skip_gain: float32 [128], P('tensor'), may hold values from 0.5 to 1.5
- group_gain: float32 [8192], P('tensor'), may hold values from 0.5 to 1.5
- carry_state: float32 [128, 64, 128], P('tensor'), may hold values from -5 to 5
- out_weight: bfloat16 [8192, 4096], P('tensor', 'context'), may hold values from -0.0625 to 0.0625
- residual: bfloat16 [8192, 4096], P(('context', 'tensor')), may hold values from -6 to 6
- final_gain: float32 [4096], replicated, may hold values from 0.5 to 1.5
Outputs:
- layer_output: bfloat16 [8192, 4096], P('context')
The draws below stay inside these ranges and needn't reach their ends.
Inputs may be any that keep to these rules, and one draw needn't show every extreme that they name: Every head's decay coefficient exp(decay_log) is below one.
All inputs are finite; a program needn't handle non-finite values.
Results may differ from the reference program's by a relative error of at most 0.0042.
Values may be sent and summed in bfloat16 or wider, within the bound.
No kernel may reach another device: no remote copies, remote signals or barrier semaphores. Data moves between devices by JAX's collectives and lax.ppermute only.
A program may use at most 192 MiB of HBM per device.

```python
import jax
import jax.numpy as jnp
from jax import lax

D = 4096
HEADS = 128
HEAD_DIM = 64
STATE = 128
NGROUPS = 4
NORM_GROUPS = 4
SPAN = 128
WINDOW_TOKENS = 8192
N_TENSOR = 4


def head_rates(key):
    base = jax.random.fold_in(key, 7)
    pick_key, slow_key, fast_key, jitter_key = jax.random.split(base, 4)
    share = 0.5
    slow_heads = jax.random.uniform(pick_key, (HEADS,)) < share
    slow_rate = jax.random.uniform(slow_key, (HEADS,), minval=0.3, maxval=1.5) / WINDOW_TOKENS
    fast_rate = jax.random.uniform(fast_key, (HEADS,), minval=1.0 / 50.0, maxval=1.0 / 30.0)
    rate = jnp.where(slow_heads, slow_rate, fast_rate)
    jitter = jax.random.uniform(jitter_key, (HEADS,), minval=-0.5, maxval=0.5)
    return (rate, jitter)


def inverse_softplus_map(target):
    return target + jnp.log(-jnp.expm1(-target))


def draw_decay_log(key, part):
    rate, jitter = head_rates(key)
    return (0.5 * jnp.log(rate) + jitter).astype(jnp.float32)


def draw_step_bias(key, part):
    rate, jitter = head_rates(key)
    target = jnp.sqrt(rate) * jnp.exp(-jitter)
    return inverse_softplus_map(target).astype(jnp.float32)


def draw_step_raw(key, part):
    rate, jitter = head_rates(key)
    mixing_factor = jnp.sqrt(rate) * jnp.exp(jitter)
    offset_bias = inverse_softplus_map(jnp.sqrt(rate) * jnp.exp(-jitter))
    base = jax.random.fold_in(key, 11)
    drawn_key, pos_key, loss_key = jax.random.split(base, 3)
    unmodified_input = jax.random.uniform(drawn_key, (WINDOW_TOKENS, HEADS), minval=-0.7, maxval=0.7)
    spike_positions = jax.random.randint(pos_key, (16,), 0, WINDOW_TOKENS)
    spike_token_rows = jnp.any(jnp.arange(WINDOW_TOKENS)[:, None] == spike_positions[None, :], axis=1)
    objective_value = jax.random.uniform(loss_key, (WINDOW_TOKENS, HEADS), minval=0.2, maxval=0.5)
    spike_raw_values = inverse_softplus_map(objective_value / mixing_factor[None, :]) - offset_bias[None, :]
    spike_raw_values = jnp.maximum(spike_raw_values, 0.7)
    return jnp.where(spike_token_rows[:, None], spike_raw_values, unmodified_input).astype(jnp.bfloat16)


def block_scale(stream_key, dims, shards, least, top_value):
    def one(axis_at, shards_of):
        draws = jax.random.uniform(jax.random.fold_in(jax.random.fold_in(stream_key, 6), axis_at), (shards_of,), jnp.float32, least / len(shards), top_value / len(shards))
        return jnp.repeat(jnp.exp(draws), dims[axis_at] // shards_of).reshape((-1,) + (1,) * (len(dims) - axis_at - 1))

    gain = one(*shards[0])
    for cut in shards[1:]:
        gain = gain * one(*cut)
    return gain


def bell_draw(stream_key, shape, width, bound, shards=(), held_as=jnp.bfloat16):
    entries = width * jax.random.normal(stream_key, shape, jnp.float32)
    if shards:
        entries = entries * block_scale(stream_key, shape, shards, -0.22, 0.18)
    return jnp.clip(entries, -bound, bound).astype(held_as)


def setup_inputs(seed: int = 0) -> dict:
    key_list = jax.random.split(jax.random.key(seed), 14)
    mixer_values = bell_draw(key_list[0], (WINDOW_TOKENS, HEADS * HEAD_DIM), 1.0, 6.0, ((0, 64), (1, 4)))
    gate_values = bell_draw(key_list[1], (WINDOW_TOKENS, HEADS * HEAD_DIM), 1.0, 6.0, ((0, 64), (1, 4)))
    input_coefs = bell_draw(key_list[2], (WINDOW_TOKENS, NGROUPS * STATE), 1.0, 6.0, ((0, 64), (1, 4)))
    output_coefs = bell_draw(key_list[3], (WINDOW_TOKENS, NGROUPS * STATE), STATE ** -0.5, 0.5, ((0, 64), (1, 4)))
    step_raw = draw_step_raw(jax.random.fold_in(key_list[13], 71), 0)
    step_bias = draw_step_bias(jax.random.fold_in(key_list[13], 71), 0)
    decay_log = draw_decay_log(jax.random.fold_in(key_list[13], 71), 0)
    skip_gain = jnp.clip(0.5 + 1.0 * jax.random.uniform(key_list[7], (HEADS,), jnp.float32) ** block_scale(key_list[7], (HEADS,), ((0, 4),), -0.2, 0.2), 0.5, 1.5)
    group_gain = jnp.clip(1.0 + 0.1 * jax.random.normal(key_list[8], (HEADS * HEAD_DIM,), jnp.float32), 0.5, 1.5)
    carry_state = bell_draw(key_list[9], (HEADS, HEAD_DIM, STATE), 0.7, 5.0, ((0, 4),), jnp.float32)
    out_weight = bell_draw(key_list[10], (HEADS * HEAD_DIM, D), (HEADS * HEAD_DIM) ** -0.5, 0.0625, ((0, 4), (1, 64)))
    residual = bell_draw(key_list[11], (WINDOW_TOKENS, D), 1.0, 6.0, ((0, 256),))
    final_gain = jnp.clip(1.0 + 0.1 * jax.random.normal(key_list[12], (D,), jnp.float32), 0.5, 1.5)
    return {"mixer_values": mixer_values, "gate_values": gate_values, "input_coefs": input_coefs, "output_coefs": output_coefs, "step_raw": step_raw, "step_bias": step_bias, "decay_log": decay_log, "skip_gain": skip_gain, "group_gain": group_gain, "carry_state": carry_state, "out_weight": out_weight, "residual": residual, "final_gain": final_gain}


EPSILON = 1e-05
HIGHEST = lax.Precision.HIGHEST

def reference(mixer_values, gate_values, input_coefs, output_coefs, step_raw, step_bias, decay_log, skip_gain, group_gain, carry_state, out_weight, residual, final_gain):
    repeat = HEADS // NGROUPS
    blocks = WINDOW_TOKENS // SPAN
    inner_width = HEADS * HEAD_DIM
    shard_width = inner_width // N_TENSOR
    causal = jnp.arange(SPAN)[:, None] >= jnp.arange(SPAN)[None, :]

    def one_block(running, pieces):
        values, gates, incoming, outgoing, raw_steps, resid_rows = pieces
        step_size = jax.nn.softplus(raw_steps.astype(jnp.float32) + step_bias)
        cumulative = jnp.cumsum(-jnp.exp(decay_log) * step_size, axis=0)
        head_vals = values.astype(jnp.float32).reshape(SPAN, NGROUPS, repeat, HEAD_DIM)
        in_coefs = incoming.astype(jnp.float32).reshape(SPAN, NGROUPS, STATE)
        out_coefs = outgoing.astype(jnp.float32).reshape(SPAN, NGROUPS, STATE)
        steps_grouped = step_size.reshape(SPAN, NGROUPS, repeat)
        scores = jnp.einsum('ign,jgn->gij', out_coefs, in_coefs, precision=HIGHEST)
        by_head = cumulative.T.reshape(NGROUPS, repeat, SPAN)
        log_gaps = by_head[..., :, None] - by_head[..., None, :]
        within = jnp.exp(jnp.where(causal, log_gaps, -jnp.inf))
        weights = scores[:, None] * within * jnp.transpose(steps_grouped, (1, 2, 0))[:, :, None, :]
        diagonal = jnp.einsum('grij,jgrp->igrp', weights, head_vals, precision=HIGHEST)
        carried = jnp.einsum('ign,grpn->igrp', out_coefs, running.reshape(NGROUPS, repeat, HEAD_DIM, STATE), precision=HIGHEST)
        carried = carried * jnp.exp(cumulative).reshape(SPAN, NGROUPS, repeat)[..., None]
        mixer_out = (diagonal + carried + skip_gain.reshape(NGROUPS, repeat)[:, :, None] * head_vals).reshape(SPAN, inner_width)
        block_log = cumulative[-1]
        to_end = jnp.exp(block_log[None, :] - cumulative).reshape(SPAN, NGROUPS, repeat)
        fresh_terms = jnp.einsum('jgrp,jgn->grpn', head_vals * (steps_grouped * to_end)[..., None], in_coefs, precision=HIGHEST)
        updated = jnp.exp(block_log)[:, None, None] * running + fresh_terms.reshape(HEADS, HEAD_DIM, STATE)
        gated_out = mixer_out * jax.nn.silu(gates.astype(jnp.float32))
        grouped = gated_out.reshape(SPAN, NORM_GROUPS, -1)
        normed = grouped * lax.rsqrt(lax.optimization_barrier(jnp.mean(grouped * grouped, axis=-1, keepdims=True)) + EPSILON)
        normed = (normed.reshape(SPAN, inner_width) * group_gain).astype(jnp.bfloat16)
        summed = jnp.zeros((SPAN, D), jnp.float32)
        for member in range(N_TENSOR):
            shard_term = jnp.dot(normed[:, member * shard_width:(member + 1) * shard_width], out_weight[member * shard_width:(member + 1) * shard_width], preferred_element_type=jnp.float32)
            summed = summed + shard_term
        combined = resid_rows.astype(jnp.float32) + summed
        output = combined * lax.rsqrt(lax.optimization_barrier(jnp.mean(combined * combined, axis=-1, keepdims=True)) + EPSILON) * final_gain
        return (updated, output.astype(jnp.bfloat16))
    pieces = (mixer_values.reshape(blocks, SPAN, inner_width), gate_values.reshape(blocks, SPAN, inner_width), input_coefs.reshape(blocks, SPAN, NGROUPS * STATE), output_coefs.reshape(blocks, SPAN, NGROUPS * STATE), step_raw.reshape(blocks, SPAN, HEADS), residual.reshape(blocks, SPAN, D))
    final_state, outputs = lax.scan(one_block, carry_state.astype(jnp.float32), pieces)
    return outputs.reshape(WINDOW_TOKENS, D)
```

```python
import functools

import jax
import jax.numpy as jnp
from jax import lax
from jax.experimental import pallas as pl
from jax.experimental.pallas import tpu as pltpu
from jax.sharding import Mesh, PartitionSpec as P

EPSILON = 1e-05
HIGHEST = lax.Precision.HIGHEST
SPAN = 128
STATE = 128
HEAD_DIM = 64
EXTRA = 8
BF16, F32 = jnp.bfloat16, jnp.float32
CONTEXT = ("yh", "z", "x")
TENSOR = ("yl", "core")
SLICES = ("z", "x")
VMEM_LIMIT = 48 * 2**20


def call(kernel, outs, *, scratch=(), flops=0, smem=0, args=()):
    specs = [pl.BlockSpec(memory_space=pltpu.SMEM)] * smem
    specs += [pl.BlockSpec(memory_space=pltpu.VMEM)] * (len(args) - smem)
    moved = sum(a.size * a.dtype.itemsize for a in (*args, *jax.tree.leaves(outs)))
    return pl.pallas_call(
        kernel,
        out_shape=outs,
        in_specs=specs,
        out_specs=jax.tree.map(lambda _: pl.BlockSpec(memory_space=pltpu.VMEM), outs),
        scratch_shapes=scratch,
        compiler_params=pltpu.CompilerParams(vmem_limit_bytes=VMEM_LIMIT),
        cost_estimate=pl.CostEstimate(flops=flops, bytes_accessed=moved, transcendentals=0),
    )(*args)


def dot(a, b, precision=None):
    return lax.dot_general(
        a, b, (((1,), (0,)), ((), ())), precision=precision, preferred_element_type=F32
    )


def steps_of(raw, bias, decay_log):
    v = raw.astype(F32) + bias
    step = jnp.maximum(v, 0.0) + jnp.log1p(jnp.exp(-jnp.abs(v)))
    rows = lax.broadcasted_iota(jnp.int32, (SPAN, SPAN), 0)
    columns = lax.broadcasted_iota(jnp.int32, (SPAN, SPAN), 1)
    lower = jnp.where(rows >= columns, 1.0, 0.0).astype(F32)
    cumulative = dot(lower, -jnp.exp(decay_log) * step, HIGHEST)
    return step, cumulative


def split(a):
    high = a.astype(BF16)
    return high, (a - high.astype(F32)).astype(BF16)


def first_lanes(shape):
    return lax.broadcasted_iota(jnp.int32, shape, len(shape) - 1) < HEAD_DIM


def column(a, h):
    return jnp.broadcast_to(a[:, h : h + 1], (a.shape[0], 2 * HEAD_DIM))


def states_kernel(x_ref, b_ref, raw_ref, bias_ref, decay_ref, out_ref):
    step, cumulative = steps_of(raw_ref[...], bias_ref[...], decay_ref[...])
    last = cumulative[SPAN - 1 : SPAN, :]
    weight = step * jnp.exp(last - cumulative)
    b_t = jnp.transpose(b_ref[...])
    b_twice = jnp.concatenate([b_t, b_t], axis=1)
    low = first_lanes((SPAN, SPAN))
    for pair in range(step.shape[1] // 2):
        lanes = slice(pair * SPAN, (pair + 1) * SPAN)
        scale = jnp.where(low, column(weight, 2 * pair), column(weight, 2 * pair + 1))
        scaled = x_ref[:, lanes].astype(F32) * scale
        state = dot(b_twice, jnp.concatenate(split(scaled), axis=0))
        log = jnp.where(
            low[:1], column(last, 2 * pair), column(last, 2 * pair + 1)
        )
        for half in range(2):
            rows = slice(half * (STATE // 2), (half + 1) * (STATE // 2))
            out_ref[2 * pair + half, : STATE // 2, :] = state[rows]
            out_ref[2 * pair + half, STATE // 2 :, :] = jnp.broadcast_to(log, (EXTRA, SPAN))


def decay_and_state(parts_ref, k):
    decay = jnp.exp(parts_ref[k, STATE // 2 : STATE // 2 + 1, :])
    return decay, parts_ref[k, : STATE // 2, :]


def end_kernel(parts_ref, carry_ref, out_ref):
    run = carry_ref[...]
    for k in range(parts_ref.shape[0]):
        decay, state = decay_and_state(parts_ref, k)
        run = decay * run + state
    out_ref[...] = run


def enter_kernel(late_ref, parts_ref, carry_ref, sent_ref, out_ref):
    run = jnp.where(late_ref[0] > 0, sent_ref[...], carry_ref[...])
    for k in range(parts_ref.shape[0]):
        out_ref[k] = run
        decay, state = decay_and_state(parts_ref, k)
        run = decay * run + state


def mix_kernel(
    x_ref, gate_ref, b_ref, c_ref, raw_ref, bias_ref, decay_ref, skip_ref, gain_ref, state_ref, out_ref, gated_ref
):
    step, cumulative = steps_of(raw_ref[...], bias_ref[...], decay_ref[...])
    step_t, cumulative_t = jnp.transpose(step), jnp.transpose(cumulative)
    scores = lax.dot_general(
        c_ref[...], b_ref[...], (((1,), (1,)), ((), ())), preferred_element_type=F32
    )
    rows = lax.broadcasted_iota(jnp.int32, (SPAN, SPAN), 0)
    columns = lax.broadcasted_iota(jnp.int32, (SPAN, SPAN), 1)
    causal = rows >= columns
    low = first_lanes((SPAN, SPAN))
    c_twice = jnp.concatenate([c_ref[...], c_ref[...]], axis=1)
    squares = jnp.zeros((SPAN, SPAN), F32)
    pairs = step.shape[1] // 2
    for pair in range(pairs):
        lanes = slice(pair * SPAN, (pair + 1) * SPAN)
        x = x_ref[:, lanes]
        at, weights = [], []
        for h in (2 * pair, 2 * pair + 1):
            here = column(cumulative, h)
            within = jnp.exp(jnp.where(causal, here - cumulative_t[h : h + 1, :], -jnp.inf))
            at.append(here)
            weights.append(jnp.concatenate(split(scores * within * step_t[h : h + 1, :]), axis=1))
        both = dot(jnp.concatenate(weights, axis=0), jnp.concatenate([x, x], axis=0))
        carried = dot(c_twice, jnp.concatenate(split(state_ref[lanes, :]), axis=0))
        mixed = (
            jnp.where(low, both[:SPAN], both[SPAN:])
            + carried * jnp.exp(jnp.where(low, at[0], at[1]))
            + skip_ref[:, lanes] * x.astype(F32)
        )
        gate = gate_ref[:, lanes].astype(F32)
        gated = mixed * (gate / (1.0 + jnp.exp(-gate)))
        gated_ref[:, lanes] = gated
        squares += gated * gated
    width = pairs * SPAN
    root = lax.rsqrt(jnp.sum(squares, axis=-1, keepdims=True) / width + EPSILON)
    for pair in range(pairs):
        lanes = slice(pair * SPAN, (pair + 1) * SPAN)
        out_ref[:, lanes] = (gated_ref[:, lanes] * root * gain_ref[:, lanes]).astype(BF16)


def project_kernel(place_ref, own_ref, left_ref, right_ref, far_a_ref, far_b_ref, weight_ref, out_ref):
    def one(a, row):
        product = lax.dot_general(
            a, weight_ref[...], (((1,), (1,)), ((), ())), preferred_element_type=F32
        )
        out_ref[pl.ds(pl.multiple_of(row, SPAN // 2), a.shape[0]), :] = product.astype(BF16)

    one(own_ref[...], place_ref[0] * SPAN)
    one(left_ref[...], place_ref[1] * SPAN)
    one(right_ref[...], place_ref[2] * SPAN)
    one(far_a_ref[...], place_ref[3] * SPAN)
    one(far_b_ref[...], place_ref[3] * SPAN + SPAN // 2)


def finish_kernel(late_ref, parts_ref, residual_ref, gain_ref, out_ref, combined_ref, *, n_x, n_t, n_z):
    late = late_ref[0] > 0
    tokens = residual_ref.shape[0]
    sums = []
    for x in range(n_x):
        total = parts_ref[x * n_t].astype(F32)
        for t in range(1, n_t):
            total += parts_ref[x * n_t + t].astype(F32)
        sums.append(total)
    squares = jnp.zeros((tokens, 2 * HEAD_DIM), F32)
    for z in range(n_z):
        piece = slice(z * 2 * HEAD_DIM, (z + 1) * 2 * HEAD_DIM)
        own = [total[:, piece] for total in sums]
        swapped = [jnp.concatenate([a[:, HEAD_DIM:], a[:, :HEAD_DIM]], axis=1) for a in own]
        ordered = [jnp.where(late, b, a) for a, b in zip(own, swapped)]
        for yh in range(2):
            for x in range(0, n_x, 2):
                block = ((yh * n_z + z) * n_x + x) // 2
                lanes = slice(block * 2 * HEAD_DIM, (block + 1) * 2 * HEAD_DIM)
                half = slice(yh * HEAD_DIM, (yh + 1) * HEAD_DIM)
                both = jnp.concatenate([ordered[x][:, half], ordered[x + 1][:, half]], axis=1)
                combined = residual_ref[:, lanes].astype(F32) + both
                combined_ref[:, lanes] = combined
                squares += combined * combined
    root = lax.rsqrt(jnp.sum(squares, axis=-1, keepdims=True) / combined_ref.shape[1] + EPSILON)
    out_ref[...] = (combined_ref[...] * root * gain_ref[...]).astype(BF16)


def ring(n, by):
    return [(i, (i + by) % n) for i in range(n)]


def on_device(
    mixer_values,
    gate_values,
    input_coefs,
    output_coefs,
    step_raw,
    step_bias,
    decay_log,
    skip_gain,
    group_gain,
    carry_state,
    out_weight,
    residual,
    final_gain,
):
    tokens, inner = mixer_values.shape
    heads = step_raw.shape[1]
    n_z, n_x = lax.axis_size("z"), lax.axis_size("x")
    n_t = lax.axis_size("yl") * lax.axis_size("core")
    slices = n_z * n_x
    at_x = lax.axis_index("x")
    late = lax.axis_index("yh").astype(jnp.int32).reshape(1)
    bias, decay = step_bias.reshape(1, heads), decay_log.reshape(1, heads)
    skip = jnp.repeat(skip_gain, HEAD_DIM).reshape(1, inner)

    weight = out_weight.T
    weight = jnp.concatenate([weight, lax.ppermute(weight, "yh", ring(2, 1))], axis=0)
    weight = lax.all_gather(weight, "z", axis=0, tiled=True)

    half = STATE // 2
    states = call(
        states_kernel,
        jax.ShapeDtypeStruct((slices, half + EXTRA, 2 * HEAD_DIM), F32),
        flops=2 * tokens * inner * STATE * 2,
        args=(mixer_values, input_coefs, step_raw, bias, decay),
    )
    parts = lax.all_to_all(states, SLICES, 0, 0, tiled=True)

    mine = lax.axis_index(SLICES)
    pair = lax.dynamic_index_in_dim(carry_state.reshape(heads // 2, 2 * HEAD_DIM, STATE), mine // 2, 0, False)
    carry = lax.dynamic_slice_in_dim(pair.T, (mine % 2) * half, half, 0)
    ends = call(
        end_kernel, jax.ShapeDtypeStruct(carry.shape, F32), flops=10**6, args=(parts, carry)
    )
    sent = lax.ppermute(ends, "yh", [(0, 1)])
    entering = call(
        enter_kernel,
        jax.ShapeDtypeStruct((slices, half, 2 * HEAD_DIM), F32),
        flops=10**6,
        smem=1,
        args=(late, parts, carry, sent),
    )
    entering = lax.all_to_all(entering, SLICES, 0, 0, tiled=True).reshape(slices * half, 2 * HEAD_DIM)

    normed = call(
        mix_kernel,
        jax.ShapeDtypeStruct((tokens, inner), BF16),
        scratch=[pltpu.VMEM((tokens, inner), F32)],
        flops=2 * tokens * inner * tokens * 4,
        args=(
            mixer_values,
            gate_values,
            input_coefs,
            output_coefs,
            step_raw,
            bias,
            decay,
            skip,
            group_gain.reshape(1, inner),
            entering,
        ),
    )
    left = lax.ppermute(normed, "x", ring(n_x, 1))
    right = lax.ppermute(normed, "x", ring(n_x, -1))
    far_a = lax.ppermute(left[: tokens // 2], "x", ring(n_x, 1))
    far_b = lax.ppermute(right[tokens // 2 :], "x", ring(n_x, -1))
    place = (at_x + jnp.array([0, n_x - 1, 1, 2], jnp.int32)) % n_x
    partial = call(
        project_kernel,
        jax.ShapeDtypeStruct((n_x * tokens, weight.shape[0]), BF16),
        flops=2 * n_x * tokens * inner * weight.shape[0],
        smem=1,
        args=(place, normed, left, right, far_a, far_b, weight),
    )
    partial = lax.all_to_all(partial, ("x", *TENSOR), 0, 0, tiled=True)
    rows = residual.shape[0]
    done = call(
        functools.partial(finish_kernel, n_x=n_x, n_t=n_t, n_z=n_z),
        jax.ShapeDtypeStruct(residual.shape, BF16),
        scratch=[pltpu.VMEM(residual.shape, F32)],
        flops=10**6,
        smem=1,
        args=(late, partial.reshape(n_x * n_t, rows, weight.shape[0]), residual, final_gain.reshape(1, -1)),
    )
    across = lax.ppermute(done, "yl", ring(2, 1))
    mine_two = jnp.stack([done, across])
    theirs_two = lax.ppermute(mine_two, "core", ring(2, 1))
    first_y, first_core = lax.axis_index("yl") == 0, lax.axis_index("core") == 0
    even = jnp.where(first_core, mine_two, theirs_two)
    odd = jnp.where(first_core, theirs_two, mine_two)
    low = jnp.where(first_y, jnp.stack([even[0], odd[0]]), jnp.stack([even[1], odd[1]]))
    high = jnp.where(first_y, jnp.stack([even[1], odd[1]]), jnp.stack([even[0], odd[0]]))
    return jnp.concatenate([low, high]).reshape(tokens, residual.shape[1])


def solution(mesh):
    fine = Mesh(mesh.devices.reshape(2, 8, 4, 2, 2), (*CONTEXT, *TENSOR))
    return jax.shard_map(
        on_device,
        mesh=fine,
        in_specs=(
            P(CONTEXT, TENSOR),
            P(CONTEXT, TENSOR),
            P(CONTEXT, TENSOR),
            P(CONTEXT, TENSOR),
            P(CONTEXT, TENSOR),
            P(TENSOR),
            P(TENSOR),
            P(TENSOR),
            P(TENSOR),
            P(TENSOR, None, None),
            P(TENSOR, CONTEXT),
            P((*CONTEXT, *TENSOR), None),
            P(),
        ),
        out_specs=P(CONTEXT, None),
        check_vma=False,
    )
```

```python
import functools

import jax
import jax.numpy as jnp
from jax import lax
from jax.experimental import pallas as pl
from jax.experimental.pallas import tpu as pltpu
from jax.sharding import Mesh, PartitionSpec as P

EPSILON = 1e-05
HIGHEST = lax.Precision.HIGHEST
SPAN = 128
STATE = 128
HEAD_DIM = 64
EXTRA = 8
BF16, F32 = jnp.bfloat16, jnp.float32
CONTEXT = ("yh", "z", "x")
TENSOR = ("yl", "core")
GROUPS = ("yh", "z")
VMEM_LIMIT = 14 * 2**20


def call(kernel, outs, *, scratch=(), flops=0, smem=0, hbm=0, args=()):
    specs = [pl.BlockSpec(memory_space=pltpu.SMEM)] * smem
    specs += [pl.BlockSpec(memory_space=pltpu.VMEM)] * (len(args) - smem - hbm)
    specs += [pl.BlockSpec(memory_space=pl.ANY)] * hbm
    moved = sum(a.size * a.dtype.itemsize for a in (*args, *jax.tree.leaves(outs)))
    return pl.pallas_call(
        kernel,
        out_shape=outs,
        in_specs=specs,
        out_specs=jax.tree.map(lambda _: pl.BlockSpec(memory_space=pltpu.VMEM), outs),
        scratch_shapes=scratch,
        compiler_params=pltpu.CompilerParams(vmem_limit_bytes=VMEM_LIMIT),
        cost_estimate=pl.CostEstimate(flops=flops, bytes_accessed=moved, transcendentals=0),
    )(*args)


def dot(a, b, precision=None):
    return lax.dot_general(
        a, b, (((1,), (0,)), ((), ())), precision=precision, preferred_element_type=F32
    )


def steps_of(raw, bias, decay_log):
    v = raw.astype(F32) + bias
    step = jnp.maximum(v, 0.0) + jnp.log1p(jnp.exp(-jnp.abs(v)))
    rows = lax.broadcasted_iota(jnp.int32, (SPAN, SPAN), 0)
    columns = lax.broadcasted_iota(jnp.int32, (SPAN, SPAN), 1)
    lower = jnp.where(rows >= columns, 1.0, 0.0).astype(F32)
    cumulative = dot(lower, -jnp.exp(decay_log) * step, HIGHEST)
    return step, cumulative


def split(a):
    high = a.astype(BF16)
    return high, (a - high.astype(F32)).astype(BF16)


def first_lanes(shape):
    return lax.broadcasted_iota(jnp.int32, shape, len(shape) - 1) < HEAD_DIM


def column(a, h):
    return jnp.broadcast_to(a[:, h : h + 1], (a.shape[0], 2 * HEAD_DIM))


def group_columns(ref):
    inner = (ref.shape[1] - 3 * SPAN) // 2
    x, gate = ref.at[:, :inner], ref.at[:, inner : 2 * inner]
    b, c, raw = (ref.at[:, 2 * inner + i * SPAN : 2 * inner + (i + 1) * SPAN] for i in range(3))
    return x, gate, b, c, raw


def fresh_states(x_ref, b, step, cumulative):
    last = cumulative[SPAN - 1 : SPAN, :]
    weight = step * jnp.exp(last - cumulative)
    b_t = jnp.transpose(b)
    b_twice = jnp.concatenate([b_t, b_t], axis=1)
    low = first_lanes((SPAN, SPAN))
    for pair in range(x_ref.shape[1] // SPAN):
        lanes = slice(pair * SPAN, (pair + 1) * SPAN)
        scale = jnp.where(low, column(weight, 2 * pair), column(weight, 2 * pair + 1))
        scaled = x_ref[:, lanes].astype(F32) * scale
        state = dot(b_twice, jnp.concatenate(split(scaled), axis=0))
        log = jnp.where(low[:1], column(last, 2 * pair), column(last, 2 * pair + 1))
        yield pair, state, log


def states_kernel(x_ref, b_ref, raw_ref, bias_ref, decay_ref, out_ref):
    step, cumulative = steps_of(raw_ref[...], bias_ref[...], decay_ref[...])
    each = out_ref.shape[1] // SPAN
    for pair, state, log in fresh_states(x_ref, b_ref[...], step, cumulative):
        member, at = divmod(pair, each)
        out_ref[member, at * STATE : (at + 1) * STATE, :] = state
        out_ref[member, each * STATE + at : each * STATE + at + 1, :] = log


def group_kernel(parts_ref, out_ref):
    members, rows, _ = parts_ref.shape
    pairs = rows // STATE
    slices, size = out_ref.shape[0], out_ref.shape[1] - EXTRA
    for pair in range(pairs):
        here = slice(pair * STATE, (pair + 1) * STATE)
        at = pairs * STATE + pair
        log = parts_ref[0, at : at + 1, :]
        state = parts_ref[0, here, :]
        for member in range(1, members):
            more = parts_ref[member, at : at + 1, :]
            state = jnp.exp(more) * state + parts_ref[member, here, :]
            log = log + more
        for i in range(STATE // size):
            out_ref[pair * (STATE // size) + i, :size, :] = state[i * size : (i + 1) * size]
            out_ref[pair * (STATE // size) + i, size:, :] = jnp.broadcast_to(log, (EXTRA, SPAN))


def enter_kernel(parts_ref, carry_ref, out_ref):
    size = out_ref.shape[1]
    run = carry_ref[...]
    for k in range(parts_ref.shape[0]):
        out_ref[k] = run
        run = jnp.exp(parts_ref[k, size : size + 1, :]) * run + parts_ref[k, :size, :]


def local_kernel(block_ref, bias_ref, decay_ref, skip_ref, mixed_ref, state_ref, log_ref):
    x_ref, _, b_ref, c_ref, raw_ref = group_columns(block_ref)
    heads = bias_ref.shape[1]
    step, cumulative = steps_of(raw_ref[...][:, :heads], bias_ref[...], decay_ref[...])
    step_t, cumulative_t = jnp.transpose(step), jnp.transpose(cumulative)
    scores = lax.dot_general(
        c_ref[...], b_ref[...], (((1,), (1,)), ((), ())), preferred_element_type=F32
    )
    rows = lax.broadcasted_iota(jnp.int32, (SPAN, SPAN), 0)
    columns = lax.broadcasted_iota(jnp.int32, (SPAN, SPAN), 1)
    causal = rows >= columns
    low = first_lanes((SPAN, SPAN))
    for pair, state, log in fresh_states(x_ref, b_ref[...], step, cumulative):
        lanes = slice(pair * SPAN, (pair + 1) * SPAN)
        state_ref[lanes, :] = state
        log_ref[pair : pair + 1, :] = log
        x = x_ref[:, lanes]
        weights = []
        for h in (2 * pair, 2 * pair + 1):
            gap = column(cumulative, h) - cumulative_t[h : h + 1, :]
            within = jnp.exp(jnp.where(causal, gap, -jnp.inf))
            weights.append(jnp.concatenate(split(scores * within * step_t[h : h + 1, :]), axis=1))
        both = dot(jnp.concatenate(weights, axis=0), jnp.concatenate([x, x], axis=0))
        mixed_ref[:, lanes] = jnp.where(low, both[:SPAN], both[SPAN:]) + skip_ref[:, lanes] * x.astype(F32)


def mix_kernel(place_ref, entering_ref, bias_ref, decay_ref, gain_ref, *refs):
    operands, (out_ref, enter_ref, logs_ref, mixed_ref, gated_ref, semaphores) = refs[:-6], refs[-6:]
    n = len(operands) // 4
    blocks, logs, states, mixed = (operands[i * n : (i + 1) * n] for i in range(4))
    pairs = entering_ref.shape[0] // SPAN
    state_copies = [
        pltpu.make_async_copy(states[i], enter_ref.at[place_ref[i]], semaphores.at[i]) for i in range(n)
    ]
    mixed_copies = [
        pltpu.make_async_copy(mixed[i], mixed_ref.at[i], semaphores.at[n + i]) for i in range(n)
    ]
    for copy in (*state_copies, *mixed_copies):
        copy.start()
    for i in range(n):
        logs_ref[place_ref[i]] = logs[i][...]
    for copy in state_copies:
        copy.wait()
    for pair in range(pairs):
        lanes = slice(pair * SPAN, (pair + 1) * SPAN)
        run = entering_ref[lanes, :]
        for p in range(n):
            fresh = enter_ref[p, lanes, :]
            enter_ref[p, lanes, :] = run
            run = jnp.exp(logs_ref[p, pair : pair + 1, :]) * run + fresh
    heads = bias_ref.shape[1]
    low = first_lanes((SPAN, SPAN))
    for i, block_ref in enumerate(blocks):
        mixed_copies[i].wait()
        _, gate_ref, _, c_ref, raw_ref = group_columns(block_ref)
        _, cumulative = steps_of(raw_ref[...][:, :heads], bias_ref[...], decay_ref[...])
        c_twice = jnp.concatenate([c_ref[...], c_ref[...]], axis=1)
        squares = jnp.zeros((SPAN, SPAN), F32)
        place = place_ref[i]
        for pair in range(pairs):
            lanes = slice(pair * SPAN, (pair + 1) * SPAN)
            at = jnp.where(low, column(cumulative, 2 * pair), column(cumulative, 2 * pair + 1))
            carried = dot(c_twice, jnp.concatenate(split(enter_ref[place, lanes, :]), axis=0))
            mixed = mixed_ref[i, :, lanes] + carried * jnp.exp(at)
            gate = gate_ref[:, lanes].astype(F32)
            gated = mixed * (gate / (1.0 + jnp.exp(-gate)))
            gated_ref[:, lanes] = gated
            squares += gated * gated
        root = lax.rsqrt(jnp.sum(squares, axis=-1, keepdims=True) / (pairs * SPAN) + EPSILON)
        to = pl.ds(pl.multiple_of(place * SPAN, SPAN), SPAN)
        for pair in range(pairs):
            lanes = slice(pair * SPAN, (pair + 1) * SPAN)
            out_ref[to, lanes] = (gated_ref[:, lanes] * root * gain_ref[:, lanes]).astype(BF16)


def project_kernel(tokens_ref, weight_ref, out_ref):
    product = lax.dot_general(
        tokens_ref[...], weight_ref[...], (((1,), (1,)), ((), ())), preferred_element_type=F32
    )
    out_ref[...] = product.astype(BF16)


def project(tokens, weight, tile=256):
    rows, depth = tokens.shape
    columns = weight.shape[0]
    return pl.pallas_call(
        project_kernel,
        grid=(columns // tile,),
        out_shape=jax.ShapeDtypeStruct((rows, columns), BF16),
        in_specs=[pl.BlockSpec((rows, depth), lambda i: (0, 0)), pl.BlockSpec((tile, depth), lambda i: (i, 0))],
        out_specs=pl.BlockSpec((rows, tile), lambda i: (0, i)),
        compiler_params=pltpu.CompilerParams(vmem_limit_bytes=VMEM_LIMIT),
        cost_estimate=pl.CostEstimate(
            flops=2 * rows * depth * columns, bytes_accessed=weight.size * 2, transcendentals=0
        ),
    )(tokens, weight)


def finish_kernel(late_ref, parts_ref, residual_ref, gain_ref, out_ref, combined_ref, *, n_x, n_t, n_z):
    late = late_ref[0] > 0
    tokens = residual_ref.shape[0]
    sums = []
    for x in range(n_x):
        total = parts_ref[x * n_t].astype(F32)
        for t in range(1, n_t):
            total += parts_ref[x * n_t + t].astype(F32)
        sums.append(total)
    squares = jnp.zeros((tokens, 2 * HEAD_DIM), F32)
    for z in range(n_z):
        piece = slice(z * 2 * HEAD_DIM, (z + 1) * 2 * HEAD_DIM)
        own = [total[:, piece] for total in sums]
        swapped = [jnp.concatenate([a[:, HEAD_DIM:], a[:, :HEAD_DIM]], axis=1) for a in own]
        ordered = [jnp.where(late, b, a) for a, b in zip(own, swapped)]
        for yh in range(2):
            for x in range(0, n_x, 2):
                block = ((yh * n_z + z) * n_x + x) // 2
                lanes = slice(block * 2 * HEAD_DIM, (block + 1) * 2 * HEAD_DIM)
                half = slice(yh * HEAD_DIM, (yh + 1) * HEAD_DIM)
                both = jnp.concatenate([ordered[x][:, half], ordered[x + 1][:, half]], axis=1)
                combined = residual_ref[:, lanes].astype(F32) + both
                combined_ref[:, lanes] = combined
                squares += combined * combined
    root = lax.rsqrt(jnp.sum(squares, axis=-1, keepdims=True) / combined_ref.shape[1] + EPSILON)
    out_ref[...] = (combined_ref[...] * root * gain_ref[...]).astype(BF16)


def ring(n, by):
    return [(i, (i + by) % n) for i in range(n)]


def on_device(
    mixer_values,
    gate_values,
    input_coefs,
    output_coefs,
    step_raw,
    step_bias,
    decay_log,
    skip_gain,
    group_gain,
    carry_state,
    out_weight,
    residual,
    final_gain,
):
    tokens, inner = mixer_values.shape
    heads = step_raw.shape[1]
    n_z, n_x = lax.axis_size("z"), lax.axis_size("x")
    n_t = lax.axis_size("yl") * lax.axis_size("core")
    groups = 2 * n_z
    at_x = lax.axis_index("x")
    late = lax.axis_index("yh").astype(jnp.int32).reshape(1)
    bias, decay = step_bias.reshape(1, heads), decay_log.reshape(1, heads)
    skip = jnp.repeat(skip_gain, HEAD_DIM).reshape(1, inner)
    pairs = heads // 2
    quarter = inner // n_x
    size = quarter // groups

    states = call(
        states_kernel,
        jax.ShapeDtypeStruct((n_x, quarter + EXTRA, SPAN), F32),
        flops=2 * tokens * inner * STATE * 2,
        args=(mixer_values, input_coefs, step_raw, bias, decay),
    )
    parts = lax.all_to_all(states, "x", 0, 0, tiled=True)

    weight = out_weight.T
    across = lax.ppermute(weight, "yh", ring(2, 1))
    across, parts = lax.optimization_barrier((across, parts))
    weight = jnp.concatenate([weight, across], axis=0)
    weight = lax.all_gather(weight, "z", axis=0, tiled=True)

    own = jnp.concatenate(
        [mixer_values, gate_values, input_coefs, output_coefs, jnp.pad(step_raw, ((0, 0), (0, SPAN - heads)))], axis=1
    )
    own, parts = lax.optimization_barrier((own, parts))
    left = lax.ppermute(own, "x", ring(n_x, 1))
    right = lax.ppermute(own, "x", ring(n_x, -1))
    far = jnp.concatenate(
        [
            lax.ppermute(left[: tokens // 2], "x", ring(n_x, 1)),
            lax.ppermute(right[tokens // 2 :], "x", ring(n_x, -1)),
        ]
    )
    place = (at_x + jnp.array([0, n_x - 1, 1, 2], jnp.int32)) % n_x

    grouped = call(
        group_kernel, jax.ShapeDtypeStruct((groups, size + EXTRA, SPAN), F32), flops=10**6, args=(parts,)
    )
    parts = lax.all_to_all(grouped, GROUPS, 0, 0, tiled=True)
    mine = lax.axis_index(GROUPS)
    each = STATE // size
    carry = lax.dynamic_index_in_dim(
        carry_state.reshape(pairs, SPAN, STATE), at_x * (pairs // n_x) + mine // each, 0, False
    )
    carry = lax.dynamic_slice_in_dim(carry.T, (mine % each) * size, size, 0)
    entering = call(
        enter_kernel, jax.ShapeDtypeStruct((groups, size, SPAN), F32), flops=10**6, args=(parts, carry)
    )
    entering = lax.all_to_all(entering, GROUPS, 0, 0, tiled=True).reshape(1, quarter, SPAN)
    entering = lax.all_to_all(jnp.broadcast_to(entering, (n_x, quarter, SPAN)), "x", 0, 0, tiled=True)

    blocks = (own, left, right, far)
    locals_ = []
    for block in blocks:
        outs = call(
            local_kernel,
            [
                jax.ShapeDtypeStruct((tokens, inner), F32),
                jax.ShapeDtypeStruct((inner, SPAN), F32),
                jax.ShapeDtypeStruct((pairs, SPAN), F32),
            ],
            flops=2 * tokens * inner * tokens * 6,
            args=(block, bias, decay, skip),
        )
        locals_.append(outs)
    mixed, fresh, logs = zip(*locals_)
    normed = call(
        mix_kernel,
        jax.ShapeDtypeStruct((n_x * tokens, inner), BF16),
        scratch=[
            pltpu.VMEM((n_x, inner, SPAN), F32),
            pltpu.VMEM((n_x, pairs, SPAN), F32),
            pltpu.VMEM((n_x, tokens, inner), F32),
            pltpu.VMEM((tokens, inner), F32),
            pltpu.SemaphoreType.DMA((2 * n_x,)),
        ],
        flops=2 * n_x * tokens * inner * STATE * 2,
        smem=1,
        hbm=2 * n_x,
        args=(
            place,
            entering.reshape(inner, SPAN),
            bias,
            decay,
            group_gain.reshape(1, inner),
            *blocks,
            *logs,
            *fresh,
            *mixed,
        ),
    )
    partial = project(normed, weight)
    partial = lax.all_to_all(partial, ("x", *TENSOR), 0, 0, tiled=True)
    rows = residual.shape[0]
    done = call(
        functools.partial(finish_kernel, n_x=n_x, n_t=n_t, n_z=n_z),
        jax.ShapeDtypeStruct(residual.shape, BF16),
        scratch=[pltpu.VMEM(residual.shape, F32)],
        flops=10**6,
        smem=1,
        args=(late, partial.reshape(n_x * n_t, rows, weight.shape[0]), residual, final_gain.reshape(1, -1)),
    )
    across = lax.ppermute(done, "yl", ring(2, 1))
    mine_two = jnp.stack([done, across])
    theirs_two = lax.ppermute(mine_two, "core", ring(2, 1))
    first_y, first_core = lax.axis_index("yl") == 0, lax.axis_index("core") == 0
    even = jnp.where(first_core, mine_two, theirs_two)
    odd = jnp.where(first_core, theirs_two, mine_two)
    low = jnp.where(first_y, jnp.stack([even[0], odd[0]]), jnp.stack([even[1], odd[1]]))
    high = jnp.where(first_y, jnp.stack([even[1], odd[1]]), jnp.stack([even[0], odd[0]]))
    return jnp.concatenate([low, high]).reshape(tokens, residual.shape[1])


def solution(mesh):
    fine = Mesh(mesh.devices.reshape(2, 8, 4, 2, 2), (*CONTEXT, *TENSOR))
    return jax.shard_map(
        on_device,
        mesh=fine,
        in_specs=(
            P(CONTEXT, TENSOR),
            P(CONTEXT, TENSOR),
            P(CONTEXT, TENSOR),
            P(CONTEXT, TENSOR),
            P(CONTEXT, TENSOR),
            P(TENSOR),
            P(TENSOR),
            P(TENSOR),
            P(TENSOR),
            P(TENSOR, None, None),
            P(TENSOR, CONTEXT),
            P((*CONTEXT, *TENSOR), None),
            P(),
        ),
        out_specs=P(CONTEXT, None),
        check_vma=False,
    )
```

```python
import functools

import jax
import jax.numpy as jnp
from jax import lax
from jax.experimental import pallas as pl
from jax.experimental.pallas import tpu as pltpu
from jax.sharding import Mesh, PartitionSpec as P

EPSILON = 1e-05
HIGHEST = lax.Precision.HIGHEST
SPAN = 128
STATE = 128
HEAD_DIM = 64
EXTRA = 8
BF16, F32 = jnp.bfloat16, jnp.float32
CONTEXT = ("yh", "z", "x")
TENSOR = ("yl", "core")
GROUPS = ("yh", "z")
VMEM_LIMIT = 14 * 2**20
VMEM_MOST = 61 * 2**20


def call(kernel, outs, *, scratch=(), flops=0, smem=0, vmem=0, hbm_outs=0, args=()):
    specs = [pl.BlockSpec(memory_space=pltpu.SMEM)] * smem
    specs += [pl.BlockSpec(memory_space=pltpu.VMEM)] * vmem
    specs += [pl.BlockSpec(memory_space=pltpu.HBM)] * (len(args) - smem - vmem)
    places = [pltpu.VMEM] * (len(outs) - hbm_outs) + [pltpu.HBM] * hbm_outs
    moved = sum(a.size * a.dtype.itemsize for a in (*args, *outs))
    return pl.pallas_call(
        kernel,
        out_shape=list(outs),
        in_specs=specs,
        out_specs=[pl.BlockSpec(memory_space=m) for m in places],
        scratch_shapes=scratch,
        compiler_params=pltpu.CompilerParams(
            vmem_limit_bytes=VMEM_MOST if len(args) > smem + vmem else VMEM_LIMIT
        ),
        cost_estimate=pl.CostEstimate(flops=flops, bytes_accessed=moved, transcendentals=0),
    )(*args)


def copies(pairs, semaphores, first=0):
    started = [pltpu.make_async_copy(a, b, semaphores.at[first + i]) for i, (a, b) in enumerate(pairs)]
    for copy in started:
        copy.start()
    return started


def dot(a, b, precision=None):
    return lax.dot_general(
        a, b, (((1,), (0,)), ((), ())), precision=precision, preferred_element_type=F32
    )


def steps_of(raw_t, bias, decay_log):
    v = raw_t.astype(F32) + bias
    step = jnp.maximum(v, 0.0) + jnp.log1p(jnp.exp(-jnp.abs(v)))
    rows = lax.broadcasted_iota(jnp.int32, (SPAN, SPAN), 0)
    columns = lax.broadcasted_iota(jnp.int32, (SPAN, SPAN), 1)
    upper = jnp.where(rows <= columns, 1.0, 0.0).astype(F32)
    return step, dot(-jnp.exp(decay_log) * step, upper, HIGHEST)


def split(a):
    high = a.astype(BF16)
    return high, (a - high.astype(F32)).astype(BF16)


def first_lanes(shape):
    return lax.broadcasted_iota(jnp.int32, shape, len(shape) - 1) < HEAD_DIM


def column(a, h):
    return jnp.broadcast_to(a[:, h : h + 1], (a.shape[0], 2 * HEAD_DIM))


def fresh_states(x_ref, b, step_t, cumulative_t):
    last = cumulative_t[:, SPAN - 1 : SPAN]
    weight = jnp.transpose(step_t * jnp.exp(last - cumulative_t))
    b_t = jnp.transpose(b)
    b_twice = jnp.concatenate([b_t, b_t], axis=1)
    low = first_lanes((SPAN, SPAN))
    for pair in range(x_ref.shape[1] // SPAN):
        lanes = slice(pair * SPAN, (pair + 1) * SPAN)
        scale = jnp.where(low, column(weight, 2 * pair), column(weight, 2 * pair + 1))
        scaled = x_ref[:, lanes].astype(F32) * scale
        state = dot(b_twice, jnp.concatenate(split(scaled), axis=0))
        log = jnp.where(
            low[:1], column(last[2 * pair : 2 * pair + 1], 0), column(last[2 * pair + 1 : 2 * pair + 2], 0)
        )
        yield pair, state, log


def states_kernel(x_hbm, gate_hbm, b_hbm, c_hbm, raw_hbm, bias_hbm, decay_hbm, out_ref, packed_hbm, *scratch):
    packed_ref, bias_ref, decay_ref, semaphores = scratch
    inner, heads = x_hbm.shape[1], raw_hbm.shape[0]
    at = 2 * inner
    x_ref = packed_ref.at[:, :inner]
    gets = copies(
        [
            (raw_hbm, packed_ref.at[:heads, at + 2 * SPAN :]),
            (bias_hbm, bias_ref),
            (decay_hbm, decay_ref),
            (b_hbm, packed_ref.at[:, at : at + SPAN]),
            (x_hbm, x_ref),
            (c_hbm, packed_ref.at[:, at + SPAN : at + 2 * SPAN]),
            (gate_hbm, packed_ref.at[:, inner:at]),
        ],
        semaphores,
    )
    packed_ref[heads:, at + 2 * SPAN :] = jnp.zeros((SPAN - heads, SPAN), BF16)
    for copy in gets[:3]:
        copy.wait()
    step, cumulative = steps_of(packed_ref[:heads, at + 2 * SPAN :], bias_ref[...], decay_ref[...])
    for copy in gets[3:]:
        copy.wait()
    (put,) = copies([(packed_ref, packed_hbm)], semaphores, len(gets))
    each = out_ref.shape[1] // SPAN
    for pair, state, log in fresh_states(x_ref, packed_ref[:, at : at + SPAN], step, cumulative):
        member, place = divmod(pair, each)
        out_ref[member, place * STATE : (place + 1) * STATE, :] = state
        out_ref[member, each * STATE + place : each * STATE + place + 1, :] = log
    put.wait()


def group_kernel(parts_ref, out_ref):
    members, rows, _ = parts_ref.shape
    pairs = rows // STATE
    slices, size = out_ref.shape[0], out_ref.shape[1] - EXTRA
    for pair in range(pairs):
        here = slice(pair * STATE, (pair + 1) * STATE)
        at = pairs * STATE + pair
        log = parts_ref[0, at : at + 1, :]
        state = parts_ref[0, here, :]
        for member in range(1, members):
            more = parts_ref[member, at : at + 1, :]
            state = jnp.exp(more) * state + parts_ref[member, here, :]
            log = log + more
        for i in range(STATE // size):
            out_ref[pair * (STATE // size) + i, :size, :] = state[i * size : (i + 1) * size]
            out_ref[pair * (STATE // size) + i, size:, :] = jnp.broadcast_to(log, (EXTRA, SPAN))


def enter_kernel(parts_ref, carry_ref, out_ref):
    size = out_ref.shape[1]
    run = carry_ref[...]
    for k in range(parts_ref.shape[0]):
        out_ref[k] = run
        run = jnp.exp(parts_ref[k, size : size + 1, :]) * run + parts_ref[k, :size, :]


def local_kernel(bias_ref, decay_ref, skip_ref, block_hbm, log_ref, mixed_hbm, state_hbm, *scratch):
    x_ref, coefs_ref, mixed_ref, state_ref, semaphores = scratch
    inner, heads = x_ref.shape[1], bias_ref.shape[0]
    for copy in copies(
        [(block_hbm.at[:, :inner], x_ref), (block_hbm.at[:, 2 * inner :], coefs_ref)], semaphores
    ):
        copy.wait()
    b, c = coefs_ref[:, :SPAN], coefs_ref[:, SPAN : 2 * SPAN]
    step_t, cumulative_t = steps_of(coefs_ref[:heads, 2 * SPAN :], bias_ref[...], decay_ref[...])
    cumulative = jnp.transpose(cumulative_t)
    scores = lax.dot_general(c, b, (((1,), (1,)), ((), ())), preferred_element_type=F32)
    rows = lax.broadcasted_iota(jnp.int32, (SPAN, SPAN), 0)
    columns = lax.broadcasted_iota(jnp.int32, (SPAN, SPAN), 1)
    causal = rows >= columns
    low = first_lanes((SPAN, SPAN))
    for pair, state, log in fresh_states(x_ref, b, step_t, cumulative_t):
        lanes = slice(pair * SPAN, (pair + 1) * SPAN)
        state_ref[lanes, :] = state
        log_ref[pair : pair + 1, :] = log
        x = x_ref[:, lanes]
        weights = []
        for h in (2 * pair, 2 * pair + 1):
            gap = column(cumulative, h) - cumulative_t[h : h + 1, :]
            within = jnp.exp(jnp.where(causal, gap, -jnp.inf))
            weights.append(jnp.concatenate(split(scores * within * step_t[h : h + 1, :]), axis=1))
        both = dot(jnp.concatenate(weights, axis=0), jnp.concatenate([x, x], axis=0))
        mixed_ref[:, lanes] = jnp.where(low, both[:SPAN], both[SPAN:]) + skip_ref[:, lanes] * x.astype(F32)
    for copy in copies([(state_ref, state_hbm), (mixed_ref, mixed_hbm)], semaphores, 2):
        copy.wait()


def mix_kernel(n, place_ref, entering_ref, bias_ref, decay_ref, gain_ref, *refs):
    logs, operands = refs[:n], refs[n : 4 * n + 1]
    out_ref, enter_ref, logs_ref, mixed_ref, block_ref, gated_ref, normed_ref, weight_ref, semaphores = refs[4 * n + 1 :]
    states, mixed, blocks, weight_hbm = operands[:n], operands[n : 2 * n], operands[2 * n : 3 * n], operands[3 * n]
    inner, heads = gated_ref.shape[1], bias_ref.shape[0]
    pairs = inner // SPAN
    state_copies = copies([(states[i], enter_ref.at[place_ref[i]]) for i in range(n)], semaphores)
    block_copies = copies([(blocks[i].at[:, inner:], block_ref.at[i]) for i in range(n)], semaphores, n)
    mixed_copies = copies([(mixed[i], mixed_ref.at[i]) for i in range(n)], semaphores, 2 * n)
    (weight_copy,) = copies([(weight_hbm, weight_ref)], semaphores, 3 * n)
    for i in range(n):
        logs_ref[place_ref[i]] = logs[i][...]
    for copy in state_copies:
        copy.wait()
    for pair in range(pairs):
        lanes = slice(pair * SPAN, (pair + 1) * SPAN)
        run = entering_ref[lanes, :]
        for p in range(n):
            fresh = enter_ref[p, lanes, :]
            enter_ref[p, lanes, :] = run
            run = jnp.exp(logs_ref[p, pair : pair + 1, :]) * run + fresh
    low = first_lanes((SPAN, SPAN))
    for i in range(n):
        block_copies[i].wait()
        mixed_copies[i].wait()
        raw_t = block_ref[i, :heads, inner + 2 * SPAN :]
        _, cumulative_t = steps_of(raw_t, bias_ref[...], decay_ref[...])
        cumulative = jnp.transpose(cumulative_t)
        c = block_ref[i, :, inner + SPAN : inner + 2 * SPAN]
        c_twice = jnp.concatenate([c, c], axis=1)
        squares = jnp.zeros((SPAN, SPAN), F32)
        place = place_ref[i]
        for pair in range(pairs):
            lanes = slice(pair * SPAN, (pair + 1) * SPAN)
            at = jnp.where(low, column(cumulative, 2 * pair), column(cumulative, 2 * pair + 1))
            carried = dot(c_twice, jnp.concatenate(split(enter_ref[place, lanes, :]), axis=0))
            mixer_out = mixed_ref[i, :, lanes] + carried * jnp.exp(at)
            gate = block_ref[i, :, lanes].astype(F32)
            gated = mixer_out * (gate / (1.0 + jnp.exp(-gate)))
            gated_ref[:, lanes] = gated
            squares += gated * gated
        root = lax.rsqrt(jnp.sum(squares, axis=-1, keepdims=True) / inner + EPSILON)
        to = pl.ds(pl.multiple_of(place * SPAN, SPAN), SPAN)
        for pair in range(pairs):
            lanes = slice(pair * SPAN, (pair + 1) * SPAN)
            normed_ref[to, lanes] = (gated_ref[:, lanes] * root * gain_ref[:, lanes]).astype(BF16)
    weight_copy.wait()
    for tile in range(weight_ref.shape[0] // (2 * SPAN)):
        columns = slice(2 * tile * SPAN, 2 * (tile + 1) * SPAN)
        product = lax.dot_general(
            normed_ref[...], weight_ref[columns, :], (((1,), (1,)), ((), ())), preferred_element_type=F32
        )
        out_ref[:, columns] = product.astype(BF16)


def finish_kernel(late_ref, parts_ref, residual_ref, gain_ref, out_ref, combined_ref, *, n_x, n_t, n_z):
    late = late_ref[0] > 0
    tokens = residual_ref.shape[0]
    sums = []
    for x in range(n_x):
        total = parts_ref[x * n_t].astype(F32)
        for t in range(1, n_t):
            total += parts_ref[x * n_t + t].astype(F32)
        sums.append(total)
    squares = jnp.zeros((tokens, 2 * HEAD_DIM), F32)
    for z in range(n_z):
        piece = slice(z * 2 * HEAD_DIM, (z + 1) * 2 * HEAD_DIM)
        own = [total[:, piece] for total in sums]
        swapped = [jnp.concatenate([a[:, HEAD_DIM:], a[:, :HEAD_DIM]], axis=1) for a in own]
        ordered = [jnp.where(late, b, a) for a, b in zip(own, swapped)]
        for yh in range(2):
            for x in range(0, n_x, 2):
                block = ((yh * n_z + z) * n_x + x) // 2
                lanes = slice(block * 2 * HEAD_DIM, (block + 1) * 2 * HEAD_DIM)
                half = slice(yh * HEAD_DIM, (yh + 1) * HEAD_DIM)
                both = jnp.concatenate([ordered[x][:, half], ordered[x + 1][:, half]], axis=1)
                combined = residual_ref[:, lanes].astype(F32) + both
                combined_ref[:, lanes] = combined
                squares += combined * combined
    root = lax.rsqrt(jnp.sum(squares, axis=-1, keepdims=True) / combined_ref.shape[1] + EPSILON)
    out_ref[...] = (combined_ref[...] * root * gain_ref[...]).astype(BF16)


def ring(n, by):
    return [(i, (i + by) % n) for i in range(n)]


def on_device(
    mixer_values,
    gate_values,
    input_coefs,
    output_coefs,
    step_raw,
    step_bias,
    decay_log,
    skip_gain,
    group_gain,
    carry_state,
    out_weight,
    residual,
    final_gain,
):
    tokens, inner = mixer_values.shape
    heads = step_raw.shape[1]
    n_z, n_x = lax.axis_size("z"), lax.axis_size("x")
    n_t = lax.axis_size("yl") * lax.axis_size("core")
    groups = 2 * n_z
    at_x = lax.axis_index("x")
    late = lax.axis_index("yh").astype(jnp.int32).reshape(1)
    bias, decay = step_bias.reshape(heads, 1), decay_log.reshape(heads, 1)
    skip = jnp.repeat(skip_gain, HEAD_DIM).reshape(1, inner)
    pairs = heads // 2
    quarter = inner // n_x
    size = quarter // groups
    packed = 2 * inner + 3 * SPAN

    states, own = call(
        states_kernel,
        [
            jax.ShapeDtypeStruct((n_x, quarter + EXTRA, SPAN), F32),
            jax.ShapeDtypeStruct((tokens, packed), BF16),
        ],
        scratch=[
            pltpu.VMEM((tokens, packed), BF16),
            pltpu.VMEM((heads, 1), F32),
            pltpu.VMEM((heads, 1), F32),
            pltpu.SemaphoreType.DMA((8,)),
        ],
        flops=2 * tokens * inner * STATE * 2,
        hbm_outs=1,
        args=(mixer_values, gate_values, input_coefs, output_coefs, step_raw.T, bias, decay),
    )
    parts = lax.all_to_all(states, "x", 0, 0, tiled=True)

    weight = out_weight.T
    across = lax.ppermute(weight, "yh", ring(2, 1))
    across, parts, own = lax.optimization_barrier((across, parts, own))
    weight = jnp.concatenate([weight, across], axis=0)
    weight = lax.all_gather(weight, "z", axis=0, tiled=True)

    left = lax.ppermute(own, "x", ring(n_x, 1))
    right = lax.ppermute(own, "x", ring(n_x, -1))

    (grouped,) = call(
        group_kernel,
        [jax.ShapeDtypeStruct((groups, size + EXTRA, SPAN), F32)],
        flops=10**6,
        vmem=1,
        args=(parts,),
    )
    parts = lax.all_to_all(grouped, GROUPS, 0, 0, tiled=True)
    parts, left, right = lax.optimization_barrier((parts, left, right))
    onward, back, parts = lax.optimization_barrier((left[: tokens // 2], right[tokens // 2 :], parts))
    far = jnp.concatenate([lax.ppermute(onward, "x", ring(n_x, 1)), lax.ppermute(back, "x", ring(n_x, -1))])
    place = (at_x + jnp.array([0, n_x - 1, 1, 2], jnp.int32)) % n_x
    mine = lax.axis_index(GROUPS)
    each = STATE // size
    carry = lax.dynamic_index_in_dim(
        carry_state.reshape(pairs, SPAN, STATE), at_x * (pairs // n_x) + mine // each, 0, False
    )
    carry = lax.dynamic_slice_in_dim(carry.T, (mine % each) * size, size, 0)
    (entering,) = call(
        enter_kernel,
        [jax.ShapeDtypeStruct((groups, size, SPAN), F32)],
        flops=10**6,
        vmem=2,
        args=(parts, carry),
    )
    entering = lax.all_to_all(entering, GROUPS, 0, 0, tiled=True).reshape(1, quarter, SPAN)
    entering = lax.all_to_all(jnp.broadcast_to(entering, (n_x, quarter, SPAN)), "x", 0, 0, tiled=True)

    blocks = (own, left, right, far)
    locals_ = []
    for block in blocks:
        outs = call(
            local_kernel,
            [
                jax.ShapeDtypeStruct((pairs, SPAN), F32),
                jax.ShapeDtypeStruct((tokens, inner), F32),
                jax.ShapeDtypeStruct((inner, SPAN), F32),
            ],
            scratch=[
                pltpu.VMEM((tokens, inner), BF16),
                pltpu.VMEM((tokens, 3 * SPAN), BF16),
                pltpu.VMEM((tokens, inner), F32),
                pltpu.VMEM((inner, SPAN), F32),
                pltpu.SemaphoreType.DMA((4,)),
            ],
            flops=2 * tokens * inner * tokens * 6,
            vmem=3,
            hbm_outs=2,
            args=(bias, decay, skip, block),
        )
        locals_.append(outs)
    logs, mixed, fresh = zip(*locals_)
    (partial,) = call(
        functools.partial(mix_kernel, n_x),
        [jax.ShapeDtypeStruct((n_x * tokens, weight.shape[0]), BF16)],
        scratch=[
            pltpu.VMEM((n_x, inner, SPAN), F32),
            pltpu.VMEM((n_x, pairs, SPAN), F32),
            pltpu.VMEM((n_x, tokens, inner), F32),
            pltpu.VMEM((n_x, tokens, packed - inner), BF16),
            pltpu.VMEM((tokens, inner), F32),
            pltpu.VMEM((n_x * tokens, inner), BF16),
            pltpu.VMEM(weight.shape, BF16),
            pltpu.SemaphoreType.DMA((3 * n_x + 1,)),
        ],
        flops=2 * n_x * tokens * inner * (STATE * 2 + weight.shape[0]),
        smem=1,
        vmem=4 + n_x,
        args=(
            place,
            entering.reshape(inner, SPAN),
            bias,
            decay,
            group_gain.reshape(1, inner),
            *logs,
            *fresh,
            *mixed,
            *blocks,
            weight,
        ),
    )
    partial = lax.all_to_all(partial, ("x", *TENSOR), 0, 0, tiled=True)
    rows = residual.shape[0]
    (done,) = call(
        functools.partial(finish_kernel, n_x=n_x, n_t=n_t, n_z=n_z),
        [jax.ShapeDtypeStruct(residual.shape, BF16)],
        scratch=[pltpu.VMEM(residual.shape, F32)],
        flops=10**6,
        smem=1,
        vmem=3,
        args=(late, partial.reshape(n_x * n_t, rows, weight.shape[0]), residual, final_gain.reshape(1, -1)),
    )
    across = lax.ppermute(done, "yl", ring(2, 1))
    mine_two = jnp.stack([done, across])
    theirs_two = lax.ppermute(mine_two, "core", ring(2, 1))
    first_y, first_core = lax.axis_index("yl") == 0, lax.axis_index("core") == 0
    even = jnp.where(first_core, mine_two, theirs_two)
    odd = jnp.where(first_core, theirs_two, mine_two)
    low = jnp.where(first_y, jnp.stack([even[0], odd[0]]), jnp.stack([even[1], odd[1]]))
    high = jnp.where(first_y, jnp.stack([even[1], odd[1]]), jnp.stack([even[0], odd[0]]))
    return jnp.concatenate([low, high]).reshape(tokens, residual.shape[1])


def solution(mesh):
    fine = Mesh(mesh.devices.reshape(2, 8, 4, 2, 2), (*CONTEXT, *TENSOR))
    return jax.shard_map(
        on_device,
        mesh=fine,
        in_specs=(
            P(CONTEXT, TENSOR),
            P(CONTEXT, TENSOR),
            P(CONTEXT, TENSOR),
            P(CONTEXT, TENSOR),
            P(CONTEXT, TENSOR),
            P(TENSOR),
            P(TENSOR),
            P(TENSOR),
            P(TENSOR),
            P(TENSOR, None, None),
            P(TENSOR, CONTEXT),
            P((*CONTEXT, *TENSOR), None),
            P(),
        ),
        out_specs=P(CONTEXT, None),
        check_vma=False,
    )
```

```python
import functools

import jax
import jax.numpy as jnp
from jax import lax
from jax.experimental import pallas as pl
from jax.experimental.pallas import tpu as pltpu
from jax.sharding import Mesh, PartitionSpec as P

EPSILON = 1e-05
HIGHEST = lax.Precision.HIGHEST
SPAN = 128
STATE = 128
HEAD_DIM = 64
EXTRA = 8
BF16, F32 = jnp.bfloat16, jnp.float32
CONTEXT = ("yh", "z", "x")
TENSOR = ("yl", "core")
GROUPS = ("yh", "z")
VMEM_LIMIT = 14 * 2**20
VMEM_MOST = 61 * 2**20


def call(kernel, outs, *, scratch=(), flops=0, smem=0, vmem=0, hbm_outs=0, args=()):
    specs = [pl.BlockSpec(memory_space=pltpu.SMEM)] * smem
    specs += [pl.BlockSpec(memory_space=pltpu.VMEM)] * vmem
    specs += [pl.BlockSpec(memory_space=pltpu.HBM)] * (len(args) - smem - vmem)
    places = [pltpu.VMEM] * (len(outs) - hbm_outs) + [pltpu.HBM] * hbm_outs
    moved = sum(a.size * a.dtype.itemsize for a in (*args, *outs))
    return pl.pallas_call(
        kernel,
        out_shape=list(outs),
        in_specs=specs,
        out_specs=[pl.BlockSpec(memory_space=m) for m in places],
        scratch_shapes=scratch,
        compiler_params=pltpu.CompilerParams(
            vmem_limit_bytes=VMEM_MOST if len(args) > smem + vmem else VMEM_LIMIT
        ),
        cost_estimate=pl.CostEstimate(flops=flops, bytes_accessed=moved, transcendentals=0),
    )(*args)


def copies(pairs, semaphores, first=0):
    started = [pltpu.make_async_copy(a, b, semaphores.at[first + i]) for i, (a, b) in enumerate(pairs)]
    for copy in started:
        copy.start()
    return started


def dot(a, b, precision=None):
    return lax.dot_general(
        a, b, (((1,), (0,)), ((), ())), precision=precision, preferred_element_type=F32
    )


def as_column(row):
    square = (row.shape[1], row.shape[1])
    same = lax.broadcasted_iota(jnp.int32, square, 0) == lax.broadcasted_iota(jnp.int32, square, 1)
    return jnp.sum(jnp.where(same, jnp.broadcast_to(row, square), 0.0), axis=1, keepdims=True)


def steps_of(raw_t, bias, decay_log):
    v = raw_t.astype(F32) + as_column(bias)
    step = jnp.maximum(v, 0.0) + jnp.log1p(jnp.exp(-jnp.abs(v)))
    rows = lax.broadcasted_iota(jnp.int32, (SPAN, SPAN), 0)
    columns = lax.broadcasted_iota(jnp.int32, (SPAN, SPAN), 1)
    upper = jnp.where(rows <= columns, 1.0, 0.0).astype(F32)
    return step, dot(-jnp.exp(as_column(decay_log)) * step, upper, HIGHEST)


def split(a):
    high = a.astype(BF16)
    return high, (a - high.astype(F32)).astype(BF16)


def first_lanes(shape):
    return lax.broadcasted_iota(jnp.int32, shape, len(shape) - 1) < HEAD_DIM


def column(a, h):
    return jnp.broadcast_to(a[:, h : h + 1], (a.shape[0], 2 * HEAD_DIM))


def pair_row(a, pair):
    low = first_lanes((1, 2 * HEAD_DIM))
    return jnp.where(low, column(a[2 * pair : 2 * pair + 1], 0), column(a[2 * pair + 1 : 2 * pair + 2], 0))


def fresh_states(x_ref, b, step_t, cumulative_t, x_in=()):
    last = cumulative_t[:, SPAN - 1 : SPAN]
    weight = jnp.transpose(step_t * jnp.exp(last - cumulative_t))
    b_t = jnp.transpose(b)
    b_twice = jnp.concatenate([b_t, b_t], axis=1)
    low = first_lanes((SPAN, SPAN))
    pairs = x_ref.shape[1] // SPAN
    for pair in range(pairs):
        if x_in and pair % (pairs // len(x_in)) == 0:
            for copy in x_in[pair // (pairs // len(x_in))]:
                copy.wait()
        lanes = slice(pair * SPAN, (pair + 1) * SPAN)
        scale = jnp.where(low, column(weight, 2 * pair), column(weight, 2 * pair + 1))
        scaled = x_ref[:, lanes].astype(F32) * scale
        state = dot(b_twice, jnp.concatenate(split(scaled), axis=0))
        yield pair, state, pair_row(last, pair)


def states_kernel(x_hbm, gate_hbm, b_hbm, c_hbm, raw_hbm, bias_hbm, decay_hbm, out_ref, top_hbm, bottom_hbm, *scratch):
    packed_ref, bias_ref, decay_ref, semaphores = scratch
    inner, heads = x_hbm.shape[1], raw_hbm.shape[0]
    at = 2 * inner
    x_ref = packed_ref.at[:, :inner]
    gets = copies(
        [
            (raw_hbm, packed_ref.at[:heads, at + 2 * SPAN :]),
            (bias_hbm, bias_ref),
            (decay_hbm, decay_ref),
            (b_hbm, packed_ref.at[:, at : at + SPAN]),
            (x_hbm, x_ref),
            (c_hbm, packed_ref.at[:, at + SPAN : at + 2 * SPAN]),
            (gate_hbm, packed_ref.at[:, inner:at]),
        ],
        semaphores,
    )
    packed_ref[heads:, at + 2 * SPAN :] = jnp.zeros((SPAN - heads, SPAN), BF16)
    for copy in gets[:3]:
        copy.wait()
    step, cumulative = steps_of(packed_ref[:heads, at + 2 * SPAN :], bias_ref[...], decay_ref[...])
    for copy in gets[3:]:
        copy.wait()
    half = SPAN // 2
    puts = copies([(packed_ref.at[:half], top_hbm), (packed_ref.at[half:], bottom_hbm)], semaphores, len(gets))
    each = out_ref.shape[1] // SPAN
    for pair, state, log in fresh_states(x_ref, packed_ref[:, at : at + SPAN], step, cumulative):
        member, place = divmod(pair, each)
        out_ref[member, place * STATE : (place + 1) * STATE, :] = state
        out_ref[member, each * STATE + place : each * STATE + place + 1, :] = log
    for put in puts:
        put.wait()


def group_kernel(parts_ref, out_ref):
    members, rows, _ = parts_ref.shape
    pairs = rows // STATE
    slices, size = out_ref.shape[0], out_ref.shape[1] - EXTRA
    for pair in range(pairs):
        here = slice(pair * STATE, (pair + 1) * STATE)
        at = pairs * STATE + pair
        log = parts_ref[0, at : at + 1, :]
        state = parts_ref[0, here, :]
        for member in range(1, members):
            more = parts_ref[member, at : at + 1, :]
            state = jnp.exp(more) * state + parts_ref[member, here, :]
            log = log + more
        for i in range(STATE // size):
            out_ref[pair * (STATE // size) + i, :size, :] = state[i * size : (i + 1) * size]
            out_ref[pair * (STATE // size) + i, size:, :] = jnp.broadcast_to(log, (EXTRA, SPAN))


def enter_kernel(parts_ref, carry_ref, out_ref):
    size = out_ref.shape[1]
    run = carry_ref[...]
    for k in range(parts_ref.shape[0]):
        out_ref[k] = run
        run = jnp.exp(parts_ref[k, size : size + 1, :]) * run + parts_ref[k, :size, :]


def halves(pieces, columns, ref):
    half = SPAN // 2
    return [(pieces[0].at[:, columns], ref.at[:half]), (pieces[1].at[:, columns], ref.at[half:])]


def local_kernel(bias_ref, decay_ref, skip_ref, top_hbm, bottom_hbm, mixed_hbm, state_hbm, *scratch):
    x_ref, coefs_ref, mixed_ref, state_ref, gets, puts = scratch
    inner, heads = x_ref.shape[1], bias_ref.shape[1]
    step = inner // 4
    pieces = (top_hbm, bottom_hbm)
    coefs_in = copies(halves(pieces, slice(2 * inner, None), coefs_ref), gets)
    x_in = [
        copies(halves(pieces, pl.ds(i * step, step), x_ref.at[:, pl.ds(i * step, step)]), gets, 2 + 2 * i)
        for i in range(4)
    ]
    for copy in coefs_in:
        copy.wait()
    b, c = coefs_ref[:, :SPAN], coefs_ref[:, SPAN : 2 * SPAN]
    step_t, cumulative_t = steps_of(coefs_ref[:heads, 2 * SPAN :], bias_ref[...], decay_ref[...])
    cumulative = jnp.transpose(cumulative_t)
    scores = lax.dot_general(c, b, (((1,), (1,)), ((), ())), preferred_element_type=F32)
    rows = lax.broadcasted_iota(jnp.int32, (SPAN, SPAN), 0)
    columns = lax.broadcasted_iota(jnp.int32, (SPAN, SPAN), 1)
    causal = rows >= columns
    low = first_lanes((SPAN, SPAN))
    each = step // SPAN
    out = []
    for pair, state, _ in fresh_states(x_ref, b, step_t, cumulative_t, x_in):
        lanes = slice(pair * SPAN, (pair + 1) * SPAN)
        state_ref[lanes, :] = state
        x = x_ref[:, lanes]
        weights = []
        for h in (2 * pair, 2 * pair + 1):
            gap = column(cumulative, h) - cumulative_t[h : h + 1, :]
            within = jnp.exp(jnp.where(causal, gap, -jnp.inf))
            weights.append(jnp.concatenate(split(scores * within * step_t[h : h + 1, :]), axis=1))
        both = dot(jnp.concatenate(weights, axis=0), jnp.concatenate([x, x], axis=0))
        mixed_ref[:, lanes] = jnp.where(low, both[:SPAN], both[SPAN:]) + skip_ref[:, lanes] * x.astype(F32)
        if pair % each == each - 1:
            part = pl.ds(pair // each * step, step)
            out += copies(
                [
                    (state_ref.at[part], state_hbm.at[part]),
                    (mixed_ref.at[:, part], mixed_hbm.at[:, part]),
                ],
                puts,
                len(out),
            )
    for copy in out:
        copy.wait()


def fold_kernel(n, place_ref, bias_ref, decay_ref, *refs):
    states, mixed, blocks = refs[:n], refs[n : 2 * n], refs[2 * n : 4 * n]
    out, (enter_ref, logs_ref, mixed_ref, coefs_ref, gets, puts) = refs[4 * n : 5 * n], refs[5 * n :]
    inner, heads = mixed_ref.shape[2], bias_ref.shape[1]
    pairs = inner // SPAN
    coefs_in, state_in, mixed_in = [], [], []
    for i in range(n):
        coefs_in += copies(
            halves(blocks[2 * i : 2 * i + 2], slice(2 * inner, None), coefs_ref.at[i]), gets, 2 * i
        )
    for i in range(n):
        state_in += copies([(states[i], enter_ref.at[place_ref[i]])], gets, 2 * n + i)
    for i in range(n):
        mixed_in += copies([(mixed[i], mixed_ref.at[i])], gets, 3 * n + i)
    for copy in coefs_in:
        copy.wait()
    for i in range(n):
        raw_t = coefs_ref[i, :heads, 2 * SPAN :]
        logs_ref[place_ref[i]] = steps_of(raw_t, bias_ref[...], decay_ref[...])[1]
    for copy in state_in:
        copy.wait()
    for pair in range(pairs):
        lanes = slice(pair * SPAN, (pair + 1) * SPAN)
        run = jnp.zeros((SPAN, SPAN), F32)
        for p in range(n):
            fresh = enter_ref[p, lanes, :]
            enter_ref[p, lanes, :] = run
            run = jnp.exp(pair_row(logs_ref[p, :, SPAN - 1 :], pair)) * run + fresh
    low = first_lanes((SPAN, SPAN))
    out_copies = []
    for i in range(n):
        mixed_in[i].wait()
        place = place_ref[i]
        cumulative = jnp.transpose(logs_ref[place])
        c = coefs_ref[i, :, SPAN : 2 * SPAN]
        c_twice = jnp.concatenate([c, c], axis=1)
        for pair in range(pairs):
            lanes = slice(pair * SPAN, (pair + 1) * SPAN)
            at = jnp.where(low, column(cumulative, 2 * pair), column(cumulative, 2 * pair + 1))
            carried = dot(c_twice, jnp.concatenate(split(enter_ref[place, lanes, :]), axis=0))
            mixed_ref[i, :, lanes] += carried * jnp.exp(at)
        out_copies += copies([(mixed_ref.at[i], out[i])], puts, i)
    for copy in out_copies:
        copy.wait()


def mix_kernel(n, place_ref, bias_ref, decay_ref, gain_ref, *refs):
    entering_hbm, mixed, blocks, weight_hbm = refs[0], refs[1 : n + 1], refs[n + 1 : 3 * n + 1], refs[3 * n + 1]
    out_ref, enter_ref, logs_ref, mixed_ref, block_ref, normed_ref, weight_ref, semaphores = refs[3 * n + 2 :]
    inner, heads = mixed_ref.shape[2], bias_ref.shape[1]
    pairs = inner // SPAN
    block_in, mixed_in = [], []
    for i in range(n):
        block_in += copies(
            halves(blocks[2 * i : 2 * i + 2], slice(inner, None), block_ref.at[i]), semaphores, 2 * i
        )
        if i == 0:
            (enter_in,) = copies([(entering_hbm, enter_ref)], semaphores, 3 * n)
        mixed_in += copies([(mixed[i], mixed_ref.at[i])], semaphores, 2 * n + i)
    (weight_in,) = copies([(weight_hbm, weight_ref)], semaphores, 3 * n + 1)
    for i in range(n):
        for copy in block_in[2 * i : 2 * i + 2]:
            copy.wait()
        raw_t = block_ref[i, :heads, inner + 2 * SPAN :]
        logs_ref[place_ref[i]] = steps_of(raw_t, bias_ref[...], decay_ref[...])[1]
    before = jnp.zeros((heads, 1), F32)
    for p in range(n):
        here = logs_ref[p]
        logs_ref[p] = here + before
        before = before + here[:, SPAN - 1 :]
    enter_in.wait()
    low = first_lanes((SPAN, SPAN))
    for i in range(n):
        mixed_in[i].wait()
        place = place_ref[i]
        cumulative = jnp.transpose(logs_ref[place])
        c = block_ref[i, :, inner + SPAN : inner + 2 * SPAN]
        c_twice = jnp.concatenate([c, c], axis=1)
        squares = jnp.zeros((SPAN, SPAN), F32)
        for pair in range(pairs):
            lanes = slice(pair * SPAN, (pair + 1) * SPAN)
            at = jnp.where(low, column(cumulative, 2 * pair), column(cumulative, 2 * pair + 1))
            carried = dot(c_twice, jnp.concatenate(split(enter_ref[lanes, :]), axis=0))
            mixer_out = mixed_ref[i, :, lanes] + carried * jnp.exp(at)
            gate = block_ref[i, :, lanes].astype(F32)
            gated = mixer_out * (gate / (1.0 + jnp.exp(-gate)))
            mixed_ref[i, :, lanes] = gated
            squares += gated * gated
        root = lax.rsqrt(jnp.sum(squares, axis=-1, keepdims=True) / inner + EPSILON)
        to = pl.ds(pl.multiple_of(place * SPAN, SPAN), SPAN)
        for pair in range(pairs):
            lanes = slice(pair * SPAN, (pair + 1) * SPAN)
            normed_ref[to, lanes] = (mixed_ref[i, :, lanes] * root * gain_ref[:, lanes]).astype(BF16)
    weight_in.wait()
    for tile in range(weight_ref.shape[0] // (2 * SPAN)):
        columns = slice(2 * tile * SPAN, 2 * (tile + 1) * SPAN)
        product = lax.dot_general(
            normed_ref[...], weight_ref[columns, :], (((1,), (1,)), ((), ())), preferred_element_type=F32
        )
        out_ref[:, columns] = product.astype(BF16)


def finish_kernel(late_ref, parts_ref, residual_ref, gain_ref, out_ref, combined_ref, *, n_x, n_t, n_z):
    late = late_ref[0] > 0
    tokens = residual_ref.shape[0]
    sums = []
    for x in range(n_x):
        total = parts_ref[x * n_t].astype(F32)
        for t in range(1, n_t):
            total += parts_ref[x * n_t + t].astype(F32)
        sums.append(total)
    squares = jnp.zeros((tokens, 2 * HEAD_DIM), F32)
    for z in range(n_z):
        piece = slice(z * 2 * HEAD_DIM, (z + 1) * 2 * HEAD_DIM)
        own = [total[:, piece] for total in sums]
        swapped = [jnp.concatenate([a[:, HEAD_DIM:], a[:, :HEAD_DIM]], axis=1) for a in own]
        ordered = [jnp.where(late, b, a) for a, b in zip(own, swapped)]
        for yh in range(2):
            for x in range(0, n_x, 2):
                block = ((yh * n_z + z) * n_x + x) // 2
                lanes = slice(block * 2 * HEAD_DIM, (block + 1) * 2 * HEAD_DIM)
                half = slice(yh * HEAD_DIM, (yh + 1) * HEAD_DIM)
                both = jnp.concatenate([ordered[x][:, half], ordered[x + 1][:, half]], axis=1)
                combined = residual_ref[:, lanes].astype(F32) + both
                combined_ref[:, lanes] = combined
                squares += combined * combined
    root = lax.rsqrt(jnp.sum(squares, axis=-1, keepdims=True) / combined_ref.shape[1] + EPSILON)
    out_ref[...] = (combined_ref[...] * root * gain_ref[...]).astype(BF16)


def ring(n, by):
    return [(i, (i + by) % n) for i in range(n)]


def on_device(
    mixer_values,
    gate_values,
    input_coefs,
    output_coefs,
    step_raw,
    step_bias,
    decay_log,
    skip_gain,
    group_gain,
    carry_state,
    out_weight,
    residual,
    final_gain,
):
    tokens, inner = mixer_values.shape
    heads = step_raw.shape[1]
    n_z, n_x = lax.axis_size("z"), lax.axis_size("x")
    n_t = lax.axis_size("yl") * lax.axis_size("core")
    groups = 2 * n_z
    at_x = lax.axis_index("x")
    late = lax.axis_index("yh").astype(jnp.int32).reshape(1)
    bias, decay = step_bias.reshape(1, heads), decay_log.reshape(1, heads)
    skip = jnp.repeat(skip_gain, HEAD_DIM).reshape(1, inner)
    pairs = heads // 2
    quarter = inner // n_x
    size = quarter // groups
    packed = 2 * inner + 3 * SPAN

    half_block = jax.ShapeDtypeStruct((tokens // 2, packed), BF16)
    values = jax.ShapeDtypeStruct((tokens, inner), F32)

    weight = out_weight.T
    across = lax.ppermute(weight, "yh", ring(2, 1))

    states, top, bottom = call(
        states_kernel,
        [jax.ShapeDtypeStruct((n_x, quarter + EXTRA, SPAN), F32), half_block, half_block],
        scratch=[
            pltpu.VMEM((tokens, packed), BF16),
            pltpu.VMEM((1, heads), F32),
            pltpu.VMEM((1, heads), F32),
            pltpu.SemaphoreType.DMA((9,)),
        ],
        flops=2 * tokens * inner * STATE * 2,
        hbm_outs=2,
        args=(mixer_values, gate_values, input_coefs, output_coefs, step_raw.T, bias, decay),
    )
    across, states = lax.optimization_barrier((across, states))
    parts = lax.all_to_all(states, "x", 0, 0, tiled=True)
    weight = jnp.concatenate([weight, across], axis=0)
    weight = lax.all_gather(weight, "z", axis=0, tiled=True)

    parts, top, bottom = lax.optimization_barrier((parts, top, bottom))
    own = (top, bottom)
    left = tuple(lax.ppermute(a, "x", ring(n_x, 1)) for a in own)
    right = tuple(lax.ppermute(a, "x", ring(n_x, -1)) for a in (bottom, top))[::-1]
    place = (at_x + jnp.array([0, n_x - 1, 1, 2], jnp.int32)) % n_x

    def local(block):
        return call(
            local_kernel,
            [values, jax.ShapeDtypeStruct((inner, SPAN), F32)],
            scratch=[
                pltpu.VMEM((tokens, inner), BF16),
                pltpu.VMEM((tokens, 3 * SPAN), BF16),
                pltpu.VMEM((tokens, inner), F32),
                pltpu.VMEM((inner, SPAN), F32),
                pltpu.SemaphoreType.DMA((10,)),
                pltpu.SemaphoreType.DMA((8,)),
            ],
            flops=2 * tokens * inner * tokens * 6,
            vmem=3,
            hbm_outs=2,
            args=(bias, decay, skip, *block),
        )

    (grouped,) = call(
        group_kernel,
        [jax.ShapeDtypeStruct((groups, size + EXTRA, SPAN), F32)],
        flops=10**6,
        vmem=1,
        args=(parts,),
    )
    parts = lax.all_to_all(grouped, GROUPS, 0, 0, tiled=True)
    own_local, parts, onward, back = lax.optimization_barrier((local(own), parts, left[0], right[1]))
    left, right = (onward, left[1]), (right[0], back)
    far = (lax.ppermute(onward, "x", ring(n_x, 1)), lax.ppermute(back, "x", ring(n_x, -1)))
    mine = lax.axis_index(GROUPS)
    each = STATE // size
    carry = lax.dynamic_index_in_dim(
        carry_state.reshape(pairs, SPAN, STATE), at_x * (pairs // n_x) + mine // each, 0, False
    )
    carry = lax.dynamic_slice_in_dim(carry.T, (mine % each) * size, size, 0)
    (entering,) = call(
        enter_kernel,
        [jax.ShapeDtypeStruct((groups, size, SPAN), F32)],
        flops=10**6,
        vmem=2,
        args=(parts, carry),
    )
    entering = lax.all_to_all(entering, GROUPS, 0, 0, tiled=True).reshape(1, quarter, SPAN)
    entering, left_local, right_local, far = lax.optimization_barrier((entering, local(left), local(right), far))
    entering = lax.all_to_all(jnp.broadcast_to(entering, (n_x, quarter, SPAN)), "x", 0, 0, tiled=True)

    mixed, fresh = zip(own_local, left_local, right_local, local(far))
    blocks = (*own, *left, *right, *far)
    mixed = call(
        functools.partial(fold_kernel, n_x),
        [values] * n_x,
        scratch=[
            pltpu.VMEM((n_x, inner, SPAN), F32),
            pltpu.VMEM((n_x, heads, SPAN), F32),
            pltpu.VMEM((n_x, tokens, inner), F32),
            pltpu.VMEM((n_x, tokens, 3 * SPAN), BF16),
            pltpu.SemaphoreType.DMA((4 * n_x,)),
            pltpu.SemaphoreType.DMA((n_x,)),
        ],
        flops=2 * n_x * tokens * inner * STATE * 2,
        smem=1,
        vmem=2,
        hbm_outs=n_x,
        args=(place, bias, decay, *fresh, *mixed, *blocks),
    )
    (partial,) = call(
        functools.partial(mix_kernel, n_x),
        [jax.ShapeDtypeStruct((n_x * tokens, weight.shape[0]), BF16)],
        scratch=[
            pltpu.VMEM((inner, SPAN), F32),
            pltpu.VMEM((n_x, heads, SPAN), F32),
            pltpu.VMEM((n_x, tokens, inner), F32),
            pltpu.VMEM((n_x, tokens, packed - inner), BF16),
            pltpu.VMEM((n_x * tokens, inner), BF16),
            pltpu.VMEM(weight.shape, BF16),
            pltpu.SemaphoreType.DMA((3 * n_x + 2,)),
        ],
        flops=2 * n_x * tokens * inner * (STATE * 2 + weight.shape[0]),
        smem=1,
        vmem=3,
        args=(
            place,
            bias,
            decay,
            group_gain.reshape(1, inner),
            entering.reshape(inner, SPAN),
            *mixed,
            *blocks,
            weight,
        ),
    )
    partial = lax.all_to_all(partial, ("x", *TENSOR), 0, 0, tiled=True)
    rows = residual.shape[0]
    (done,) = call(
        functools.partial(finish_kernel, n_x=n_x, n_t=n_t, n_z=n_z),
        [jax.ShapeDtypeStruct(residual.shape, BF16)],
        scratch=[pltpu.VMEM(residual.shape, F32)],
        flops=10**6,
        smem=1,
        vmem=3,
        args=(late, partial.reshape(n_x * n_t, rows, weight.shape[0]), residual, final_gain.reshape(1, -1)),
    )
    across = lax.ppermute(done, "yl", ring(2, 1))
    mine_two = jnp.stack([done, across])
    theirs_two = lax.ppermute(mine_two, "core", ring(2, 1))
    first_y, first_core = lax.axis_index("yl") == 0, lax.axis_index("core") == 0
    even = jnp.where(first_core, mine_two, theirs_two)
    odd = jnp.where(first_core, theirs_two, mine_two)
    low = jnp.where(first_y, jnp.stack([even[0], odd[0]]), jnp.stack([even[1], odd[1]]))
    high = jnp.where(first_y, jnp.stack([even[1], odd[1]]), jnp.stack([even[0], odd[0]]))
    return jnp.concatenate([low, high]).reshape(tokens, residual.shape[1])


def solution(mesh):
    fine = Mesh(mesh.devices.reshape(2, 8, 4, 2, 2), (*CONTEXT, *TENSOR))
    return jax.shard_map(
        on_device,
        mesh=fine,
        in_specs=(
            P(CONTEXT, TENSOR),
            P(CONTEXT, TENSOR),
            P(CONTEXT, TENSOR),
            P(CONTEXT, TENSOR),
            P(CONTEXT, TENSOR),
            P(TENSOR),
            P(TENSOR),
            P(TENSOR),
            P(TENSOR),
            P(TENSOR, None, None),
            P(TENSOR, CONTEXT),
            P((*CONTEXT, *TENSOR), None),
            P(),
        ),
        out_specs=P(CONTEXT, None),
        check_vma=False,
    )
```

```python
import functools

import jax
import jax.numpy as jnp
from jax import lax
from jax.experimental import pallas as pl
from jax.experimental.pallas import tpu as pltpu
from jax.sharding import Mesh, PartitionSpec as P

EPSILON = 1e-05
HIGHEST = lax.Precision.HIGHEST
SPAN = 128
STATE = 128
HEAD_DIM = 64
EXTRA = 8
BF16, F32 = jnp.bfloat16, jnp.float32
CONTEXT = ("yh", "z", "x")
TENSOR = ("yl", "core")
GROUPS = ("yh", "z")
VMEM_LIMIT = 14 * 2**20
VMEM_MOST = 61 * 2**20


def call(kernel, outs, *, scratch=(), flops=0, smem=0, vmem=0, hbm_outs=0, args=()):
    specs = [pl.BlockSpec(memory_space=pltpu.SMEM)] * smem
    specs += [pl.BlockSpec(memory_space=pltpu.VMEM)] * vmem
    specs += [pl.BlockSpec(memory_space=pltpu.HBM)] * (len(args) - smem - vmem)
    places = [pltpu.VMEM] * (len(outs) - hbm_outs) + [pltpu.HBM] * hbm_outs
    moved = sum(a.size * a.dtype.itemsize for a in (*args, *outs))
    return pl.pallas_call(
        kernel,
        out_shape=list(outs),
        in_specs=specs,
        out_specs=[pl.BlockSpec(memory_space=m) for m in places],
        scratch_shapes=scratch,
        compiler_params=pltpu.CompilerParams(
            vmem_limit_bytes=VMEM_MOST if len(args) > smem + vmem else VMEM_LIMIT
        ),
        cost_estimate=pl.CostEstimate(flops=flops, bytes_accessed=moved, transcendentals=0),
    )(*args)


def copies(pairs, semaphores, first=0):
    started = [pltpu.make_async_copy(a, b, semaphores.at[first + i]) for i, (a, b) in enumerate(pairs)]
    for copy in started:
        copy.start()
    return started


def dot(a, b, precision=None):
    return lax.dot_general(
        a, b, (((1,), (0,)), ((), ())), precision=precision, preferred_element_type=F32
    )


def as_column(row):
    square = (row.shape[1], row.shape[1])
    same = lax.broadcasted_iota(jnp.int32, square, 0) == lax.broadcasted_iota(jnp.int32, square, 1)
    return jnp.sum(jnp.where(same, jnp.broadcast_to(row, square), 0.0), axis=1, keepdims=True)


def steps_of(raw_t, bias, decay_log):
    v = raw_t.astype(F32) + as_column(bias)
    step = jnp.maximum(v, 0.0) + jnp.log1p(jnp.exp(-jnp.abs(v)))
    rows = lax.broadcasted_iota(jnp.int32, (SPAN, SPAN), 0)
    columns = lax.broadcasted_iota(jnp.int32, (SPAN, SPAN), 1)
    upper = jnp.where(rows <= columns, 1.0, 0.0).astype(F32)
    return step, dot(-jnp.exp(as_column(decay_log)) * step, upper, HIGHEST)


def split(a):
    high = a.astype(BF16)
    return high, (a - high.astype(F32)).astype(BF16)


def first_lanes(shape):
    return lax.broadcasted_iota(jnp.int32, shape, len(shape) - 1) < HEAD_DIM


def column(a, h):
    return jnp.broadcast_to(a[:, h : h + 1], (a.shape[0], 2 * HEAD_DIM))


def pair_row(a, pair):
    low = first_lanes((1, 2 * HEAD_DIM))
    return jnp.where(low, column(a[2 * pair : 2 * pair + 1], 0), column(a[2 * pair + 1 : 2 * pair + 2], 0))


def fresh_states(x_ref, b, step_t, cumulative_t, x_in=()):
    last = cumulative_t[:, SPAN - 1 : SPAN]
    weight = jnp.transpose(step_t * jnp.exp(last - cumulative_t))
    b_t = jnp.transpose(b)
    b_twice = jnp.concatenate([b_t, b_t], axis=1)
    low = first_lanes((SPAN, SPAN))
    pairs = x_ref.shape[1] // SPAN
    for pair in range(pairs):
        if x_in and pair % (pairs // len(x_in)) == 0:
            for copy in x_in[pair // (pairs // len(x_in))]:
                copy.wait()
        lanes = slice(pair * SPAN, (pair + 1) * SPAN)
        scale = jnp.where(low, column(weight, 2 * pair), column(weight, 2 * pair + 1))
        scaled = x_ref[:, lanes].astype(F32) * scale
        state = dot(b_twice, jnp.concatenate(split(scaled), axis=0))
        yield pair, state, pair_row(last, pair)


def states_kernel(x_hbm, gate_hbm, b_hbm, c_hbm, raw_hbm, bias_hbm, decay_hbm, out_ref, top_hbm, bottom_hbm, *scratch):
    packed_ref, bias_ref, decay_ref, semaphores = scratch
    inner, heads = x_hbm.shape[1], raw_hbm.shape[0]
    at = 2 * inner
    x_ref = packed_ref.at[:, :inner]
    gets = copies(
        [
            (raw_hbm, packed_ref.at[:heads, at + 2 * SPAN :]),
            (bias_hbm, bias_ref),
            (decay_hbm, decay_ref),
            (b_hbm, packed_ref.at[:, at : at + SPAN]),
            (x_hbm, x_ref),
            (c_hbm, packed_ref.at[:, at + SPAN : at + 2 * SPAN]),
            (gate_hbm, packed_ref.at[:, inner:at]),
        ],
        semaphores,
    )
    packed_ref[heads:, at + 2 * SPAN :] = jnp.zeros((SPAN - heads, SPAN), BF16)
    for copy in gets[:3]:
        copy.wait()
    step, cumulative = steps_of(packed_ref[:heads, at + 2 * SPAN :], bias_ref[...], decay_ref[...])
    for copy in gets[3:]:
        copy.wait()
    half = SPAN // 2
    puts = copies([(packed_ref.at[:half], top_hbm), (packed_ref.at[half:], bottom_hbm)], semaphores, len(gets))
    each = out_ref.shape[1] // SPAN
    for pair, state, log in fresh_states(x_ref, packed_ref[:, at : at + SPAN], step, cumulative):
        member, place = divmod(pair, each)
        out_ref[member, place * STATE : (place + 1) * STATE, :] = state
        out_ref[member, each * STATE + place : each * STATE + place + 1, :] = log
    for put in puts:
        put.wait()


def group_kernel(parts_ref, out_ref):
    members, rows, _ = parts_ref.shape
    pairs = rows // STATE
    slices, size = out_ref.shape[0], out_ref.shape[1] - EXTRA
    for pair in range(pairs):
        here = slice(pair * STATE, (pair + 1) * STATE)
        at = pairs * STATE + pair
        log = parts_ref[0, at : at + 1, :]
        state = parts_ref[0, here, :]
        for member in range(1, members):
            more = parts_ref[member, at : at + 1, :]
            state = jnp.exp(more) * state + parts_ref[member, here, :]
            log = log + more
        for i in range(STATE // size):
            out_ref[pair * (STATE // size) + i, :size, :] = state[i * size : (i + 1) * size]
            out_ref[pair * (STATE // size) + i, size:, :] = jnp.broadcast_to(log, (EXTRA, SPAN))


def enter_kernel(parts_ref, carry_ref, out_ref):
    size = out_ref.shape[1]
    run = carry_ref[...]
    for k in range(parts_ref.shape[0]):
        out_ref[k] = run
        run = jnp.exp(parts_ref[k, size : size + 1, :]) * run + parts_ref[k, :size, :]


def halves(pieces, columns, ref):
    half = SPAN // 2
    return [(pieces[0].at[:, columns], ref.at[:half]), (pieces[1].at[:, columns], ref.at[half:])]


def local_kernel(bias_ref, decay_ref, skip_ref, top_hbm, bottom_hbm, mixed_hbm, state_hbm, *scratch):
    x_ref, coefs_ref, mixed_ref, state_ref, gets, puts = scratch
    inner, heads = x_ref.shape[1], bias_ref.shape[1]
    step = inner // 4
    pieces = (top_hbm, bottom_hbm)
    coefs_in = copies(halves(pieces, slice(2 * inner, None), coefs_ref), gets)
    x_in = [
        copies(halves(pieces, pl.ds(i * step, step), x_ref.at[:, pl.ds(i * step, step)]), gets, 2 + 2 * i)
        for i in range(4)
    ]
    for copy in coefs_in:
        copy.wait()
    b, c = coefs_ref[:, :SPAN], coefs_ref[:, SPAN : 2 * SPAN]
    step_t, cumulative_t = steps_of(coefs_ref[:heads, 2 * SPAN :], bias_ref[...], decay_ref[...])
    cumulative = jnp.transpose(cumulative_t)
    scores = lax.dot_general(c, b, (((1,), (1,)), ((), ())), preferred_element_type=F32)
    rows = lax.broadcasted_iota(jnp.int32, (SPAN, SPAN), 0)
    columns = lax.broadcasted_iota(jnp.int32, (SPAN, SPAN), 1)
    causal = rows >= columns
    low = first_lanes((SPAN, SPAN))
    each = step // SPAN
    out = []
    for pair, state, _ in fresh_states(x_ref, b, step_t, cumulative_t, x_in):
        lanes = slice(pair * SPAN, (pair + 1) * SPAN)
        state_ref[lanes, :] = state
        x = x_ref[:, lanes]
        weights = []
        for h in (2 * pair, 2 * pair + 1):
            gap = column(cumulative, h) - cumulative_t[h : h + 1, :]
            within = jnp.exp(jnp.where(causal, gap, -jnp.inf))
            weights.append(jnp.concatenate(split(scores * within * step_t[h : h + 1, :]), axis=1))
        both = dot(jnp.concatenate(weights, axis=0), jnp.concatenate([x, x], axis=0))
        mixed_ref[:, lanes] = jnp.where(low, both[:SPAN], both[SPAN:]) + skip_ref[:, lanes] * x.astype(F32)
        if pair % each == each - 1:
            part = pl.ds(pair // each * step, step)
            out += copies(
                [
                    (state_ref.at[part], state_hbm.at[part]),
                    (mixed_ref.at[:, part], mixed_hbm.at[:, part]),
                ],
                puts,
                len(out),
            )
    for copy in out:
        copy.wait()


def fold_kernel(n, place_ref, bias_ref, decay_ref, *refs):
    states, mixed, blocks = refs[:n], refs[n : 2 * n], refs[2 * n : 4 * n]
    out, (enter_ref, logs_ref, mixed_ref, coefs_ref, gets, puts) = refs[4 * n : 5 * n], refs[5 * n :]
    inner, heads = mixed_ref.shape[2], bias_ref.shape[1]
    pairs = inner // SPAN
    coefs_in, state_in, mixed_in = [], [], []
    for i in range(n):
        coefs_in += copies(
            halves(blocks[2 * i : 2 * i + 2], slice(2 * inner, None), coefs_ref.at[i]), gets, 2 * i
        )
    for i in range(n):
        state_in += copies([(states[i], enter_ref.at[place_ref[i]])], gets, 2 * n + i)
    for i in range(n):
        mixed_in += copies([(mixed[i], mixed_ref.at[i])], gets, 3 * n + i)
    for copy in coefs_in:
        copy.wait()
    for i in range(n):
        raw_t = coefs_ref[i, :heads, 2 * SPAN :]
        logs_ref[place_ref[i]] = steps_of(raw_t, bias_ref[...], decay_ref[...])[1]
    for copy in state_in:
        copy.wait()
    for pair in range(pairs):
        lanes = slice(pair * SPAN, (pair + 1) * SPAN)
        run = jnp.zeros((SPAN, SPAN), F32)
        for p in range(n):
            fresh = enter_ref[p, lanes, :]
            enter_ref[p, lanes, :] = run
            run = jnp.exp(pair_row(logs_ref[p, :, SPAN - 1 :], pair)) * run + fresh
    low = first_lanes((SPAN, SPAN))
    out_copies = []
    for i in range(n):
        mixed_in[i].wait()
        place = place_ref[i]
        cumulative = jnp.transpose(logs_ref[place])
        c = coefs_ref[i, :, SPAN : 2 * SPAN]
        c_twice = jnp.concatenate([c, c], axis=1)
        for pair in range(pairs):
            lanes = slice(pair * SPAN, (pair + 1) * SPAN)
            at = jnp.where(low, column(cumulative, 2 * pair), column(cumulative, 2 * pair + 1))
            carried = dot(c_twice, jnp.concatenate(split(enter_ref[place, lanes, :]), axis=0))
            mixed_ref[i, :, lanes] += carried * jnp.exp(at)
        out_copies += copies([(mixed_ref.at[i], out[i])], puts, i)
    for copy in out_copies:
        copy.wait()


def mix_kernel(n, place_ref, bias_ref, decay_ref, gain_ref, enter_ref, *refs):
    mixed, blocks, weight_hbm = refs[:n], refs[n : 3 * n], refs[3 * n]
    out_ref, logs_ref, mixed_ref, block_ref, normed_ref, weight_ref, semaphores = refs[3 * n + 1 :]
    inner, heads = mixed_ref.shape[2], bias_ref.shape[1]
    pairs = inner // SPAN
    block_in, mixed_in = [], []
    for i in range(n):
        block_in += copies(
            halves(blocks[2 * i : 2 * i + 2], slice(inner, None), block_ref.at[i]), semaphores, 2 * i
        )
        mixed_in += copies([(mixed[i], mixed_ref.at[i])], semaphores, 2 * n + i)
    (weight_in,) = copies([(weight_hbm, weight_ref)], semaphores, 3 * n)
    for i in range(n):
        for copy in block_in[2 * i : 2 * i + 2]:
            copy.wait()
        raw_t = block_ref[i, :heads, inner + 2 * SPAN :]
        logs_ref[place_ref[i]] = steps_of(raw_t, bias_ref[...], decay_ref[...])[1]
    before = jnp.zeros((heads, 1), F32)
    for p in range(n):
        here = logs_ref[p]
        logs_ref[p] = here + before
        before = before + here[:, SPAN - 1 :]
    low = first_lanes((SPAN, SPAN))
    for i in range(n):
        mixed_in[i].wait()
        place = place_ref[i]
        cumulative = jnp.transpose(logs_ref[place])
        c = block_ref[i, :, inner + SPAN : inner + 2 * SPAN]
        c_twice = jnp.concatenate([c, c], axis=1)
        squares = jnp.zeros((SPAN, SPAN), F32)
        for pair in range(pairs):
            lanes = slice(pair * SPAN, (pair + 1) * SPAN)
            at = jnp.where(low, column(cumulative, 2 * pair), column(cumulative, 2 * pair + 1))
            carried = dot(c_twice, jnp.concatenate(split(enter_ref[lanes, :]), axis=0))
            mixer_out = mixed_ref[i, :, lanes] + carried * jnp.exp(at)
            gate = block_ref[i, :, lanes].astype(F32)
            gated = mixer_out * (gate / (1.0 + jnp.exp(-gate)))
            mixed_ref[i, :, lanes] = gated
            squares += gated * gated
        root = lax.rsqrt(jnp.sum(squares, axis=-1, keepdims=True) / inner + EPSILON)
        to = pl.ds(pl.multiple_of(place * SPAN, SPAN), SPAN)
        for pair in range(pairs):
            lanes = slice(pair * SPAN, (pair + 1) * SPAN)
            normed_ref[to, lanes] = (mixed_ref[i, :, lanes] * root * gain_ref[:, lanes]).astype(BF16)
    weight_in.wait()
    for tile in range(weight_ref.shape[0] // (2 * SPAN)):
        columns = slice(2 * tile * SPAN, 2 * (tile + 1) * SPAN)
        product = lax.dot_general(
            normed_ref[...], weight_ref[columns, :], (((1,), (1,)), ((), ())), preferred_element_type=F32
        )
        out_ref[:, columns] = product.astype(BF16)


def finish_kernel(late_ref, parts_ref, residual_ref, gain_ref, out_ref, combined_ref, *, n_x, n_t, n_z):
    late = late_ref[0] > 0
    tokens = residual_ref.shape[0]
    sums = []
    for x in range(n_x):
        total = parts_ref[x * n_t].astype(F32)
        for t in range(1, n_t):
            total += parts_ref[x * n_t + t].astype(F32)
        sums.append(total)
    squares = jnp.zeros((tokens, 2 * HEAD_DIM), F32)
    for z in range(n_z):
        piece = slice(z * 2 * HEAD_DIM, (z + 1) * 2 * HEAD_DIM)
        own = [total[:, piece] for total in sums]
        swapped = [jnp.concatenate([a[:, HEAD_DIM:], a[:, :HEAD_DIM]], axis=1) for a in own]
        ordered = [jnp.where(late, b, a) for a, b in zip(own, swapped)]
        for yh in range(2):
            for x in range(0, n_x, 2):
                block = ((yh * n_z + z) * n_x + x) // 2
                lanes = slice(block * 2 * HEAD_DIM, (block + 1) * 2 * HEAD_DIM)
                half = slice(yh * HEAD_DIM, (yh + 1) * HEAD_DIM)
                both = jnp.concatenate([ordered[x][:, half], ordered[x + 1][:, half]], axis=1)
                combined = residual_ref[:, lanes].astype(F32) + both
                combined_ref[:, lanes] = combined
                squares += combined * combined
    root = lax.rsqrt(jnp.sum(squares, axis=-1, keepdims=True) / combined_ref.shape[1] + EPSILON)
    out_ref[...] = (combined_ref[...] * root * gain_ref[...]).astype(BF16)


def ring(n, by):
    return [(i, (i + by) % n) for i in range(n)]


def on_device(
    mixer_values,
    gate_values,
    input_coefs,
    output_coefs,
    step_raw,
    step_bias,
    decay_log,
    skip_gain,
    group_gain,
    carry_state,
    out_weight,
    residual,
    final_gain,
):
    tokens, inner = mixer_values.shape
    heads = step_raw.shape[1]
    n_z, n_x = lax.axis_size("z"), lax.axis_size("x")
    n_t = lax.axis_size("yl") * lax.axis_size("core")
    groups = 2 * n_z
    at_x = lax.axis_index("x")
    late = lax.axis_index("yh").astype(jnp.int32).reshape(1)
    bias, decay = step_bias.reshape(1, heads), decay_log.reshape(1, heads)
    skip = jnp.repeat(skip_gain, HEAD_DIM).reshape(1, inner)
    pairs = heads // 2
    quarter = inner // n_x
    size = quarter // groups
    packed = 2 * inner + 3 * SPAN

    half_block = jax.ShapeDtypeStruct((tokens // 2, packed), BF16)
    values = jax.ShapeDtypeStruct((tokens, inner), F32)

    weight = out_weight.T
    across = lax.ppermute(weight, "yh", ring(2, 1))

    states, top, bottom = call(
        states_kernel,
        [jax.ShapeDtypeStruct((n_x, quarter + EXTRA, SPAN), F32), half_block, half_block],
        scratch=[
            pltpu.VMEM((tokens, packed), BF16),
            pltpu.VMEM((1, heads), F32),
            pltpu.VMEM((1, heads), F32),
            pltpu.SemaphoreType.DMA((9,)),
        ],
        flops=2 * tokens * inner * STATE * 2,
        hbm_outs=2,
        args=(mixer_values, gate_values, input_coefs, output_coefs, step_raw.T, bias, decay),
    )
    parts = lax.all_to_all(states, "x", 0, 0, tiled=True)
    across, parts = lax.optimization_barrier((across, parts))
    weight = jnp.concatenate([weight, across], axis=0)
    weight = lax.all_gather(weight, "z", axis=0, tiled=True)

    parts, top, bottom = lax.optimization_barrier((parts, top, bottom))
    own = (top, bottom)
    left = tuple(lax.ppermute(a, "x", ring(n_x, 1)) for a in own)
    right = tuple(lax.ppermute(a, "x", ring(n_x, -1)) for a in (bottom, top))[::-1]
    place = (at_x + jnp.array([0, n_x - 1, 1, 2], jnp.int32)) % n_x

    def local(block):
        return call(
            local_kernel,
            [values, jax.ShapeDtypeStruct((inner, SPAN), F32)],
            scratch=[
                pltpu.VMEM((tokens, inner), BF16),
                pltpu.VMEM((tokens, 3 * SPAN), BF16),
                pltpu.VMEM((tokens, inner), F32),
                pltpu.VMEM((inner, SPAN), F32),
                pltpu.SemaphoreType.DMA((10,)),
                pltpu.SemaphoreType.DMA((8,)),
            ],
            flops=10**6,
            vmem=3,
            hbm_outs=2,
            args=(bias, decay, skip, *block),
        )

    (grouped,) = call(
        group_kernel,
        [jax.ShapeDtypeStruct((groups, size + EXTRA, SPAN), F32)],
        flops=10**6,
        vmem=1,
        args=(parts,),
    )
    parts = lax.all_to_all(grouped, GROUPS, 0, 0, tiled=True)
    own_local, parts, onward, back = lax.optimization_barrier((local(own), parts, left[0], right[1]))
    left, right = (onward, left[1]), (right[0], back)
    far = (lax.ppermute(onward, "x", ring(n_x, 1)), lax.ppermute(back, "x", ring(n_x, -1)))
    mine = lax.axis_index(GROUPS)
    each = STATE // size
    carry = lax.dynamic_index_in_dim(
        carry_state.reshape(pairs, SPAN, STATE), at_x * (pairs // n_x) + mine // each, 0, False
    )
    carry = lax.dynamic_slice_in_dim(carry.T, (mine % each) * size, size, 0)
    (entering,) = call(
        enter_kernel,
        [jax.ShapeDtypeStruct((groups, size, SPAN), F32)],
        flops=10**6,
        vmem=2,
        args=(parts, carry),
    )
    entering = lax.all_to_all(entering, GROUPS, 0, 0, tiled=True).reshape(1, quarter, SPAN)
    entering, left_local, right_local, far = lax.optimization_barrier((entering, local(left), local(right), far))
    entering = lax.all_to_all(jnp.broadcast_to(entering, (n_x, quarter, SPAN)), "x", 0, 0, tiled=True)

    mixed, fresh = zip(own_local, left_local, right_local, local(far))
    blocks = (*own, *left, *right, *far)
    mixed = call(
        functools.partial(fold_kernel, n_x),
        [values] * n_x,
        scratch=[
            pltpu.VMEM((n_x, inner, SPAN), F32),
            pltpu.VMEM((n_x, heads, SPAN), F32),
            pltpu.VMEM((n_x, tokens, inner), F32),
            pltpu.VMEM((n_x, tokens, 3 * SPAN), BF16),
            pltpu.SemaphoreType.DMA((4 * n_x,)),
            pltpu.SemaphoreType.DMA((n_x,)),
        ],
        flops=2 * n_x * tokens * inner * STATE * 2,
        smem=1,
        vmem=2,
        hbm_outs=n_x,
        args=(place, bias, decay, *fresh, *mixed, *blocks),
    )
    (partial,) = call(
        functools.partial(mix_kernel, n_x),
        [jax.ShapeDtypeStruct((n_x * tokens, weight.shape[0]), BF16)],
        scratch=[
            pltpu.VMEM((n_x, heads, SPAN), F32),
            pltpu.VMEM((n_x, tokens, inner), F32),
            pltpu.VMEM((n_x, tokens, packed - inner), BF16),
            pltpu.VMEM((n_x * tokens, inner), BF16),
            pltpu.VMEM(weight.shape, BF16),
            pltpu.SemaphoreType.DMA((3 * n_x + 1,)),
        ],
        flops=2 * n_x * tokens * inner * (STATE * 2 + weight.shape[0]),
        smem=1,
        vmem=4,
        args=(
            place,
            bias,
            decay,
            group_gain.reshape(1, inner),
            entering.reshape(inner, SPAN),
            *mixed,
            *blocks,
            weight,
        ),
    )
    partial = lax.all_to_all(partial, ("x", *TENSOR), 0, 0, tiled=True)
    rows = residual.shape[0]
    (done,) = call(
        functools.partial(finish_kernel, n_x=n_x, n_t=n_t, n_z=n_z),
        [jax.ShapeDtypeStruct(residual.shape, BF16)],
        scratch=[pltpu.VMEM(residual.shape, F32)],
        flops=10**6,
        smem=1,
        vmem=3,
        args=(late, partial.reshape(n_x * n_t, rows, weight.shape[0]), residual, final_gain.reshape(1, -1)),
    )
    across = lax.ppermute(done, "yl", ring(2, 1))
    mine_two = jnp.stack([done, across])
    theirs_two = lax.ppermute(mine_two, "core", ring(2, 1))
    first_y, first_core = lax.axis_index("yl") == 0, lax.axis_index("core") == 0
    even = jnp.where(first_core, mine_two, theirs_two)
    odd = jnp.where(first_core, theirs_two, mine_two)
    low = jnp.where(first_y, jnp.stack([even[0], odd[0]]), jnp.stack([even[1], odd[1]]))
    high = jnp.where(first_y, jnp.stack([even[1], odd[1]]), jnp.stack([even[0], odd[0]]))
    return jnp.concatenate([low, high]).reshape(tokens, residual.shape[1])


def solution(mesh):
    fine = Mesh(mesh.devices.reshape(2, 8, 4, 2, 2), (*CONTEXT, *TENSOR))
    return jax.shard_map(
        on_device,
        mesh=fine,
        in_specs=(
            P(CONTEXT, TENSOR),
            P(CONTEXT, TENSOR),
            P(CONTEXT, TENSOR),
            P(CONTEXT, TENSOR),
            P(CONTEXT, TENSOR),
            P(TENSOR),
            P(TENSOR),
            P(TENSOR),
            P(TENSOR),
            P(TENSOR, None, None),
            P(TENSOR, CONTEXT),
            P((*CONTEXT, *TENSOR), None),
            P(),
        ),
        out_specs=P(CONTEXT, None),
        check_vma=False,
    )
```

```python
import functools

import jax
import jax.numpy as jnp
from jax import lax
from jax.experimental import pallas as pl
from jax.experimental.pallas import tpu as pltpu
from jax.sharding import Mesh, PartitionSpec as P

EPSILON = 1e-05
HIGHEST = lax.Precision.HIGHEST
SPAN = 128
STATE = 128
HEAD_DIM = 64
EXTRA = 8
BF16, F32 = jnp.bfloat16, jnp.float32
CONTEXT = ("yh", "z", "x")
TENSOR = ("yl", "core")
GROUPS = ("yh", "z")
VMEM_LIMIT = 14 * 2**20
VMEM_MOST = 61 * 2**20


def call(kernel, outs, *, scratch=(), flops=0, smem=0, vmem=0, hbm_outs=0, args=()):
    specs = [pl.BlockSpec(memory_space=pltpu.SMEM)] * smem
    specs += [pl.BlockSpec(memory_space=pltpu.VMEM)] * vmem
    specs += [pl.BlockSpec(memory_space=pltpu.HBM)] * (len(args) - smem - vmem)
    places = [pltpu.VMEM] * (len(outs) - hbm_outs) + [pltpu.HBM] * hbm_outs
    moved = sum(a.size * a.dtype.itemsize for a in (*args, *outs))
    return pl.pallas_call(
        kernel,
        out_shape=list(outs),
        in_specs=specs,
        out_specs=[pl.BlockSpec(memory_space=m) for m in places],
        scratch_shapes=scratch,
        compiler_params=pltpu.CompilerParams(
            vmem_limit_bytes=VMEM_MOST if len(args) > smem + vmem else VMEM_LIMIT
        ),
        cost_estimate=pl.CostEstimate(flops=flops, bytes_accessed=moved, transcendentals=0),
    )(*args)


def copies(pairs, semaphores, first=0):
    started = [pltpu.make_async_copy(a, b, semaphores.at[first + i]) for i, (a, b) in enumerate(pairs)]
    for copy in started:
        copy.start()
    return started


def dot(a, b, precision=None):
    return lax.dot_general(
        a, b, (((1,), (0,)), ((), ())), precision=precision, preferred_element_type=F32
    )


def as_column(row):
    square = (row.shape[1], row.shape[1])
    same = lax.broadcasted_iota(jnp.int32, square, 0) == lax.broadcasted_iota(jnp.int32, square, 1)
    return jnp.sum(jnp.where(same, jnp.broadcast_to(row, square), 0.0), axis=1, keepdims=True)


def steps_of(raw_t, bias, decay_log):
    v = raw_t.astype(F32) + as_column(bias)
    step = jnp.maximum(v, 0.0) + jnp.log1p(jnp.exp(-jnp.abs(v)))
    rows = lax.broadcasted_iota(jnp.int32, (SPAN, SPAN), 0)
    columns = lax.broadcasted_iota(jnp.int32, (SPAN, SPAN), 1)
    upper = jnp.where(rows <= columns, 1.0, 0.0).astype(F32)
    return step, dot(-jnp.exp(as_column(decay_log)) * step, upper, HIGHEST)


def split(a):
    high = a.astype(BF16)
    return high, (a - high.astype(F32)).astype(BF16)


def first_lanes(shape):
    return lax.broadcasted_iota(jnp.int32, shape, len(shape) - 1) < HEAD_DIM


def column(a, h):
    return jnp.broadcast_to(a[:, h : h + 1], (a.shape[0], 2 * HEAD_DIM))


def pair_row(a, pair):
    low = first_lanes((1, 2 * HEAD_DIM))
    return jnp.where(low, column(a[2 * pair : 2 * pair + 1], 0), column(a[2 * pair + 1 : 2 * pair + 2], 0))


def fresh_states(x_ref, b, step_t, cumulative_t, x_in=()):
    last = cumulative_t[:, SPAN - 1 : SPAN]
    weight = jnp.transpose(step_t * jnp.exp(last - cumulative_t))
    b_t = jnp.transpose(b)
    b_twice = jnp.concatenate([b_t, b_t], axis=1)
    low = first_lanes((SPAN, SPAN))
    pairs = x_ref.shape[1] // SPAN
    for pair in range(pairs):
        if x_in and pair % (pairs // len(x_in)) == 0:
            for copy in x_in[pair // (pairs // len(x_in))]:
                copy.wait()
        lanes = slice(pair * SPAN, (pair + 1) * SPAN)
        scale = jnp.where(low, column(weight, 2 * pair), column(weight, 2 * pair + 1))
        scaled = x_ref[:, lanes].astype(F32) * scale
        state = dot(b_twice, jnp.concatenate(split(scaled), axis=0))
        yield pair, state, pair_row(last, pair)


def states_kernel(x_hbm, gate_hbm, b_hbm, c_hbm, raw_hbm, bias_hbm, decay_hbm, out_ref, top_hbm, bottom_hbm, *scratch):
    packed_ref, bias_ref, decay_ref, semaphores = scratch
    inner, heads = x_hbm.shape[1], raw_hbm.shape[0]
    at = 2 * inner
    x_ref = packed_ref.at[:, :inner]
    gets = copies(
        [
            (raw_hbm, packed_ref.at[:heads, at + 2 * SPAN :]),
            (bias_hbm, bias_ref),
            (decay_hbm, decay_ref),
            (b_hbm, packed_ref.at[:, at : at + SPAN]),
            (x_hbm, x_ref),
            (c_hbm, packed_ref.at[:, at + SPAN : at + 2 * SPAN]),
            (gate_hbm, packed_ref.at[:, inner:at]),
        ],
        semaphores,
    )
    packed_ref[heads:, at + 2 * SPAN :] = jnp.zeros((SPAN - heads, SPAN), BF16)
    for copy in gets[:3]:
        copy.wait()
    step, cumulative = steps_of(packed_ref[:heads, at + 2 * SPAN :], bias_ref[...], decay_ref[...])
    for copy in gets[3:]:
        copy.wait()
    half = SPAN // 2
    puts = copies([(packed_ref.at[:half], top_hbm), (packed_ref.at[half:], bottom_hbm)], semaphores, len(gets))
    each = out_ref.shape[1] // SPAN
    for pair, state, log in fresh_states(x_ref, packed_ref[:, at : at + SPAN], step, cumulative):
        member, place = divmod(pair, each)
        out_ref[member, place * STATE : (place + 1) * STATE, :] = state
        out_ref[member, each * STATE + place : each * STATE + place + 1, :] = log
    for put in puts:
        put.wait()


def group_kernel(parts_ref, out_ref):
    members, rows, _ = parts_ref.shape
    pairs = rows // STATE
    slices, size = out_ref.shape[0], out_ref.shape[1] - EXTRA
    for pair in range(pairs):
        here = slice(pair * STATE, (pair + 1) * STATE)
        at = pairs * STATE + pair
        log = parts_ref[0, at : at + 1, :]
        state = parts_ref[0, here, :]
        for member in range(1, members):
            more = parts_ref[member, at : at + 1, :]
            state = jnp.exp(more) * state + parts_ref[member, here, :]
            log = log + more
        for i in range(STATE // size):
            out_ref[pair * (STATE // size) + i, :size, :] = state[i * size : (i + 1) * size]
            out_ref[pair * (STATE // size) + i, size:, :] = jnp.broadcast_to(log, (EXTRA, SPAN))


def enter_kernel(parts_ref, carry_ref, out_ref):
    size = out_ref.shape[1]
    run = carry_ref[...]
    for k in range(parts_ref.shape[0]):
        out_ref[k] = run
        run = jnp.exp(parts_ref[k, size : size + 1, :]) * run + parts_ref[k, :size, :]


def halves(pieces, columns, ref):
    half = SPAN // 2
    return [(pieces[0].at[:, columns], ref.at[:half]), (pieces[1].at[:, columns], ref.at[half:])]


def local_block(x_ref, coefs_ref, bias_ref, decay_ref, skip_ref, mixed_ref, state_ref, x_in=(), after=None):
    heads = bias_ref.shape[1]
    b, c = coefs_ref[:, :SPAN], coefs_ref[:, SPAN : 2 * SPAN]
    step_t, cumulative_t = steps_of(coefs_ref[:heads, 2 * SPAN :], bias_ref[...], decay_ref[...])
    cumulative = jnp.transpose(cumulative_t)
    scores = lax.dot_general(c, b, (((1,), (1,)), ((), ())), preferred_element_type=F32)
    rows = lax.broadcasted_iota(jnp.int32, (SPAN, SPAN), 0)
    columns = lax.broadcasted_iota(jnp.int32, (SPAN, SPAN), 1)
    causal = rows >= columns
    low = first_lanes((SPAN, SPAN))
    for pair, state, _ in fresh_states(x_ref, b, step_t, cumulative_t, x_in):
        lanes = slice(pair * SPAN, (pair + 1) * SPAN)
        state_ref[lanes, :] = state
        x = x_ref[:, lanes]
        weights = []
        for h in (2 * pair, 2 * pair + 1):
            gap = column(cumulative, h) - cumulative_t[h : h + 1, :]
            within = jnp.exp(jnp.where(causal, gap, -jnp.inf))
            weights.append(jnp.concatenate(split(scores * within * step_t[h : h + 1, :]), axis=1))
        both = dot(jnp.concatenate(weights, axis=0), jnp.concatenate([x, x], axis=0))
        mixed_ref[:, lanes] = jnp.where(low, both[:SPAN], both[SPAN:]) + skip_ref[:, lanes] * x.astype(F32)
        if after is not None:
            after(pair)
    return cumulative_t


def local_kernel(bias_ref, decay_ref, skip_ref, top_hbm, bottom_hbm, mixed_hbm, state_hbm, *scratch):
    x_ref, coefs_ref, mixed_ref, state_ref, gets, puts = scratch
    inner = x_ref.shape[1]
    step = inner // 4
    each = step // SPAN
    pieces = (top_hbm, bottom_hbm)
    coefs_in = copies(halves(pieces, slice(2 * inner, None), coefs_ref), gets)
    x_in = [
        copies(halves(pieces, pl.ds(i * step, step), x_ref.at[:, pl.ds(i * step, step)]), gets, 2 + 2 * i)
        for i in range(4)
    ]
    for copy in coefs_in:
        copy.wait()
    out = []

    def after(pair):
        if pair % each == each - 1:
            part = pl.ds(pair // each * step, step)
            moves = [(state_ref.at[part], state_hbm.at[part]), (mixed_ref.at[:, part], mixed_hbm.at[:, part])]
            out.extend(copies(moves, puts, len(out)))

    local_block(x_ref, coefs_ref, bias_ref, decay_ref, skip_ref, mixed_ref, state_ref, x_in, after)
    for copy in out:
        copy.wait()


def fold_kernel(n, place_ref, bias_ref, decay_ref, skip_ref, state_hbm, own_hbm, *refs):
    blocks, out = refs[: 2 * n], refs[2 * n : 3 * n]
    x_ref, enter_ref, logs_ref, mixed_ref, coefs_ref, gets, puts = refs[3 * n :]
    inner, heads = mixed_ref.shape[2], bias_ref.shape[1]
    pairs = inner // SPAN
    coefs_in, x_in = [], []
    for i in range(n):
        pieces = blocks[2 * i : 2 * i + 2]
        coefs_in.append(copies(halves(pieces, slice(2 * inner, None), coefs_ref.at[i]), gets, 2 * i))
        if i:
            x_in.append(copies(halves(pieces, slice(0, inner), x_ref.at[i - 1]), gets, 2 * (n + i)))
    own_in = copies([(state_hbm, enter_ref.at[place_ref[0]]), (own_hbm, mixed_ref.at[0])], gets, 2 * n)
    for i in range(n):
        for copy in coefs_in[i]:
            copy.wait()
        place = place_ref[i]
        if i:
            logs_ref[place] = local_block(
                x_ref.at[i - 1],
                coefs_ref.at[i],
                bias_ref,
                decay_ref,
                skip_ref,
                mixed_ref.at[i],
                enter_ref.at[place],
                [x_in[i - 1]],
            )
        else:
            logs_ref[place] = steps_of(coefs_ref[i, :heads, 2 * SPAN :], bias_ref[...], decay_ref[...])[1]
    for copy in own_in:
        copy.wait()
    for pair in range(pairs):
        lanes = slice(pair * SPAN, (pair + 1) * SPAN)
        run = jnp.zeros((SPAN, SPAN), F32)
        for p in range(n):
            fresh = enter_ref[p, lanes, :]
            enter_ref[p, lanes, :] = run
            run = jnp.exp(pair_row(logs_ref[p, :, SPAN - 1 :], pair)) * run + fresh
    low = first_lanes((SPAN, SPAN))
    out_copies = []
    for i in range(n):
        place = place_ref[i]
        cumulative = jnp.transpose(logs_ref[place])
        c = coefs_ref[i, :, SPAN : 2 * SPAN]
        c_twice = jnp.concatenate([c, c], axis=1)
        for pair in range(pairs):
            lanes = slice(pair * SPAN, (pair + 1) * SPAN)
            at = jnp.where(low, column(cumulative, 2 * pair), column(cumulative, 2 * pair + 1))
            carried = dot(c_twice, jnp.concatenate(split(enter_ref[place, lanes, :]), axis=0))
            mixed_ref[i, :, lanes] += carried * jnp.exp(at)
        out_copies += copies([(mixed_ref.at[i], out[i])], puts, i)
    for copy in out_copies:
        copy.wait()


def mix_kernel(n, place_ref, bias_ref, decay_ref, gain_ref, enter_ref, *refs):
    mixed, blocks, weight_hbm = refs[:n], refs[n : 3 * n], refs[3 * n]
    out_ref, logs_ref, mixed_ref, block_ref, normed_ref, weight_ref, semaphores = refs[3 * n + 1 :]
    inner, heads = mixed_ref.shape[2], bias_ref.shape[1]
    pairs = inner // SPAN
    block_in, mixed_in = [], []
    for i in range(n):
        block_in += copies(
            halves(blocks[2 * i : 2 * i + 2], slice(inner, None), block_ref.at[i]), semaphores, 2 * i
        )
        mixed_in += copies([(mixed[i], mixed_ref.at[i])], semaphores, 2 * n + i)
    (weight_in,) = copies([(weight_hbm, weight_ref)], semaphores, 3 * n)
    for i in range(n):
        for copy in block_in[2 * i : 2 * i + 2]:
            copy.wait()
        raw_t = block_ref[i, :heads, inner + 2 * SPAN :]
        logs_ref[place_ref[i]] = steps_of(raw_t, bias_ref[...], decay_ref[...])[1]
    before = jnp.zeros((heads, 1), F32)
    for p in range(n):
        here = logs_ref[p]
        logs_ref[p] = here + before
        before = before + here[:, SPAN - 1 :]
    low = first_lanes((SPAN, SPAN))
    for i in range(n):
        mixed_in[i].wait()
        place = place_ref[i]
        cumulative = jnp.transpose(logs_ref[place])
        c = block_ref[i, :, inner + SPAN : inner + 2 * SPAN]
        c_twice = jnp.concatenate([c, c], axis=1)
        squares = jnp.zeros((SPAN, SPAN), F32)
        for pair in range(pairs):
            lanes = slice(pair * SPAN, (pair + 1) * SPAN)
            at = jnp.where(low, column(cumulative, 2 * pair), column(cumulative, 2 * pair + 1))
            carried = dot(c_twice, jnp.concatenate(split(enter_ref[lanes, :]), axis=0))
            mixer_out = mixed_ref[i, :, lanes] + carried * jnp.exp(at)
            gate = block_ref[i, :, lanes].astype(F32)
            gated = mixer_out * (gate / (1.0 + jnp.exp(-gate)))
            mixed_ref[i, :, lanes] = gated
            squares += gated * gated
        root = lax.rsqrt(jnp.sum(squares, axis=-1, keepdims=True) / inner + EPSILON)
        to = pl.ds(pl.multiple_of(place * SPAN, SPAN), SPAN)
        for pair in range(pairs):
            lanes = slice(pair * SPAN, (pair + 1) * SPAN)
            normed_ref[to, lanes] = (mixed_ref[i, :, lanes] * root * gain_ref[:, lanes]).astype(BF16)
    weight_in.wait()
    for tile in range(weight_ref.shape[0] // (2 * SPAN)):
        columns = slice(2 * tile * SPAN, 2 * (tile + 1) * SPAN)
        product = lax.dot_general(
            normed_ref[...], weight_ref[columns, :], (((1,), (1,)), ((), ())), preferred_element_type=F32
        )
        out_ref[:, columns] = product.astype(BF16)


def finish_kernel(late_ref, parts_ref, residual_ref, gain_ref, out_ref, combined_ref, *, n_x, n_t, n_z):
    late = late_ref[0] > 0
    tokens = residual_ref.shape[0]
    sums = []
    for x in range(n_x):
        total = parts_ref[x * n_t].astype(F32)
        for t in range(1, n_t):
            total += parts_ref[x * n_t + t].astype(F32)
        sums.append(total)
    squares = jnp.zeros((tokens, 2 * HEAD_DIM), F32)
    for z in range(n_z):
        piece = slice(z * 2 * HEAD_DIM, (z + 1) * 2 * HEAD_DIM)
        own = [total[:, piece] for total in sums]
        swapped = [jnp.concatenate([a[:, HEAD_DIM:], a[:, :HEAD_DIM]], axis=1) for a in own]
        ordered = [jnp.where(late, b, a) for a, b in zip(own, swapped)]
        for yh in range(2):
            for x in range(0, n_x, 2):
                block = ((yh * n_z + z) * n_x + x) // 2
                lanes = slice(block * 2 * HEAD_DIM, (block + 1) * 2 * HEAD_DIM)
                half = slice(yh * HEAD_DIM, (yh + 1) * HEAD_DIM)
                both = jnp.concatenate([ordered[x][:, half], ordered[x + 1][:, half]], axis=1)
                combined = residual_ref[:, lanes].astype(F32) + both
                combined_ref[:, lanes] = combined
                squares += combined * combined
    root = lax.rsqrt(jnp.sum(squares, axis=-1, keepdims=True) / combined_ref.shape[1] + EPSILON)
    out_ref[...] = (combined_ref[...] * root * gain_ref[...]).astype(BF16)


def ring(n, by):
    return [(i, (i + by) % n) for i in range(n)]


def on_device(
    mixer_values,
    gate_values,
    input_coefs,
    output_coefs,
    step_raw,
    step_bias,
    decay_log,
    skip_gain,
    group_gain,
    carry_state,
    out_weight,
    residual,
    final_gain,
):
    tokens, inner = mixer_values.shape
    heads = step_raw.shape[1]
    n_z, n_x = lax.axis_size("z"), lax.axis_size("x")
    n_t = lax.axis_size("yl") * lax.axis_size("core")
    groups = 2 * n_z
    at_x = lax.axis_index("x")
    late = lax.axis_index("yh").astype(jnp.int32).reshape(1)
    bias, decay = step_bias.reshape(1, heads), decay_log.reshape(1, heads)
    skip = jnp.repeat(skip_gain, HEAD_DIM).reshape(1, inner)
    pairs = heads // 2
    quarter = inner // n_x
    size = quarter // groups
    packed = 2 * inner + 3 * SPAN

    half_block = jax.ShapeDtypeStruct((tokens // 2, packed), BF16)
    values = jax.ShapeDtypeStruct((tokens, inner), F32)

    weight = out_weight.T
    across = lax.ppermute(weight, "yh", ring(2, 1))

    states, top, bottom = call(
        states_kernel,
        [jax.ShapeDtypeStruct((n_x, quarter + EXTRA, SPAN), F32), half_block, half_block],
        scratch=[
            pltpu.VMEM((tokens, packed), BF16),
            pltpu.VMEM((1, heads), F32),
            pltpu.VMEM((1, heads), F32),
            pltpu.SemaphoreType.DMA((9,)),
        ],
        flops=2 * tokens * inner * STATE * 2,
        hbm_outs=2,
        args=(mixer_values, gate_values, input_coefs, output_coefs, step_raw.T, bias, decay),
    )
    parts = lax.all_to_all(states, "x", 0, 0, tiled=True)
    across, parts = lax.optimization_barrier((across, parts))
    weight = jnp.concatenate([weight, across], axis=0)
    weight = lax.all_gather(weight, "z", axis=0, tiled=True)

    parts, top, bottom = lax.optimization_barrier((parts, top, bottom))
    own = (top, bottom)
    left_top = lax.ppermute(top, "x", ring(n_x, 1))
    right_bottom = lax.ppermute(bottom, "x", ring(n_x, -1))
    place = (at_x + jnp.array([0, n_x - 1, 1, 2], jnp.int32)) % n_x

    own_local = call(
        local_kernel,
        [values, jax.ShapeDtypeStruct((inner, SPAN), F32)],
        scratch=[
            pltpu.VMEM((tokens, inner), BF16),
            pltpu.VMEM((tokens, 3 * SPAN), BF16),
            pltpu.VMEM((tokens, inner), F32),
            pltpu.VMEM((inner, SPAN), F32),
            pltpu.SemaphoreType.DMA((10,)),
            pltpu.SemaphoreType.DMA((8,)),
        ],
        flops=10**6,
        vmem=3,
        hbm_outs=2,
        args=(bias, decay, skip, *own),
    )

    (grouped,) = call(
        group_kernel,
        [jax.ShapeDtypeStruct((groups, size + EXTRA, SPAN), F32)],
        flops=10**6,
        vmem=1,
        args=(parts,),
    )
    parts = lax.all_to_all(grouped, GROUPS, 0, 0, tiled=True)
    (mixed, fresh), parts, left_top, right_bottom, top_later, bottom_later = lax.optimization_barrier(
        (own_local, parts, left_top, right_bottom, top, bottom)
    )
    left = (left_top, lax.ppermute(bottom_later, "x", ring(n_x, 1)))
    right = (lax.ppermute(top_later, "x", ring(n_x, -1)), right_bottom)
    far = (lax.ppermute(left_top, "x", ring(n_x, 1)), lax.ppermute(right_bottom, "x", ring(n_x, -1)))
    mine = lax.axis_index(GROUPS)
    each = STATE // size
    carry = lax.dynamic_index_in_dim(
        carry_state.reshape(pairs, SPAN, STATE), at_x * (pairs // n_x) + mine // each, 0, False
    )
    carry = lax.dynamic_slice_in_dim(carry.T, (mine % each) * size, size, 0)
    (entering,) = call(
        enter_kernel,
        [jax.ShapeDtypeStruct((groups, size, SPAN), F32)],
        flops=10**6,
        vmem=2,
        args=(parts, carry),
    )
    entering = lax.all_to_all(entering, GROUPS, 0, 0, tiled=True).reshape(1, quarter, SPAN)
    entering, left, right, far = lax.optimization_barrier((entering, left, right, far))
    entering = lax.all_to_all(jnp.broadcast_to(entering, (n_x, quarter, SPAN)), "x", 0, 0, tiled=True)

    blocks = (*own, *left, *right, *far)
    mixed = call(
        functools.partial(fold_kernel, n_x),
        [values] * n_x,
        scratch=[
            pltpu.VMEM((n_x - 1, tokens, inner), BF16),
            pltpu.VMEM((n_x, inner, SPAN), F32),
            pltpu.VMEM((n_x, heads, SPAN), F32),
            pltpu.VMEM((n_x, tokens, inner), F32),
            pltpu.VMEM((n_x, tokens, 3 * SPAN), BF16),
            pltpu.SemaphoreType.DMA((4 * n_x,)),
            pltpu.SemaphoreType.DMA((n_x,)),
        ],
        flops=2 * n_x * tokens * inner * STATE * 2,
        smem=1,
        vmem=3,
        hbm_outs=n_x,
        args=(place, bias, decay, skip, fresh, mixed, *blocks),
    )
    (partial,) = call(
        functools.partial(mix_kernel, n_x),
        [jax.ShapeDtypeStruct((n_x * tokens, weight.shape[0]), BF16)],
        scratch=[
            pltpu.VMEM((n_x, heads, SPAN), F32),
            pltpu.VMEM((n_x, tokens, inner), F32),
            pltpu.VMEM((n_x, tokens, packed - inner), BF16),
            pltpu.VMEM((n_x * tokens, inner), BF16),
            pltpu.VMEM(weight.shape, BF16),
            pltpu.SemaphoreType.DMA((3 * n_x + 1,)),
        ],
        flops=2 * n_x * tokens * inner * (STATE * 2 + weight.shape[0]),
        smem=1,
        vmem=4,
        args=(
            place,
            bias,
            decay,
            group_gain.reshape(1, inner),
            entering.reshape(inner, SPAN),
            *mixed,
            *blocks,
            weight,
        ),
    )
    partial = lax.all_to_all(partial, ("x", *TENSOR), 0, 0, tiled=True)
    rows = residual.shape[0]
    (done,) = call(
        functools.partial(finish_kernel, n_x=n_x, n_t=n_t, n_z=n_z),
        [jax.ShapeDtypeStruct(residual.shape, BF16)],
        scratch=[pltpu.VMEM(residual.shape, F32)],
        flops=10**6,
        smem=1,
        vmem=3,
        args=(late, partial.reshape(n_x * n_t, rows, weight.shape[0]), residual, final_gain.reshape(1, -1)),
    )
    across = lax.ppermute(done, "yl", ring(2, 1))
    mine_two = jnp.stack([done, across])
    theirs_two = lax.ppermute(mine_two, "core", ring(2, 1))
    first_y, first_core = lax.axis_index("yl") == 0, lax.axis_index("core") == 0
    even = jnp.where(first_core, mine_two, theirs_two)
    odd = jnp.where(first_core, theirs_two, mine_two)
    low = jnp.where(first_y, jnp.stack([even[0], odd[0]]), jnp.stack([even[1], odd[1]]))
    high = jnp.where(first_y, jnp.stack([even[1], odd[1]]), jnp.stack([even[0], odd[0]]))
    return jnp.concatenate([low, high]).reshape(tokens, residual.shape[1])


def solution(mesh):
    fine = Mesh(mesh.devices.reshape(2, 8, 4, 2, 2), (*CONTEXT, *TENSOR))
    return jax.shard_map(
        on_device,
        mesh=fine,
        in_specs=(
            P(CONTEXT, TENSOR),
            P(CONTEXT, TENSOR),
            P(CONTEXT, TENSOR),
            P(CONTEXT, TENSOR),
            P(CONTEXT, TENSOR),
            P(TENSOR),
            P(TENSOR),
            P(TENSOR),
            P(TENSOR),
            P(TENSOR, None, None),
            P(TENSOR, CONTEXT),
            P((*CONTEXT, *TENSOR), None),
            P(),
        ),
        out_specs=P(CONTEXT, None),
        check_vma=False,
    )
```

```python
import functools

import jax
import jax.numpy as jnp
from jax import lax
from jax.experimental import pallas as pl
from jax.experimental.pallas import tpu as pltpu
from jax.sharding import Mesh, PartitionSpec as P

EPSILON = 1e-05
HIGHEST = lax.Precision.HIGHEST
SPAN = 128
STATE = 128
HEAD_DIM = 64
EXTRA = 8
BF16, F32 = jnp.bfloat16, jnp.float32
CONTEXT = ("yh", "z", "x")
TENSOR = ("yl", "core")
GROUPS = ("yh", "z")
VMEM_LIMIT = 14 * 2**20
VMEM_MOST = 61 * 2**20


def call(kernel, outs, *, scratch=(), flops=0, smem=0, vmem=0, hbm_outs=0, args=()):
    specs = [pl.BlockSpec(memory_space=pltpu.SMEM)] * smem
    specs += [pl.BlockSpec(memory_space=pltpu.VMEM)] * vmem
    specs += [pl.BlockSpec(memory_space=pltpu.HBM)] * (len(args) - smem - vmem)
    places = [pltpu.VMEM] * (len(outs) - hbm_outs) + [pltpu.HBM] * hbm_outs
    moved = sum(a.size * a.dtype.itemsize for a in (*args, *outs))
    return pl.pallas_call(
        kernel,
        out_shape=list(outs),
        in_specs=specs,
        out_specs=[pl.BlockSpec(memory_space=m) for m in places],
        scratch_shapes=scratch,
        compiler_params=pltpu.CompilerParams(
            vmem_limit_bytes=VMEM_MOST if len(args) > smem + vmem else VMEM_LIMIT
        ),
        cost_estimate=pl.CostEstimate(flops=flops, bytes_accessed=moved, transcendentals=0),
    )(*args)


def copies(pairs, semaphores, first=0):
    started = [pltpu.make_async_copy(a, b, semaphores.at[first + i]) for i, (a, b) in enumerate(pairs)]
    for copy in started:
        copy.start()
    return started


def dot(a, b, precision=None):
    return lax.dot_general(
        a, b, (((1,), (0,)), ((), ())), precision=precision, preferred_element_type=F32
    )


def as_column(row):
    square = (row.shape[1], row.shape[1])
    same = lax.broadcasted_iota(jnp.int32, square, 0) == lax.broadcasted_iota(jnp.int32, square, 1)
    return jnp.sum(jnp.where(same, jnp.broadcast_to(row, square), 0.0), axis=1, keepdims=True)


def steps_of(raw_t, bias, decay_log):
    v = raw_t.astype(F32) + as_column(bias)
    step = jnp.maximum(v, 0.0) + jnp.log1p(jnp.exp(-jnp.abs(v)))
    rows = lax.broadcasted_iota(jnp.int32, (SPAN, SPAN), 0)
    columns = lax.broadcasted_iota(jnp.int32, (SPAN, SPAN), 1)
    upper = jnp.where(rows <= columns, 1.0, 0.0).astype(F32)
    return step, dot(-jnp.exp(as_column(decay_log)) * step, upper, HIGHEST)


def split(a):
    high = a.astype(BF16)
    return high, (a - high.astype(F32)).astype(BF16)


def first_lanes(shape):
    return lax.broadcasted_iota(jnp.int32, shape, len(shape) - 1) < HEAD_DIM


def column(a, h):
    return jnp.broadcast_to(a[:, h : h + 1], (a.shape[0], 2 * HEAD_DIM))


def pair_row(a, pair):
    low = first_lanes((1, 2 * HEAD_DIM))
    return jnp.where(low, column(a[2 * pair : 2 * pair + 1], 0), column(a[2 * pair + 1 : 2 * pair + 2], 0))


def fresh_states(x_ref, b, step_t, cumulative_t, x_in=()):
    last = cumulative_t[:, SPAN - 1 : SPAN]
    weight = jnp.transpose(step_t * jnp.exp(last - cumulative_t))
    b_t = jnp.transpose(b)
    b_twice = jnp.concatenate([b_t, b_t], axis=1)
    low = first_lanes((SPAN, SPAN))
    pairs = x_ref.shape[1] // SPAN
    for pair in range(pairs):
        if x_in and pair % (pairs // len(x_in)) == 0:
            for copy in x_in[pair // (pairs // len(x_in))]:
                copy.wait()
        lanes = slice(pair * SPAN, (pair + 1) * SPAN)
        scale = jnp.where(low, column(weight, 2 * pair), column(weight, 2 * pair + 1))
        scaled = x_ref[:, lanes].astype(F32) * scale
        state = dot(b_twice, jnp.concatenate(split(scaled), axis=0))
        yield pair, state, pair_row(last, pair)


def states_kernel(x_hbm, gate_hbm, b_hbm, c_hbm, raw_hbm, bias_hbm, decay_hbm, out_ref, top_hbm, bottom_hbm, *scratch):
    packed_ref, bias_ref, decay_ref, semaphores = scratch
    inner, heads = x_hbm.shape[1], raw_hbm.shape[0]
    at = 2 * inner
    x_ref = packed_ref.at[:, :inner]
    gets = copies(
        [
            (raw_hbm, packed_ref.at[:heads, at + 2 * SPAN :]),
            (bias_hbm, bias_ref),
            (decay_hbm, decay_ref),
            (b_hbm, packed_ref.at[:, at : at + SPAN]),
            (x_hbm, x_ref),
            (c_hbm, packed_ref.at[:, at + SPAN : at + 2 * SPAN]),
            (gate_hbm, packed_ref.at[:, inner:at]),
        ],
        semaphores,
    )
    packed_ref[heads:, at + 2 * SPAN :] = jnp.zeros((SPAN - heads, SPAN), BF16)
    for copy in gets[:3]:
        copy.wait()
    step, cumulative = steps_of(packed_ref[:heads, at + 2 * SPAN :], bias_ref[...], decay_ref[...])
    for copy in gets[3:]:
        copy.wait()
    half = SPAN // 2
    puts = copies([(packed_ref.at[:half], top_hbm), (packed_ref.at[half:], bottom_hbm)], semaphores, len(gets))
    each = out_ref.shape[1] // SPAN
    for pair, state, log in fresh_states(x_ref, packed_ref[:, at : at + SPAN], step, cumulative):
        member, place = divmod(pair, each)
        out_ref[member, place * STATE : (place + 1) * STATE, :] = state
        out_ref[member, each * STATE + place : each * STATE + place + 1, :] = log
    for put in puts:
        put.wait()


def group_kernel(parts_ref, out_ref):
    members, rows, _ = parts_ref.shape
    pairs = rows // STATE
    slices, size = out_ref.shape[0], out_ref.shape[1] - EXTRA
    for pair in range(pairs):
        here = slice(pair * STATE, (pair + 1) * STATE)
        at = pairs * STATE + pair
        log = parts_ref[0, at : at + 1, :]
        state = parts_ref[0, here, :]
        for member in range(1, members):
            more = parts_ref[member, at : at + 1, :]
            state = jnp.exp(more) * state + parts_ref[member, here, :]
            log = log + more
        for i in range(STATE // size):
            out_ref[pair * (STATE // size) + i, :size, :] = state[i * size : (i + 1) * size]
            out_ref[pair * (STATE // size) + i, size:, :] = jnp.broadcast_to(log, (EXTRA, SPAN))


def enter_kernel(parts_ref, carry_ref, out_ref):
    size = out_ref.shape[1]
    run = carry_ref[...]
    for k in range(parts_ref.shape[0]):
        out_ref[k] = run
        run = jnp.exp(parts_ref[k, size : size + 1, :]) * run + parts_ref[k, :size, :]


def halves(pieces, columns, ref):
    half = SPAN // 2
    return [(pieces[0].at[:, columns], ref.at[:half]), (pieces[1].at[:, columns], ref.at[half:])]


def local_block(x_ref, coefs_ref, bias_ref, decay_ref, skip_ref, mixed_ref, state_ref, x_in=(), after=None):
    heads = bias_ref.shape[1]
    b, c = coefs_ref[:, :SPAN], coefs_ref[:, SPAN : 2 * SPAN]
    step_t, cumulative_t = steps_of(coefs_ref[:heads, 2 * SPAN :], bias_ref[...], decay_ref[...])
    cumulative = jnp.transpose(cumulative_t)
    scores = lax.dot_general(c, b, (((1,), (1,)), ((), ())), preferred_element_type=F32)
    rows = lax.broadcasted_iota(jnp.int32, (SPAN, SPAN), 0)
    columns = lax.broadcasted_iota(jnp.int32, (SPAN, SPAN), 1)
    causal = rows >= columns
    low = first_lanes((SPAN, SPAN))
    for pair, state, _ in fresh_states(x_ref, b, step_t, cumulative_t, x_in):
        lanes = slice(pair * SPAN, (pair + 1) * SPAN)
        state_ref[lanes, :] = state
        x = x_ref[:, lanes]
        weights = []
        for h in (2 * pair, 2 * pair + 1):
            gap = column(cumulative, h) - cumulative_t[h : h + 1, :]
            within = jnp.exp(jnp.where(causal, gap, -jnp.inf))
            weights.append(jnp.concatenate(split(scores * within * step_t[h : h + 1, :]), axis=1))
        both = dot(jnp.concatenate(weights, axis=0), jnp.concatenate([x, x], axis=0))
        mixed_ref[:, lanes] = jnp.where(low, both[:SPAN], both[SPAN:]) + skip_ref[:, lanes] * x.astype(F32)
        if after is not None:
            after(pair)
    return cumulative_t


def local_kernel(bias_ref, decay_ref, skip_ref, top_hbm, bottom_hbm, mixed_hbm, state_hbm, *scratch):
    x_ref, coefs_ref, mixed_ref, state_ref, gets, puts = scratch
    inner = x_ref.shape[1]
    step = inner // 4
    each = step // SPAN
    pieces = (top_hbm, bottom_hbm)
    coefs_in = copies(halves(pieces, slice(2 * inner, None), coefs_ref), gets)
    x_in = [
        copies(halves(pieces, pl.ds(i * step, step), x_ref.at[:, pl.ds(i * step, step)]), gets, 2 + 2 * i)
        for i in range(4)
    ]
    for copy in coefs_in:
        copy.wait()
    out = []

    def after(pair):
        if pair % each == each - 1:
            part = pl.ds(pair // each * step, step)
            moves = [(state_ref.at[part], state_hbm.at[part]), (mixed_ref.at[:, part], mixed_hbm.at[:, part])]
            out.extend(copies(moves, puts, len(out)))

    local_block(x_ref, coefs_ref, bias_ref, decay_ref, skip_ref, mixed_ref, state_ref, x_in, after)
    for copy in out:
        copy.wait()


def fold_kernel(n, place_ref, bias_ref, decay_ref, skip_ref, state_hbm, own_hbm, *refs):
    blocks, out = refs[: 2 * n], refs[2 * n : 3 * n]
    x_ref, enter_ref, logs_ref, mixed_ref, coefs_ref, gets, puts = refs[3 * n :]
    inner, heads = mixed_ref.shape[2], bias_ref.shape[1]
    pairs = inner // SPAN
    coefs_in, x_in = [], []
    for i in range(n):
        pieces = blocks[2 * i : 2 * i + 2]
        coefs_in.append(copies(halves(pieces, slice(2 * inner, None), coefs_ref.at[i]), gets, 2 * i))
        if i:
            x_in.append(copies(halves(pieces, slice(0, inner), x_ref.at[i - 1]), gets, 2 * (n + i)))
    own_in = copies([(state_hbm, enter_ref.at[place_ref[0]]), (own_hbm, mixed_ref.at[0])], gets, 2 * n)
    for i in range(n):
        for copy in coefs_in[i]:
            copy.wait()
        place = place_ref[i]
        if i:
            logs_ref[place] = local_block(
                x_ref.at[i - 1],
                coefs_ref.at[i],
                bias_ref,
                decay_ref,
                skip_ref,
                mixed_ref.at[i],
                enter_ref.at[place],
                [x_in[i - 1]],
            )
        else:
            logs_ref[place] = steps_of(coefs_ref[i, :heads, 2 * SPAN :], bias_ref[...], decay_ref[...])[1]
    for copy in own_in:
        copy.wait()
    for pair in range(pairs):
        lanes = slice(pair * SPAN, (pair + 1) * SPAN)
        run = jnp.zeros((SPAN, SPAN), F32)
        for p in range(n):
            fresh = enter_ref[p, lanes, :]
            enter_ref[p, lanes, :] = run
            run = jnp.exp(pair_row(logs_ref[p, :, SPAN - 1 :], pair)) * run + fresh
    low = first_lanes((SPAN, SPAN))
    out_copies = []
    for i in range(n):
        place = place_ref[i]
        cumulative = jnp.transpose(logs_ref[place])
        c = coefs_ref[i, :, SPAN : 2 * SPAN]
        c_twice = jnp.concatenate([c, c], axis=1)
        for pair in range(pairs):
            lanes = slice(pair * SPAN, (pair + 1) * SPAN)
            at = jnp.where(low, column(cumulative, 2 * pair), column(cumulative, 2 * pair + 1))
            carried = dot(c_twice, jnp.concatenate(split(enter_ref[place, lanes, :]), axis=0))
            mixed_ref[i, :, lanes] += carried * jnp.exp(at)
        out_copies += copies([(mixed_ref.at[i], out[i])], puts, i)
    for copy in out_copies:
        copy.wait()


def mix_kernel(n, place_ref, bias_ref, decay_ref, gain_ref, enter_ref, *refs):
    mixed, blocks, weight_hbm = refs[:n], refs[n : 3 * n], refs[3 * n]
    kept_ref, sent_ref, logs_ref, mixed_ref, block_ref, normed_ref, weight_ref, semaphores = refs[3 * n + 1 :]
    inner, heads = mixed_ref.shape[2], bias_ref.shape[1]
    pairs = inner // SPAN
    block_in, mixed_in = [], []
    for i in range(n):
        block_in += copies(
            halves(blocks[2 * i : 2 * i + 2], slice(inner, None), block_ref.at[i]), semaphores, 2 * i
        )
        mixed_in += copies([(mixed[i], mixed_ref.at[i])], semaphores, 2 * n + i)
    (weight_in,) = copies([(weight_hbm, weight_ref)], semaphores, 3 * n)
    for i in range(n):
        for copy in block_in[2 * i : 2 * i + 2]:
            copy.wait()
        raw_t = block_ref[i, :heads, inner + 2 * SPAN :]
        logs_ref[place_ref[i]] = steps_of(raw_t, bias_ref[...], decay_ref[...])[1]
    before = jnp.zeros((heads, 1), F32)
    for p in range(n):
        here = logs_ref[p]
        logs_ref[p] = here + before
        before = before + here[:, SPAN - 1 :]
    low = first_lanes((SPAN, SPAN))
    for i in range(n):
        mixed_in[i].wait()
        place = place_ref[i]
        cumulative = jnp.transpose(logs_ref[place])
        c = block_ref[i, :, inner + SPAN : inner + 2 * SPAN]
        c_twice = jnp.concatenate([c, c], axis=1)
        squares = jnp.zeros((SPAN, SPAN), F32)
        for pair in range(pairs):
            lanes = slice(pair * SPAN, (pair + 1) * SPAN)
            at = jnp.where(low, column(cumulative, 2 * pair), column(cumulative, 2 * pair + 1))
            carried = dot(c_twice, jnp.concatenate(split(enter_ref[lanes, :]), axis=0))
            mixer_out = mixed_ref[i, :, lanes] + carried * jnp.exp(at)
            gate = block_ref[i, :, lanes].astype(F32)
            gated = mixer_out * (gate / (1.0 + jnp.exp(-gate)))
            mixed_ref[i, :, lanes] = gated
            squares += gated * gated
        root = lax.rsqrt(jnp.sum(squares, axis=-1, keepdims=True) / inner + EPSILON)
        to = pl.ds(pl.multiple_of(place * SPAN, SPAN), SPAN)
        for pair in range(pairs):
            lanes = slice(pair * SPAN, (pair + 1) * SPAN)
            normed_ref[to, lanes] = (mixed_ref[i, :, lanes] * root * gain_ref[:, lanes]).astype(BF16)
    weight_in.wait()
    core, width = place_ref[n], kept_ref.shape[1]
    for ref, side in ((sent_ref, 1 - core), (kept_ref, core)):
        for tile in range(width // (2 * SPAN)):
            columns = slice(2 * tile * SPAN, 2 * (tile + 1) * SPAN)
            rows = pl.ds(pl.multiple_of(side * width + 2 * tile * SPAN, 2 * SPAN), 2 * SPAN)
            ref[:, columns] = lax.dot_general(
                normed_ref[...], weight_ref[rows, :], (((1,), (1,)), ((), ())), preferred_element_type=F32
            )


def finish_kernel(late_ref, parts_ref, residual_ref, gain_ref, out_ref, combined_ref, *, n_x, n_z):
    late = late_ref[0] > 0
    tokens = residual_ref.shape[0]
    sums = []
    for x in range(n_x):
        cores = []
        for core in range(parts_ref.shape[2]):
            total = parts_ref[x, 0, core].astype(F32)
            for y in range(1, parts_ref.shape[1]):
                total += parts_ref[x, y, core].astype(F32)
            cores.append(total)
        sums.append(jnp.concatenate(cores, axis=1))
    squares = jnp.zeros((tokens, 2 * HEAD_DIM), F32)
    for z in range(n_z):
        piece = slice(z * 2 * HEAD_DIM, (z + 1) * 2 * HEAD_DIM)
        own = [total[:, piece] for total in sums]
        swapped = [jnp.concatenate([a[:, HEAD_DIM:], a[:, :HEAD_DIM]], axis=1) for a in own]
        ordered = [jnp.where(late, b, a) for a, b in zip(own, swapped)]
        for yh in range(2):
            for x in range(0, n_x, 2):
                block = ((yh * n_z + z) * n_x + x) // 2
                lanes = slice(block * 2 * HEAD_DIM, (block + 1) * 2 * HEAD_DIM)
                half = slice(yh * HEAD_DIM, (yh + 1) * HEAD_DIM)
                both = jnp.concatenate([ordered[x][:, half], ordered[x + 1][:, half]], axis=1)
                combined = residual_ref[:, lanes].astype(F32) + both
                combined_ref[:, lanes] = combined
                squares += combined * combined
    root = lax.rsqrt(jnp.sum(squares, axis=-1, keepdims=True) / combined_ref.shape[1] + EPSILON)
    out_ref[...] = (combined_ref[...] * root * gain_ref[...]).astype(BF16)


def ring(n, by):
    return [(i, (i + by) % n) for i in range(n)]


def on_device(
    mixer_values,
    gate_values,
    input_coefs,
    output_coefs,
    step_raw,
    step_bias,
    decay_log,
    skip_gain,
    group_gain,
    carry_state,
    out_weight,
    residual,
    final_gain,
):
    tokens, inner = mixer_values.shape
    heads = step_raw.shape[1]
    n_z, n_x = lax.axis_size("z"), lax.axis_size("x")
    n_t = lax.axis_size("yl") * lax.axis_size("core")
    groups = 2 * n_z
    at_x = lax.axis_index("x")
    late = lax.axis_index("yh").astype(jnp.int32).reshape(1)
    bias, decay = step_bias.reshape(1, heads), decay_log.reshape(1, heads)
    skip = jnp.repeat(skip_gain, HEAD_DIM).reshape(1, inner)
    pairs = heads // 2
    quarter = inner // n_x
    size = quarter // groups
    packed = 2 * inner + 3 * SPAN

    half_block = jax.ShapeDtypeStruct((tokens // 2, packed), BF16)
    values = jax.ShapeDtypeStruct((tokens, inner), F32)

    weight = out_weight.T
    across = lax.ppermute(weight, "yh", ring(2, 1))

    states, top, bottom = call(
        states_kernel,
        [jax.ShapeDtypeStruct((n_x, quarter + EXTRA, SPAN), F32), half_block, half_block],
        scratch=[
            pltpu.VMEM((tokens, packed), BF16),
            pltpu.VMEM((1, heads), F32),
            pltpu.VMEM((1, heads), F32),
            pltpu.SemaphoreType.DMA((9,)),
        ],
        flops=2 * tokens * inner * STATE * 2,
        hbm_outs=2,
        args=(mixer_values, gate_values, input_coefs, output_coefs, step_raw.T, bias, decay),
    )
    parts = lax.all_to_all(states, "x", 0, 0, tiled=True)
    across, parts = lax.optimization_barrier((across, parts))
    weight = jnp.concatenate([weight, across], axis=0)
    weight = lax.all_gather(weight, "z", axis=0, tiled=True)

    parts, top, bottom = lax.optimization_barrier((parts, top, bottom))
    own = (top, bottom)
    left_top = lax.ppermute(top, "x", ring(n_x, 1))
    right_bottom = lax.ppermute(bottom, "x", ring(n_x, -1))
    place = (at_x + jnp.array([0, n_x - 1, 1, 2], jnp.int32)) % n_x
    place = jnp.concatenate([place, lax.axis_index("core").astype(jnp.int32).reshape(1)])

    own_local = call(
        local_kernel,
        [values, jax.ShapeDtypeStruct((inner, SPAN), F32)],
        scratch=[
            pltpu.VMEM((tokens, inner), BF16),
            pltpu.VMEM((tokens, 3 * SPAN), BF16),
            pltpu.VMEM((tokens, inner), F32),
            pltpu.VMEM((inner, SPAN), F32),
            pltpu.SemaphoreType.DMA((10,)),
            pltpu.SemaphoreType.DMA((8,)),
        ],
        flops=10**6,
        vmem=3,
        hbm_outs=2,
        args=(bias, decay, skip, *own),
    )

    (grouped,) = call(
        group_kernel,
        [jax.ShapeDtypeStruct((groups, size + EXTRA, SPAN), F32)],
        flops=10**6,
        vmem=1,
        args=(parts,),
    )
    parts = lax.all_to_all(grouped, GROUPS, 0, 0, tiled=True)
    own_local, top_later, bottom_later = lax.optimization_barrier((own_local, top, bottom))
    left_bottom = lax.ppermute(bottom_later, "x", ring(n_x, 1))
    right_top = lax.ppermute(top_later, "x", ring(n_x, -1))
    (mixed, fresh), parts, left_top, right_bottom, place = lax.optimization_barrier(
        (own_local, parts, left_top, right_bottom, place)
    )
    left, right = (left_top, left_bottom), (right_top, right_bottom)
    far = (lax.ppermute(left_top, "x", ring(n_x, 1)), lax.ppermute(right_bottom, "x", ring(n_x, -1)))
    mine = lax.axis_index(GROUPS)
    each = STATE // size
    carry = lax.dynamic_index_in_dim(
        carry_state.reshape(pairs, SPAN, STATE), at_x * (pairs // n_x) + mine // each, 0, False
    )
    carry = lax.dynamic_slice_in_dim(carry.T, (mine % each) * size, size, 0)
    (entering,) = call(
        enter_kernel,
        [jax.ShapeDtypeStruct((groups, size, SPAN), F32)],
        flops=10**6,
        vmem=2,
        args=(parts, carry),
    )
    entering = lax.all_to_all(entering, GROUPS, 0, 0, tiled=True).reshape(1, quarter, SPAN)
    entering, left, right, far = lax.optimization_barrier((entering, left, right, far))
    entering = lax.all_to_all(jnp.broadcast_to(entering, (n_x, quarter, SPAN)), "x", 0, 0, tiled=True)

    blocks = (*own, *left, *right, *far)
    mixed = call(
        functools.partial(fold_kernel, n_x),
        [values] * n_x,
        scratch=[
            pltpu.VMEM((n_x - 1, tokens, inner), BF16),
            pltpu.VMEM((n_x, inner, SPAN), F32),
            pltpu.VMEM((n_x, heads, SPAN), F32),
            pltpu.VMEM((n_x, tokens, inner), F32),
            pltpu.VMEM((n_x, tokens, 3 * SPAN), BF16),
            pltpu.SemaphoreType.DMA((4 * n_x,)),
            pltpu.SemaphoreType.DMA((n_x,)),
        ],
        flops=2 * n_x * tokens * inner * STATE * 2,
        smem=1,
        vmem=3,
        hbm_outs=n_x,
        args=(place, bias, decay, skip, fresh, mixed, *blocks),
    )
    kept, sent = call(
        functools.partial(mix_kernel, n_x),
        [jax.ShapeDtypeStruct((n_x * tokens, weight.shape[0] // 2), F32)] * 2,
        scratch=[
            pltpu.VMEM((n_x, heads, SPAN), F32),
            pltpu.VMEM((n_x, tokens, inner), F32),
            pltpu.VMEM((n_x, tokens, packed - inner), BF16),
            pltpu.VMEM((n_x * tokens, inner), BF16),
            pltpu.VMEM(weight.shape, BF16),
            pltpu.SemaphoreType.DMA((3 * n_x + 1,)),
        ],
        flops=2 * n_x * tokens * inner * (STATE * 2 + weight.shape[0]),
        smem=1,
        vmem=4,
        args=(
            place,
            bias,
            decay,
            group_gain.reshape(1, inner),
            entering.reshape(inner, SPAN),
            *mixed,
            *blocks,
            weight,
        ),
    )
    partial = (kept + lax.ppermute(sent, "core", ring(2, 1))).astype(BF16)
    partial = lax.all_to_all(partial, ("x", *TENSOR), 0, 0, tiled=True)
    rows = residual.shape[0]
    (done,) = call(
        functools.partial(finish_kernel, n_x=n_x, n_z=n_z),
        [jax.ShapeDtypeStruct(residual.shape, BF16)],
        scratch=[pltpu.VMEM(residual.shape, F32)],
        flops=10**6,
        smem=1,
        vmem=3,
        args=(late, partial.reshape(n_x, n_t // 2, 2, rows, weight.shape[0] // 2), residual, final_gain.reshape(1, -1)),
    )
    across = lax.ppermute(done, "yl", ring(2, 1))
    mine_two = jnp.stack([done, across])
    theirs_two = lax.ppermute(mine_two, "core", ring(2, 1))
    first_y, first_core = lax.axis_index("yl") == 0, lax.axis_index("core") == 0
    even = jnp.where(first_core, mine_two, theirs_two)
    odd = jnp.where(first_core, theirs_two, mine_two)
    low = jnp.where(first_y, jnp.stack([even[0], odd[0]]), jnp.stack([even[1], odd[1]]))
    high = jnp.where(first_y, jnp.stack([even[1], odd[1]]), jnp.stack([even[0], odd[0]]))
    return jnp.concatenate([low, high]).reshape(tokens, residual.shape[1])


def solution(mesh):
    fine = Mesh(mesh.devices.reshape(2, 8, 4, 2, 2), (*CONTEXT, *TENSOR))
    return jax.shard_map(
        on_device,
        mesh=fine,
        in_specs=(
            P(CONTEXT, TENSOR),
            P(CONTEXT, TENSOR),
            P(CONTEXT, TENSOR),
            P(CONTEXT, TENSOR),
            P(CONTEXT, TENSOR),
            P(TENSOR),
            P(TENSOR),
            P(TENSOR),
            P(TENSOR),
            P(TENSOR, None, None),
            P(TENSOR, CONTEXT),
            P((*CONTEXT, *TENSOR), None),
            P(),
        ),
        out_specs=P(CONTEXT, None),
        check_vma=False,
    )
```

```python
import functools

import jax
import jax.numpy as jnp
from jax import lax
from jax.experimental import pallas as pl
from jax.experimental.pallas import tpu as pltpu
from jax.sharding import Mesh, PartitionSpec as P

EPSILON = 1e-05
HIGHEST = lax.Precision.HIGHEST
SPAN = 128
STATE = 128
HEAD_DIM = 64
EXTRA = 8
BF16, F32 = jnp.bfloat16, jnp.float32
CONTEXT = ("yh", "z", "x")
TENSOR = ("yl", "core")
GROUPS = ("yh", "z")
VMEM_LIMIT = 14 * 2**20
VMEM_MOST = 61 * 2**20


def call(kernel, outs, *, scratch=(), flops=0, smem=0, vmem=0, hbm_outs=0, limit=VMEM_MOST, args=()):
    specs = [pl.BlockSpec(memory_space=pltpu.SMEM)] * smem
    specs += [pl.BlockSpec(memory_space=pltpu.VMEM)] * vmem
    specs += [pl.BlockSpec(memory_space=pltpu.HBM)] * (len(args) - smem - vmem)
    places = [pltpu.VMEM] * (len(outs) - hbm_outs) + [pltpu.HBM] * hbm_outs
    moved = sum(a.size * a.dtype.itemsize for a in (*args, *outs))
    return pl.pallas_call(
        kernel,
        out_shape=list(outs),
        in_specs=specs,
        out_specs=[pl.BlockSpec(memory_space=m) for m in places],
        scratch_shapes=scratch,
        compiler_params=pltpu.CompilerParams(
            vmem_limit_bytes=limit if len(args) > smem + vmem else VMEM_LIMIT
        ),
        cost_estimate=pl.CostEstimate(flops=flops, bytes_accessed=moved, transcendentals=0),
    )(*args)


def copies(pairs, semaphores, first=0):
    started = [pltpu.make_async_copy(a, b, semaphores.at[first + i]) for i, (a, b) in enumerate(pairs)]
    for copy in started:
        copy.start()
    return started


def dot(a, b, precision=None):
    return lax.dot_general(
        a, b, (((1,), (0,)), ((), ())), precision=precision, preferred_element_type=F32
    )


def as_column(row):
    square = (row.shape[1], row.shape[1])
    same = lax.broadcasted_iota(jnp.int32, square, 0) == lax.broadcasted_iota(jnp.int32, square, 1)
    return jnp.sum(jnp.where(same, jnp.broadcast_to(row, square), 0.0), axis=1, keepdims=True)


def steps_of(raw_t, bias, decay_log):
    v = raw_t.astype(F32) + as_column(bias)
    step = jnp.maximum(v, 0.0) + jnp.log1p(jnp.exp(-jnp.abs(v)))
    rows = lax.broadcasted_iota(jnp.int32, (SPAN, SPAN), 0)
    columns = lax.broadcasted_iota(jnp.int32, (SPAN, SPAN), 1)
    upper = jnp.where(rows <= columns, 1.0, 0.0).astype(F32)
    return step, dot(-jnp.exp(as_column(decay_log)) * step, upper, HIGHEST)


def split(a):
    high = a.astype(BF16)
    return high, (a - high.astype(F32)).astype(BF16)


def first_lanes(shape):
    return lax.broadcasted_iota(jnp.int32, shape, len(shape) - 1) < HEAD_DIM


def column(a, h):
    return jnp.broadcast_to(a[:, h : h + 1], (a.shape[0], 2 * HEAD_DIM))


def pair_row(a, pair):
    low = first_lanes((1, 2 * HEAD_DIM))
    return jnp.where(low, column(a[2 * pair : 2 * pair + 1], 0), column(a[2 * pair + 1 : 2 * pair + 2], 0))


def fresh_states(x_ref, b, step_t, cumulative_t, x_in=()):
    last = cumulative_t[:, SPAN - 1 : SPAN]
    weight = jnp.transpose(step_t * jnp.exp(last - cumulative_t))
    b_t = jnp.transpose(b)
    b_twice = jnp.concatenate([b_t, b_t], axis=1)
    low = first_lanes((SPAN, SPAN))
    pairs = x_ref.shape[1] // SPAN
    for pair in range(pairs):
        if x_in and pair % (pairs // len(x_in)) == 0:
            for copy in x_in[pair // (pairs // len(x_in))]:
                copy.wait()
        lanes = slice(pair * SPAN, (pair + 1) * SPAN)
        scale = jnp.where(low, column(weight, 2 * pair), column(weight, 2 * pair + 1))
        scaled = x_ref[:, lanes].astype(F32) * scale
        state = dot(b_twice, jnp.concatenate(split(scaled), axis=0))
        yield pair, state, pair_row(last, pair)


def states_kernel(x_hbm, gate_hbm, b_hbm, c_hbm, raw_hbm, bias_hbm, decay_hbm, out_ref, top_hbm, bottom_hbm, *scratch):
    packed_ref, bias_ref, decay_ref, semaphores = scratch
    inner, heads = x_hbm.shape[1], raw_hbm.shape[0]
    at = 2 * inner
    x_ref = packed_ref.at[:, :inner]
    gets = copies(
        [
            (raw_hbm, packed_ref.at[:heads, at + 2 * SPAN :]),
            (bias_hbm, bias_ref),
            (decay_hbm, decay_ref),
            (b_hbm, packed_ref.at[:, at : at + SPAN]),
            (x_hbm, x_ref),
            (c_hbm, packed_ref.at[:, at + SPAN : at + 2 * SPAN]),
            (gate_hbm, packed_ref.at[:, inner:at]),
        ],
        semaphores,
    )
    packed_ref[heads:, at + 2 * SPAN :] = jnp.zeros((SPAN - heads, SPAN), BF16)
    for copy in gets[:3]:
        copy.wait()
    step, cumulative = steps_of(packed_ref[:heads, at + 2 * SPAN :], bias_ref[...], decay_ref[...])
    for copy in gets[3:]:
        copy.wait()
    half = SPAN // 2
    puts = copies([(packed_ref.at[:half], top_hbm), (packed_ref.at[half:], bottom_hbm)], semaphores, len(gets))
    each = out_ref.shape[1] // SPAN
    for pair, state, log in fresh_states(x_ref, packed_ref[:, at : at + SPAN], step, cumulative):
        member, place = divmod(pair, each)
        out_ref[member, place * STATE : (place + 1) * STATE, :] = state
        out_ref[member, each * STATE + place : each * STATE + place + 1, :] = log
    for put in puts:
        put.wait()


def group_kernel(parts_ref, out_ref):
    members, rows, _ = parts_ref.shape
    pairs = rows // STATE
    slices, size = out_ref.shape[0], out_ref.shape[1] - EXTRA
    for pair in range(pairs):
        here = slice(pair * STATE, (pair + 1) * STATE)
        at = pairs * STATE + pair
        log = parts_ref[0, at : at + 1, :]
        state = parts_ref[0, here, :]
        for member in range(1, members):
            more = parts_ref[member, at : at + 1, :]
            state = jnp.exp(more) * state + parts_ref[member, here, :]
            log = log + more
        for i in range(STATE // size):
            out_ref[pair * (STATE // size) + i, :size, :] = state[i * size : (i + 1) * size]
            out_ref[pair * (STATE // size) + i, size:, :] = jnp.broadcast_to(log, (EXTRA, SPAN))


def enter_kernel(parts_ref, carry_ref, out_ref):
    size = out_ref.shape[1]
    run = carry_ref[...]
    for k in range(parts_ref.shape[0]):
        out_ref[k] = run
        run = jnp.exp(parts_ref[k, size : size + 1, :]) * run + parts_ref[k, :size, :]


def halves(pieces, columns, ref):
    half = SPAN // 2
    return [(pieces[0].at[:, columns], ref.at[:half]), (pieces[1].at[:, columns], ref.at[half:])]


def local_block(x_ref, coefs_ref, bias_ref, decay_ref, skip_ref, mixed_ref, state_ref, x_in=(), after=None):
    heads = bias_ref.shape[1]
    b, c = coefs_ref[:, :SPAN], coefs_ref[:, SPAN : 2 * SPAN]
    step_t, cumulative_t = steps_of(coefs_ref[:heads, 2 * SPAN :], bias_ref[...], decay_ref[...])
    cumulative = jnp.transpose(cumulative_t)
    scores = lax.dot_general(c, b, (((1,), (1,)), ((), ())), preferred_element_type=F32)
    rows = lax.broadcasted_iota(jnp.int32, (SPAN, SPAN), 0)
    columns = lax.broadcasted_iota(jnp.int32, (SPAN, SPAN), 1)
    causal = rows >= columns
    low = first_lanes((SPAN, SPAN))
    for pair, state, _ in fresh_states(x_ref, b, step_t, cumulative_t, x_in):
        lanes = slice(pair * SPAN, (pair + 1) * SPAN)
        state_ref[lanes, :] = state
        x = x_ref[:, lanes]
        weights = []
        for h in (2 * pair, 2 * pair + 1):
            gap = column(cumulative, h) - cumulative_t[h : h + 1, :]
            within = jnp.exp(jnp.where(causal, gap, -jnp.inf))
            weights.append(jnp.concatenate(split(scores * within * step_t[h : h + 1, :]), axis=1))
        both = dot(jnp.concatenate(weights, axis=0), jnp.concatenate([x, x], axis=0))
        mixed_ref[:, lanes] = jnp.where(low, both[:SPAN], both[SPAN:]) + skip_ref[:, lanes] * x.astype(F32)
        if after is not None:
            after(pair)
    return cumulative_t


def local_kernel(bias_ref, decay_ref, skip_ref, top_hbm, bottom_hbm, mixed_hbm, state_hbm, *scratch):
    x_ref, coefs_ref, mixed_ref, state_ref, gets, puts = scratch
    inner = x_ref.shape[1]
    step = inner // 4
    each = step // SPAN
    pieces = (top_hbm, bottom_hbm)
    coefs_in = copies(halves(pieces, slice(2 * inner, None), coefs_ref), gets)
    x_in = [
        copies(halves(pieces, pl.ds(i * step, step), x_ref.at[:, pl.ds(i * step, step)]), gets, 2 + 2 * i)
        for i in range(4)
    ]
    for copy in coefs_in:
        copy.wait()
    out = []

    def after(pair):
        if pair % each == each - 1:
            part = pl.ds(pair // each * step, step)
            moves = [(state_ref.at[part], state_hbm.at[part]), (mixed_ref.at[:, part], mixed_hbm.at[:, part])]
            out.extend(copies(moves, puts, len(out)))

    local_block(x_ref, coefs_ref, bias_ref, decay_ref, skip_ref, mixed_ref, state_ref, x_in, after)
    for copy in out:
        copy.wait()


def fold_kernel(n, place_ref, bias_ref, decay_ref, skip_ref, *refs):
    last = n - 1
    states, given, refs = refs[:last], refs[last : 2 * last], refs[2 * last :]
    blocks, out = refs[: 2 * n], refs[2 * n : 3 * n]
    x_ref, enter_ref, logs_ref, mixed_ref, coefs_ref, gets, puts = refs[3 * n :]
    inner, heads = mixed_ref.shape[2], bias_ref.shape[1]
    pairs = inner // SPAN
    coefs_in = [
        copies(halves(blocks[2 * i : 2 * i + 2], slice(2 * inner, None), coefs_ref.at[i]), gets, 2 * i)
        for i in reversed(range(n))
    ][::-1]
    x_in = copies(halves(blocks[2 * last :], slice(0, inner), x_ref), gets, 2 * n)
    state_in = copies([(states[i], enter_ref.at[place_ref[i]]) for i in range(last)], gets, 2 * n + 2)
    mixed_in = copies([(given[i], mixed_ref.at[i]) for i in range(last)], gets, 3 * n + 2)
    for i in reversed(range(n)):
        for copy in coefs_in[i]:
            copy.wait()
        place = place_ref[i]
        if i == last:
            state_ref = enter_ref.at[place]
            logs_ref[place] = local_block(
                x_ref, coefs_ref.at[i], bias_ref, decay_ref, skip_ref, mixed_ref.at[i], state_ref, [x_in]
            )
        else:
            logs_ref[place] = steps_of(coefs_ref[i, :heads, 2 * SPAN :], bias_ref[...], decay_ref[...])[1]
    for copy in state_in:
        copy.wait()
    for pair in range(pairs):
        lanes = slice(pair * SPAN, (pair + 1) * SPAN)
        run = jnp.zeros((SPAN, SPAN), F32)
        for p in range(n):
            fresh = enter_ref[p, lanes, :]
            enter_ref[p, lanes, :] = run
            run = jnp.exp(pair_row(logs_ref[p, :, SPAN - 1 :], pair)) * run + fresh
    low = first_lanes((SPAN, SPAN))
    out_copies = []
    for i in range(n):
        if i < last:
            mixed_in[i].wait()
        place = place_ref[i]
        cumulative = jnp.transpose(logs_ref[place])
        c = coefs_ref[i, :, SPAN : 2 * SPAN]
        c_twice = jnp.concatenate([c, c], axis=1)
        for pair in range(pairs):
            lanes = slice(pair * SPAN, (pair + 1) * SPAN)
            at = jnp.where(low, column(cumulative, 2 * pair), column(cumulative, 2 * pair + 1))
            carried = dot(c_twice, jnp.concatenate(split(enter_ref[place, lanes, :]), axis=0))
            mixed_ref[i, :, lanes] += carried * jnp.exp(at)
        out_copies += copies([(mixed_ref.at[i], out[i])], puts, i)
    for copy in out_copies:
        copy.wait()


def mix_kernel(n, place_ref, bias_ref, decay_ref, gain_ref, enter_ref, *refs):
    mixed, blocks, weight_hbm = refs[:n], refs[n : 3 * n], refs[3 * n]
    kept_ref, sent_ref, logs_ref, mixed_ref, block_ref, normed_ref, weight_ref, semaphores = refs[3 * n + 1 :]
    inner, heads = mixed_ref.shape[2], bias_ref.shape[1]
    pairs = inner // SPAN
    block_in, mixed_in = [], []
    for i in range(n):
        block_in += copies(
            halves(blocks[2 * i : 2 * i + 2], slice(inner, None), block_ref.at[i]), semaphores, 2 * i
        )
        mixed_in += copies([(mixed[i], mixed_ref.at[i])], semaphores, 2 * n + i)
    (weight_in,) = copies([(weight_hbm, weight_ref)], semaphores, 3 * n)
    for i in range(n):
        for copy in block_in[2 * i : 2 * i + 2]:
            copy.wait()
        raw_t = block_ref[i, :heads, inner + 2 * SPAN :]
        logs_ref[place_ref[i]] = steps_of(raw_t, bias_ref[...], decay_ref[...])[1]
    before = jnp.zeros((heads, 1), F32)
    for p in range(n):
        here = logs_ref[p]
        logs_ref[p] = here + before
        before = before + here[:, SPAN - 1 :]
    low = first_lanes((SPAN, SPAN))
    for i in range(n):
        mixed_in[i].wait()
        place = place_ref[i]
        cumulative = jnp.transpose(logs_ref[place])
        c = block_ref[i, :, inner + SPAN : inner + 2 * SPAN]
        c_twice = jnp.concatenate([c, c], axis=1)
        squares = jnp.zeros((SPAN, SPAN), F32)
        for pair in range(pairs):
            lanes = slice(pair * SPAN, (pair + 1) * SPAN)
            at = jnp.where(low, column(cumulative, 2 * pair), column(cumulative, 2 * pair + 1))
            carried = dot(c_twice, jnp.concatenate(split(enter_ref[lanes, :]), axis=0))
            mixer_out = mixed_ref[i, :, lanes] + carried * jnp.exp(at)
            gate = block_ref[i, :, lanes].astype(F32)
            gated = mixer_out * (gate / (1.0 + jnp.exp(-gate)))
            mixed_ref[i, :, lanes] = gated
            squares += gated * gated
        root = lax.rsqrt(jnp.sum(squares, axis=-1, keepdims=True) / inner + EPSILON)
        to = pl.ds(pl.multiple_of(place * SPAN, SPAN), SPAN)
        for pair in range(pairs):
            lanes = slice(pair * SPAN, (pair + 1) * SPAN)
            normed_ref[to, lanes] = (mixed_ref[i, :, lanes] * root * gain_ref[:, lanes]).astype(BF16)
    weight_in.wait()
    core, width = place_ref[n], kept_ref.shape[1]
    for ref, side in ((sent_ref, 1 - core), (kept_ref, core)):
        for tile in range(width // (2 * SPAN)):
            columns = slice(2 * tile * SPAN, 2 * (tile + 1) * SPAN)
            rows = pl.ds(pl.multiple_of(side * width + 2 * tile * SPAN, 2 * SPAN), 2 * SPAN)
            ref[:, columns] = lax.dot_general(
                normed_ref[...], weight_ref[rows, :], (((1,), (1,)), ((), ())), preferred_element_type=F32
            )


def finish_kernel(late_ref, parts_ref, residual_ref, gain_ref, out_ref, combined_ref, *, n_x, n_z):
    late = late_ref[0] > 0
    tokens = residual_ref.shape[0]
    sums = []
    for x in range(n_x):
        cores = []
        for core in range(parts_ref.shape[2]):
            total = parts_ref[x, 0, core].astype(F32)
            for y in range(1, parts_ref.shape[1]):
                total += parts_ref[x, y, core].astype(F32)
            cores.append(total)
        sums.append(jnp.concatenate(cores, axis=1))
    squares = jnp.zeros((tokens, 2 * HEAD_DIM), F32)
    for z in range(n_z):
        piece = slice(z * 2 * HEAD_DIM, (z + 1) * 2 * HEAD_DIM)
        own = [total[:, piece] for total in sums]
        swapped = [jnp.concatenate([a[:, HEAD_DIM:], a[:, :HEAD_DIM]], axis=1) for a in own]
        ordered = [jnp.where(late, b, a) for a, b in zip(own, swapped)]
        for yh in range(2):
            for x in range(0, n_x, 2):
                block = ((yh * n_z + z) * n_x + x) // 2
                lanes = slice(block * 2 * HEAD_DIM, (block + 1) * 2 * HEAD_DIM)
                half = slice(yh * HEAD_DIM, (yh + 1) * HEAD_DIM)
                both = jnp.concatenate([ordered[x][:, half], ordered[x + 1][:, half]], axis=1)
                combined = residual_ref[:, lanes].astype(F32) + both
                combined_ref[:, lanes] = combined
                squares += combined * combined
    root = lax.rsqrt(jnp.sum(squares, axis=-1, keepdims=True) / combined_ref.shape[1] + EPSILON)
    out_ref[...] = (combined_ref[...] * root * gain_ref[...]).astype(BF16)


def ring(n, by):
    return [(i, (i + by) % n) for i in range(n)]


def on_device(
    mixer_values,
    gate_values,
    input_coefs,
    output_coefs,
    step_raw,
    step_bias,
    decay_log,
    skip_gain,
    group_gain,
    carry_state,
    out_weight,
    residual,
    final_gain,
):
    tokens, inner = mixer_values.shape
    heads = step_raw.shape[1]
    n_z, n_x = lax.axis_size("z"), lax.axis_size("x")
    n_t = lax.axis_size("yl") * lax.axis_size("core")
    groups = 2 * n_z
    at_x = lax.axis_index("x")
    late = lax.axis_index("yh").astype(jnp.int32).reshape(1)
    bias, decay = step_bias.reshape(1, heads), decay_log.reshape(1, heads)
    skip = jnp.repeat(skip_gain, HEAD_DIM).reshape(1, inner)
    pairs = heads // 2
    quarter = inner // n_x
    size = quarter // groups
    packed = 2 * inner + 3 * SPAN

    half_block = jax.ShapeDtypeStruct((tokens // 2, packed), BF16)
    values = jax.ShapeDtypeStruct((tokens, inner), F32)

    weight = out_weight.T
    across = lax.ppermute(weight, "yh", ring(2, 1))

    states, top, bottom = call(
        states_kernel,
        [jax.ShapeDtypeStruct((n_x, quarter + EXTRA, SPAN), F32), half_block, half_block],
        scratch=[
            pltpu.VMEM((tokens, packed), BF16),
            pltpu.VMEM((1, heads), F32),
            pltpu.VMEM((1, heads), F32),
            pltpu.SemaphoreType.DMA((9,)),
        ],
        flops=2 * tokens * inner * STATE * 2,
        hbm_outs=2,
        args=(mixer_values, gate_values, input_coefs, output_coefs, step_raw.T, bias, decay),
    )
    parts = lax.all_to_all(states, "x", 0, 0, tiled=True)
    across, parts = lax.optimization_barrier((across, parts))
    weight = jnp.concatenate([weight, across], axis=0)
    weight = lax.all_gather(weight, "z", axis=0, tiled=True)

    parts, top, bottom = lax.optimization_barrier((parts, top, bottom))
    own = (top, bottom)
    left_top = lax.ppermute(top, "x", ring(n_x, 1))
    right_bottom = lax.ppermute(bottom, "x", ring(n_x, -1))
    place = (at_x + jnp.array([0, n_x - 1, 1, 2], jnp.int32)) % n_x
    place = jnp.concatenate([place, lax.axis_index("core").astype(jnp.int32).reshape(1)])

    def local(block):
        return call(
            local_kernel,
            [values, jax.ShapeDtypeStruct((inner, SPAN), F32)],
            scratch=[
                pltpu.VMEM((tokens, inner), BF16),
                pltpu.VMEM((tokens, 3 * SPAN), BF16),
                pltpu.VMEM((tokens, inner), F32),
                pltpu.VMEM((inner, SPAN), F32),
                pltpu.SemaphoreType.DMA((10,)),
                pltpu.SemaphoreType.DMA((8,)),
            ],
            flops=10**6,
            vmem=3,
            hbm_outs=2,
            args=(bias, decay, skip, *block),
        )

    (grouped,) = call(
        group_kernel,
        [jax.ShapeDtypeStruct((groups, size + EXTRA, SPAN), F32)],
        flops=10**6,
        vmem=1,
        args=(parts,),
    )
    parts = lax.all_to_all(grouped, GROUPS, 0, 0, tiled=True)
    own_local, top_later, bottom_later = lax.optimization_barrier((local(own), top, bottom))
    left_bottom = lax.ppermute(bottom_later, "x", ring(n_x, 1))
    right_top = lax.ppermute(top_later, "x", ring(n_x, -1))
    own_local, parts, left_top, right_bottom, place = lax.optimization_barrier(
        (own_local, parts, left_top, right_bottom, place)
    )
    left, right = (left_top, left_bottom), (right_top, right_bottom)
    mine = lax.axis_index(GROUPS)
    each = STATE // size
    carry = lax.dynamic_index_in_dim(
        carry_state.reshape(pairs, SPAN, STATE), at_x * (pairs // n_x) + mine // each, 0, False
    )
    carry = lax.dynamic_slice_in_dim(carry.T, (mine % each) * size, size, 0)
    (entering,) = call(
        enter_kernel,
        [jax.ShapeDtypeStruct((groups, size, SPAN), F32)],
        flops=10**6,
        vmem=2,
        args=(parts, carry),
    )
    entering, onward, back = lax.optimization_barrier((entering, left_top, right_bottom))
    far = (lax.ppermute(onward, "x", ring(n_x, 1)), lax.ppermute(back, "x", ring(n_x, -1)))
    entering = lax.all_to_all(entering, GROUPS, 0, 0, tiled=True).reshape(1, quarter, SPAN)
    entering, left_local, right_local, far = lax.optimization_barrier((entering, local(left), local(right), far))
    mixed, fresh = zip(own_local, left_local, right_local)
    entering = lax.all_to_all(jnp.broadcast_to(entering, (n_x, quarter, SPAN)), "x", 0, 0, tiled=True)

    blocks = (*own, *left, *right, *far)
    mixed = call(
        functools.partial(fold_kernel, n_x),
        [values] * n_x,
        scratch=[
            pltpu.VMEM((tokens, inner), BF16),
            pltpu.VMEM((n_x, inner, SPAN), F32),
            pltpu.VMEM((n_x, heads, SPAN), F32),
            pltpu.VMEM((n_x, tokens, inner), F32),
            pltpu.VMEM((n_x, tokens, 3 * SPAN), BF16),
            pltpu.SemaphoreType.DMA((4 * n_x + 2,)),
            pltpu.SemaphoreType.DMA((n_x,)),
        ],
        flops=2 * n_x * tokens * inner * STATE * 2,
        smem=1,
        vmem=3,
        hbm_outs=n_x,
        args=(place, bias, decay, skip, *fresh, *mixed, *blocks),
    )
    kept, sent = call(
        functools.partial(mix_kernel, n_x),
        [jax.ShapeDtypeStruct((n_x * tokens, weight.shape[0] // 2), F32)] * 2,
        scratch=[
            pltpu.VMEM((n_x, heads, SPAN), F32),
            pltpu.VMEM((n_x, tokens, inner), F32),
            pltpu.VMEM((n_x, tokens, packed - inner), BF16),
            pltpu.VMEM((n_x * tokens, inner), BF16),
            pltpu.VMEM(weight.shape, BF16),
            pltpu.SemaphoreType.DMA((3 * n_x + 1,)),
        ],
        flops=2 * n_x * tokens * inner * (STATE * 2 + weight.shape[0]),
        smem=1,
        vmem=4,
        limit=52 * 2**20,
        args=(
            place,
            bias,
            decay,
            group_gain.reshape(1, inner),
            entering.reshape(inner, SPAN),
            *mixed,
            *blocks,
            weight,
        ),
    )
    partial = (kept + lax.ppermute(sent, "core", ring(2, 1))).astype(BF16)
    partial = lax.all_to_all(partial, ("x", *TENSOR), 0, 0, tiled=True)
    rows = residual.shape[0]
    (done,) = call(
        functools.partial(finish_kernel, n_x=n_x, n_z=n_z),
        [jax.ShapeDtypeStruct(residual.shape, BF16)],
        scratch=[pltpu.VMEM(residual.shape, F32)],
        flops=10**6,
        smem=1,
        vmem=3,
        args=(late, partial.reshape(n_x, n_t // 2, 2, rows, weight.shape[0] // 2), residual, final_gain.reshape(1, -1)),
    )
    across = lax.ppermute(done, "yl", ring(2, 1))
    mine_two = jnp.stack([done, across])
    theirs_two = lax.ppermute(mine_two, "core", ring(2, 1))
    first_y, first_core = lax.axis_index("yl") == 0, lax.axis_index("core") == 0
    even = jnp.where(first_core, mine_two, theirs_two)
    odd = jnp.where(first_core, theirs_two, mine_two)
    low = jnp.where(first_y, jnp.stack([even[0], odd[0]]), jnp.stack([even[1], odd[1]]))
    high = jnp.where(first_y, jnp.stack([even[1], odd[1]]), jnp.stack([even[0], odd[0]]))
    return jnp.concatenate([low, high]).reshape(tokens, residual.shape[1])


def solution(mesh):
    fine = Mesh(mesh.devices.reshape(2, 8, 4, 2, 2), (*CONTEXT, *TENSOR))
    return jax.shard_map(
        on_device,
        mesh=fine,
        in_specs=(
            P(CONTEXT, TENSOR),
            P(CONTEXT, TENSOR),
            P(CONTEXT, TENSOR),
            P(CONTEXT, TENSOR),
            P(CONTEXT, TENSOR),
            P(TENSOR),
            P(TENSOR),
            P(TENSOR),
            P(TENSOR),
            P(TENSOR, None, None),
            P(TENSOR, CONTEXT),
            P((*CONTEXT, *TENSOR), None),
            P(),
        ),
        out_specs=P(CONTEXT, None),
        check_vma=False,
    )
```

```python
import functools

import jax
import jax.numpy as jnp
from jax import lax
from jax.experimental import pallas as pl
from jax.experimental.pallas import tpu as pltpu
from jax.sharding import Mesh, PartitionSpec as P

EPSILON = 1e-05
HIGHEST = lax.Precision.HIGHEST
SPAN = 128
STATE = 128
HEAD_DIM = 64
EXTRA = 8
BF16, F32 = jnp.bfloat16, jnp.float32
CONTEXT = ("yh", "z", "x")
TENSOR = ("yl", "core")
GROUPS = ("yh", "z")
VMEM_LIMIT = 14 * 2**20
VMEM_MOST = 61 * 2**20


def call(kernel, outs, *, scratch=(), flops=0, smem=0, vmem=0, hbm_outs=0, limit=VMEM_MOST, args=()):
    specs = [pl.BlockSpec(memory_space=pltpu.SMEM)] * smem
    specs += [pl.BlockSpec(memory_space=pltpu.VMEM)] * vmem
    specs += [pl.BlockSpec(memory_space=pltpu.HBM)] * (len(args) - smem - vmem)
    places = [pltpu.VMEM] * (len(outs) - hbm_outs) + [pltpu.HBM] * hbm_outs
    moved = sum(a.size * a.dtype.itemsize for a in (*args, *outs))
    return pl.pallas_call(
        kernel,
        out_shape=list(outs),
        in_specs=specs,
        out_specs=[pl.BlockSpec(memory_space=m) for m in places],
        scratch_shapes=scratch,
        compiler_params=pltpu.CompilerParams(
            vmem_limit_bytes=limit if len(args) > smem + vmem else VMEM_LIMIT
        ),
        cost_estimate=pl.CostEstimate(flops=flops, bytes_accessed=moved, transcendentals=0),
    )(*args)


def copies(pairs, semaphores, first=0):
    started = [pltpu.make_async_copy(a, b, semaphores.at[first + i]) for i, (a, b) in enumerate(pairs)]
    for copy in started:
        copy.start()
    return started


def dot(a, b, precision=None):
    return lax.dot_general(
        a, b, (((1,), (0,)), ((), ())), precision=precision, preferred_element_type=F32
    )


def as_column(row):
    square = (row.shape[1], row.shape[1])
    same = lax.broadcasted_iota(jnp.int32, square, 0) == lax.broadcasted_iota(jnp.int32, square, 1)
    return jnp.sum(jnp.where(same, jnp.broadcast_to(row, square), 0.0), axis=1, keepdims=True)


def steps_of(raw_t, bias, decay_log):
    v = raw_t.astype(F32) + as_column(bias)
    step = jnp.maximum(v, 0.0) + jnp.log1p(jnp.exp(-jnp.abs(v)))
    rows = lax.broadcasted_iota(jnp.int32, (SPAN, SPAN), 0)
    columns = lax.broadcasted_iota(jnp.int32, (SPAN, SPAN), 1)
    upper = jnp.where(rows <= columns, 1.0, 0.0).astype(F32)
    return step, dot(-jnp.exp(as_column(decay_log)) * step, upper, HIGHEST)


def split(a):
    high = a.astype(BF16)
    return high, (a - high.astype(F32)).astype(BF16)


def first_lanes(shape):
    return lax.broadcasted_iota(jnp.int32, shape, len(shape) - 1) < HEAD_DIM


def column(a, h):
    return jnp.broadcast_to(a[:, h : h + 1], (a.shape[0], 2 * HEAD_DIM))


def pair_row(a, pair):
    low = first_lanes((1, 2 * HEAD_DIM))
    return jnp.where(low, column(a[2 * pair : 2 * pair + 1], 0), column(a[2 * pair + 1 : 2 * pair + 2], 0))


def fresh_states(x_ref, b, step_t, cumulative_t, x_in=()):
    last = cumulative_t[:, SPAN - 1 : SPAN]
    weight = jnp.transpose(step_t * jnp.exp(last - cumulative_t))
    b_t = jnp.transpose(b)
    b_twice = jnp.concatenate([b_t, b_t], axis=1)
    low = first_lanes((SPAN, SPAN))
    pairs = x_ref.shape[1] // SPAN
    for pair in range(pairs):
        if x_in and pair % (pairs // len(x_in)) == 0:
            for copy in x_in[pair // (pairs // len(x_in))]:
                copy.wait()
        lanes = slice(pair * SPAN, (pair + 1) * SPAN)
        scale = jnp.where(low, column(weight, 2 * pair), column(weight, 2 * pair + 1))
        scaled = x_ref[:, lanes].astype(F32) * scale
        state = dot(b_twice, jnp.concatenate(split(scaled), axis=0))
        yield pair, state, pair_row(last, pair)


def states_kernel(x_hbm, gate_hbm, b_hbm, c_hbm, raw_hbm, bias_hbm, decay_hbm, out_ref, top_hbm, bottom_hbm, *scratch):
    packed_ref, bias_ref, decay_ref, semaphores = scratch
    inner, heads = x_hbm.shape[1], raw_hbm.shape[0]
    at = 2 * inner
    x_ref = packed_ref.at[:, :inner]
    gets = copies(
        [
            (raw_hbm, packed_ref.at[:heads, at + 2 * SPAN :]),
            (bias_hbm, bias_ref),
            (decay_hbm, decay_ref),
            (b_hbm, packed_ref.at[:, at : at + SPAN]),
            (x_hbm, x_ref),
            (c_hbm, packed_ref.at[:, at + SPAN : at + 2 * SPAN]),
            (gate_hbm, packed_ref.at[:, inner:at]),
        ],
        semaphores,
    )
    packed_ref[heads:, at + 2 * SPAN :] = jnp.zeros((SPAN - heads, SPAN), BF16)
    for copy in gets[:3]:
        copy.wait()
    step, cumulative = steps_of(packed_ref[:heads, at + 2 * SPAN :], bias_ref[...], decay_ref[...])
    for copy in gets[3:]:
        copy.wait()
    half = SPAN // 2
    puts = copies([(packed_ref.at[:half], top_hbm), (packed_ref.at[half:], bottom_hbm)], semaphores, len(gets))
    each = out_ref.shape[1] // SPAN
    for pair, state, log in fresh_states(x_ref, packed_ref[:, at : at + SPAN], step, cumulative):
        member, place = divmod(pair, each)
        out_ref[member, place * STATE : (place + 1) * STATE, :] = state
        out_ref[member, each * STATE + place : each * STATE + place + 1, :] = log
    for put in puts:
        put.wait()


def group_kernel(parts_ref, out_ref):
    members, rows, _ = parts_ref.shape
    pairs = rows // STATE
    slices, size = out_ref.shape[0], out_ref.shape[1] - EXTRA
    for pair in range(pairs):
        here = slice(pair * STATE, (pair + 1) * STATE)
        at = pairs * STATE + pair
        log = parts_ref[0, at : at + 1, :]
        state = parts_ref[0, here, :]
        for member in range(1, members):
            more = parts_ref[member, at : at + 1, :]
            state = jnp.exp(more) * state + parts_ref[member, here, :]
            log = log + more
        for i in range(STATE // size):
            out_ref[pair * (STATE // size) + i, :size, :] = state[i * size : (i + 1) * size]
            out_ref[pair * (STATE // size) + i, size:, :] = jnp.broadcast_to(log, (EXTRA, SPAN))


def enter_kernel(parts_ref, carry_ref, out_ref):
    size = out_ref.shape[1]
    run = carry_ref[...]
    for k in range(parts_ref.shape[0]):
        out_ref[k] = run
        run = jnp.exp(parts_ref[k, size : size + 1, :]) * run + parts_ref[k, :size, :]


def halves(pieces, columns, ref):
    half = SPAN // 2
    return [(pieces[0].at[:, columns], ref.at[:half]), (pieces[1].at[:, columns], ref.at[half:])]


def local_block(x_ref, coefs_ref, bias_ref, decay_ref, skip_ref, mixed_ref, state_ref, x_in=(), after=None):
    heads = bias_ref.shape[1]
    b, c = coefs_ref[:, :SPAN], coefs_ref[:, SPAN : 2 * SPAN]
    step_t, cumulative_t = steps_of(coefs_ref[:heads, 2 * SPAN :], bias_ref[...], decay_ref[...])
    cumulative = jnp.transpose(cumulative_t)
    scores = lax.dot_general(c, b, (((1,), (1,)), ((), ())), preferred_element_type=F32)
    rows = lax.broadcasted_iota(jnp.int32, (SPAN, SPAN), 0)
    columns = lax.broadcasted_iota(jnp.int32, (SPAN, SPAN), 1)
    causal = rows >= columns
    low = first_lanes((SPAN, SPAN))
    for pair, state, _ in fresh_states(x_ref, b, step_t, cumulative_t, x_in):
        lanes = slice(pair * SPAN, (pair + 1) * SPAN)
        state_ref[lanes, :] = state
        x = x_ref[:, lanes]
        weights = []
        for h in (2 * pair, 2 * pair + 1):
            gap = column(cumulative, h) - cumulative_t[h : h + 1, :]
            within = jnp.exp(jnp.where(causal, gap, -jnp.inf))
            weights.append(jnp.concatenate(split(scores * within * step_t[h : h + 1, :]), axis=1))
        both = dot(jnp.concatenate(weights, axis=0), jnp.concatenate([x, x], axis=0))
        mixed_ref[:, lanes] = jnp.where(low, both[:SPAN], both[SPAN:]) + skip_ref[:, lanes] * x.astype(F32)
        if after is not None:
            after(pair)
    return cumulative_t


def local_kernel(bias_ref, decay_ref, skip_ref, top_hbm, bottom_hbm, mixed_hbm, state_hbm, *scratch):
    x_ref, coefs_ref, mixed_ref, state_ref, gets, puts = scratch
    inner = x_ref.shape[1]
    step = inner // 4
    each = step // SPAN
    pieces = (top_hbm, bottom_hbm)
    coefs_in = copies(halves(pieces, slice(2 * inner, None), coefs_ref), gets)
    x_in = [
        copies(halves(pieces, pl.ds(i * step, step), x_ref.at[:, pl.ds(i * step, step)]), gets, 2 + 2 * i)
        for i in range(4)
    ]
    for copy in coefs_in:
        copy.wait()
    out = []

    def after(pair):
        if pair % each == each - 1:
            part = pl.ds(pair // each * step, step)
            moves = [(state_ref.at[part], state_hbm.at[part]), (mixed_ref.at[:, part], mixed_hbm.at[:, part])]
            out.extend(copies(moves, puts, len(out)))

    local_block(x_ref, coefs_ref, bias_ref, decay_ref, skip_ref, mixed_ref, state_ref, x_in, after)
    for copy in out:
        copy.wait()


def fold_kernel(n, place_ref, bias_ref, decay_ref, skip_ref, *refs):
    last = n - 1
    states, given, refs = refs[:last], refs[last : 2 * last], refs[2 * last :]
    blocks, out = refs[: 2 * n], refs[2 * n : 3 * n]
    x_ref, enter_ref, logs_ref, mixed_ref, coefs_ref, gets, puts = refs[3 * n :]
    inner, heads = mixed_ref.shape[2], bias_ref.shape[1]
    pairs = inner // SPAN
    coefs_in = [
        copies(halves(blocks[2 * i : 2 * i + 2], slice(2 * inner, None), coefs_ref.at[i]), gets, 2 * i)
        for i in reversed(range(n))
    ][::-1]
    x_in = copies(halves(blocks[2 * last :], slice(0, inner), x_ref), gets, 2 * n)
    state_in = copies([(states[i], enter_ref.at[place_ref[i]]) for i in range(last)], gets, 2 * n + 2)
    mixed_in = copies([(given[i], mixed_ref.at[i]) for i in range(last)], gets, 3 * n + 2)
    for i in reversed(range(n)):
        for copy in coefs_in[i]:
            copy.wait()
        place = place_ref[i]
        if i == last:
            state_ref = enter_ref.at[place]
            logs_ref[place] = local_block(
                x_ref, coefs_ref.at[i], bias_ref, decay_ref, skip_ref, mixed_ref.at[i], state_ref, [x_in]
            )
        else:
            logs_ref[place] = steps_of(coefs_ref[i, :heads, 2 * SPAN :], bias_ref[...], decay_ref[...])[1]
    for copy in state_in:
        copy.wait()
    for pair in range(pairs):
        lanes = slice(pair * SPAN, (pair + 1) * SPAN)
        run = jnp.zeros((SPAN, SPAN), F32)
        for p in range(n):
            fresh = enter_ref[p, lanes, :]
            enter_ref[p, lanes, :] = run
            run = jnp.exp(pair_row(logs_ref[p, :, SPAN - 1 :], pair)) * run + fresh
    low = first_lanes((SPAN, SPAN))
    out_copies = []
    for i in range(n):
        if i < last:
            mixed_in[i].wait()
        place = place_ref[i]
        cumulative = jnp.transpose(logs_ref[place])
        c = coefs_ref[i, :, SPAN : 2 * SPAN]
        c_twice = jnp.concatenate([c, c], axis=1)
        for pair in range(pairs):
            lanes = slice(pair * SPAN, (pair + 1) * SPAN)
            at = jnp.where(low, column(cumulative, 2 * pair), column(cumulative, 2 * pair + 1))
            carried = dot(c_twice, jnp.concatenate(split(enter_ref[place, lanes, :]), axis=0))
            mixed_ref[i, :, lanes] += carried * jnp.exp(at)
        out_copies += copies([(mixed_ref.at[i], out[i])], puts, i)
    for copy in out_copies:
        copy.wait()


def mix_kernel(n, place_ref, bias_ref, decay_ref, gain_ref, enter_ref, *refs):
    mixed, blocks, weight_hbm = refs[:n], refs[n : 3 * n], refs[3 * n]
    kept_ref, sent_ref, logs_ref, mixed_ref, block_ref, normed_ref, weight_ref, enter_two, semaphores = refs[3 * n + 1 :]
    inner, heads = mixed_ref.shape[2], bias_ref.shape[1]
    pairs = inner // SPAN
    block_in, mixed_in = [], []
    for i in range(n):
        block_in += copies(
            halves(blocks[2 * i : 2 * i + 2], slice(inner, None), block_ref.at[i]), semaphores, 2 * i
        )
        mixed_in += copies([(mixed[i], mixed_ref.at[i])], semaphores, 2 * n + i)
    (weight_in,) = copies([(weight_hbm, weight_ref)], semaphores, 3 * n)
    for i in range(n):
        for copy in block_in[2 * i : 2 * i + 2]:
            copy.wait()
        raw_t = block_ref[i, :heads, inner + 2 * SPAN :]
        logs_ref[place_ref[i]] = steps_of(raw_t, bias_ref[...], decay_ref[...])[1]
    for pair in range(pairs):
        parts = split(enter_ref[pair * SPAN : (pair + 1) * SPAN, :])
        enter_two[2 * pair * SPAN : 2 * (pair + 1) * SPAN, :] = jnp.concatenate(parts, axis=0)
    before = jnp.zeros((heads, 1), F32)
    for p in range(n):
        here = logs_ref[p]
        logs_ref[p] = here + before
        before = before + here[:, SPAN - 1 :]
    low = first_lanes((SPAN, SPAN))
    for i in range(n):
        mixed_in[i].wait()
        place = place_ref[i]
        cumulative = jnp.transpose(logs_ref[place])
        c = block_ref[i, :, inner + SPAN : inner + 2 * SPAN]
        c_twice = jnp.concatenate([c, c], axis=1)
        squares = jnp.zeros((SPAN, SPAN), F32)
        for pair in range(pairs):
            lanes = slice(pair * SPAN, (pair + 1) * SPAN)
            at = jnp.where(low, column(cumulative, 2 * pair), column(cumulative, 2 * pair + 1))
            carried = dot(c_twice, enter_two[2 * pair * SPAN : 2 * (pair + 1) * SPAN, :])
            mixer_out = mixed_ref[i, :, lanes] + carried * jnp.exp(at)
            gate = block_ref[i, :, lanes].astype(F32)
            gated = mixer_out * (gate / (1.0 + jnp.exp(-gate)))
            mixed_ref[i, :, lanes] = gated
            squares += gated * gated
        root = lax.rsqrt(jnp.sum(squares, axis=-1, keepdims=True) / inner + EPSILON)
        to = pl.ds(pl.multiple_of(place * SPAN, SPAN), SPAN)
        for pair in range(pairs):
            lanes = slice(pair * SPAN, (pair + 1) * SPAN)
            normed_ref[to, lanes] = (mixed_ref[i, :, lanes] * root * gain_ref[:, lanes]).astype(BF16)
    weight_in.wait()
    core, width = place_ref[n], kept_ref.shape[1]
    for ref, side in ((sent_ref, 1 - core), (kept_ref, core)):
        for tile in range(width // (2 * SPAN)):
            columns = slice(2 * tile * SPAN, 2 * (tile + 1) * SPAN)
            rows = pl.ds(pl.multiple_of(side * width + 2 * tile * SPAN, 2 * SPAN), 2 * SPAN)
            ref[:, columns] = lax.dot_general(
                normed_ref[...], weight_ref[rows, :], (((1,), (1,)), ((), ())), preferred_element_type=F32
            )


def finish_kernel(late_ref, parts_ref, residual_ref, gain_ref, out_ref, combined_ref, *, n_x, n_z):
    late = late_ref[0] > 0
    tokens = residual_ref.shape[0]
    sums = []
    for x in range(n_x):
        cores = []
        for core in range(parts_ref.shape[2]):
            total = parts_ref[x, 0, core].astype(F32)
            for y in range(1, parts_ref.shape[1]):
                total += parts_ref[x, y, core].astype(F32)
            cores.append(total)
        sums.append(jnp.concatenate(cores, axis=1))
    squares = jnp.zeros((tokens, 2 * HEAD_DIM), F32)
    for z in range(n_z):
        piece = slice(z * 2 * HEAD_DIM, (z + 1) * 2 * HEAD_DIM)
        own = [total[:, piece] for total in sums]
        swapped = [jnp.concatenate([a[:, HEAD_DIM:], a[:, :HEAD_DIM]], axis=1) for a in own]
        ordered = [jnp.where(late, b, a) for a, b in zip(own, swapped)]
        for yh in range(2):
            for x in range(0, n_x, 2):
                block = ((yh * n_z + z) * n_x + x) // 2
                lanes = slice(block * 2 * HEAD_DIM, (block + 1) * 2 * HEAD_DIM)
                half = slice(yh * HEAD_DIM, (yh + 1) * HEAD_DIM)
                both = jnp.concatenate([ordered[x][:, half], ordered[x + 1][:, half]], axis=1)
                combined = residual_ref[:, lanes].astype(F32) + both
                combined_ref[:, lanes] = combined
                squares += combined * combined
    root = lax.rsqrt(jnp.sum(squares, axis=-1, keepdims=True) / combined_ref.shape[1] + EPSILON)
    out_ref[...] = (combined_ref[...] * root * gain_ref[...]).astype(BF16)


def ring(n, by):
    return [(i, (i + by) % n) for i in range(n)]


def on_device(
    mixer_values,
    gate_values,
    input_coefs,
    output_coefs,
    step_raw,
    step_bias,
    decay_log,
    skip_gain,
    group_gain,
    carry_state,
    out_weight,
    residual,
    final_gain,
):
    tokens, inner = mixer_values.shape
    heads = step_raw.shape[1]
    n_z, n_x = lax.axis_size("z"), lax.axis_size("x")
    n_t = lax.axis_size("yl") * lax.axis_size("core")
    groups = 2 * n_z
    at_x = lax.axis_index("x")
    late = lax.axis_index("yh").astype(jnp.int32).reshape(1)
    bias, decay = step_bias.reshape(1, heads), decay_log.reshape(1, heads)
    skip = jnp.repeat(skip_gain, HEAD_DIM).reshape(1, inner)
    pairs = heads // 2
    quarter = inner // n_x
    size = quarter // groups
    packed = 2 * inner + 3 * SPAN

    half_block = jax.ShapeDtypeStruct((tokens // 2, packed), BF16)
    values = jax.ShapeDtypeStruct((tokens, inner), F32)

    weight = out_weight.T
    across = lax.ppermute(weight, "yh", ring(2, 1))

    states, top, bottom = call(
        states_kernel,
        [jax.ShapeDtypeStruct((n_x, quarter + EXTRA, SPAN), F32), half_block, half_block],
        scratch=[
            pltpu.VMEM((tokens, packed), BF16),
            pltpu.VMEM((1, heads), F32),
            pltpu.VMEM((1, heads), F32),
            pltpu.SemaphoreType.DMA((9,)),
        ],
        flops=2 * tokens * inner * STATE * 2,
        hbm_outs=2,
        args=(mixer_values, gate_values, input_coefs, output_coefs, step_raw.T, bias, decay),
    )
    parts = lax.all_to_all(states, "x", 0, 0, tiled=True)
    across, parts = lax.optimization_barrier((across, parts))
    weight = jnp.concatenate([weight, across], axis=0)
    weight = lax.all_gather(weight, "z", axis=0, tiled=True)

    parts, top, bottom = lax.optimization_barrier((parts, top, bottom))
    own = (top, bottom)
    left_top = lax.ppermute(top, "x", ring(n_x, 1))
    right_bottom = lax.ppermute(bottom, "x", ring(n_x, -1))
    place = (at_x + jnp.array([0, n_x - 1, 1, 2], jnp.int32)) % n_x
    place = jnp.concatenate([place, lax.axis_index("core").astype(jnp.int32).reshape(1)])

    def local(block):
        return call(
            local_kernel,
            [values, jax.ShapeDtypeStruct((inner, SPAN), F32)],
            scratch=[
                pltpu.VMEM((tokens, inner), BF16),
                pltpu.VMEM((tokens, 3 * SPAN), BF16),
                pltpu.VMEM((tokens, inner), F32),
                pltpu.VMEM((inner, SPAN), F32),
                pltpu.SemaphoreType.DMA((10,)),
                pltpu.SemaphoreType.DMA((8,)),
            ],
            flops=10**6,
            vmem=3,
            hbm_outs=2,
            args=(bias, decay, skip, *block),
        )

    (grouped,) = call(
        group_kernel,
        [jax.ShapeDtypeStruct((groups, size + EXTRA, SPAN), F32)],
        flops=10**6,
        vmem=1,
        args=(parts,),
    )
    parts = lax.all_to_all(grouped, GROUPS, 0, 0, tiled=True)
    own_local, top_later, bottom_later = lax.optimization_barrier((local(own), top, bottom))
    left_bottom = lax.ppermute(bottom_later, "x", ring(n_x, 1))
    right_top = lax.ppermute(top_later, "x", ring(n_x, -1))
    own_local, parts, left_top, right_bottom, place = lax.optimization_barrier(
        (own_local, parts, left_top, right_bottom, place)
    )
    left, right = (left_top, left_bottom), (right_top, right_bottom)
    mine = lax.axis_index(GROUPS)
    each = STATE // size
    carry = lax.dynamic_index_in_dim(
        carry_state.reshape(pairs, SPAN, STATE), at_x * (pairs // n_x) + mine // each, 0, False
    )
    carry = lax.dynamic_slice_in_dim(carry.T, (mine % each) * size, size, 0)
    (entering,) = call(
        enter_kernel,
        [jax.ShapeDtypeStruct((groups, size, SPAN), F32)],
        flops=10**6,
        vmem=2,
        args=(parts, carry),
    )
    entering, onward, back = lax.optimization_barrier((entering, left_top, right_bottom))
    far = (lax.ppermute(onward, "x", ring(n_x, 1)), lax.ppermute(back, "x", ring(n_x, -1)))
    entering = lax.all_to_all(entering, GROUPS, 0, 0, tiled=True).reshape(1, quarter, SPAN)
    entering, left_local, right_local, far = lax.optimization_barrier((entering, local(left), local(right), far))
    mixed, fresh = zip(own_local, left_local, right_local)
    entering = lax.all_to_all(jnp.broadcast_to(entering, (n_x, quarter, SPAN)), "x", 0, 0, tiled=True)

    blocks = (*own, *left, *right, *far)
    mixed = call(
        functools.partial(fold_kernel, n_x),
        [values] * n_x,
        scratch=[
            pltpu.VMEM((tokens, inner), BF16),
            pltpu.VMEM((n_x, inner, SPAN), F32),
            pltpu.VMEM((n_x, heads, SPAN), F32),
            pltpu.VMEM((n_x, tokens, inner), F32),
            pltpu.VMEM((n_x, tokens, 3 * SPAN), BF16),
            pltpu.SemaphoreType.DMA((4 * n_x + 2,)),
            pltpu.SemaphoreType.DMA((n_x,)),
        ],
        flops=2 * n_x * tokens * inner * STATE * 2,
        smem=1,
        vmem=3,
        hbm_outs=n_x,
        args=(place, bias, decay, skip, *fresh, *mixed, *blocks),
    )
    kept, sent = call(
        functools.partial(mix_kernel, n_x),
        [jax.ShapeDtypeStruct((n_x * tokens, weight.shape[0] // 2), F32)] * 2,
        scratch=[
            pltpu.VMEM((n_x, heads, SPAN), F32),
            pltpu.VMEM((n_x, tokens, inner), F32),
            pltpu.VMEM((n_x, tokens, packed - inner), BF16),
            pltpu.VMEM((n_x * tokens, inner), BF16),
            pltpu.VMEM(weight.shape, BF16),
            pltpu.VMEM((2 * inner, SPAN), BF16),
            pltpu.SemaphoreType.DMA((3 * n_x + 1,)),
        ],
        flops=2 * n_x * tokens * inner * (STATE * 2 + weight.shape[0]),
        smem=1,
        vmem=4,
        limit=57 * 2**20,
        args=(
            place,
            bias,
            decay,
            group_gain.reshape(1, inner),
            entering.reshape(inner, SPAN),
            *mixed,
            *blocks,
            weight,
        ),
    )
    partial = (kept + lax.ppermute(sent, "core", ring(2, 1))).astype(BF16)
    partial = lax.all_to_all(partial, ("x", *TENSOR), 0, 0, tiled=True)
    rows = residual.shape[0]
    (done,) = call(
        functools.partial(finish_kernel, n_x=n_x, n_z=n_z),
        [jax.ShapeDtypeStruct(residual.shape, BF16)],
        scratch=[pltpu.VMEM(residual.shape, F32)],
        flops=10**6,
        smem=1,
        vmem=3,
        args=(late, partial.reshape(n_x, n_t // 2, 2, rows, weight.shape[0] // 2), residual, final_gain.reshape(1, -1)),
    )
    across = lax.ppermute(done, "yl", ring(2, 1))
    mine_two = jnp.stack([done, across])
    theirs_two = lax.ppermute(mine_two, "core", ring(2, 1))
    first_y, first_core = lax.axis_index("yl") == 0, lax.axis_index("core") == 0
    even = jnp.where(first_core, mine_two, theirs_two)
    odd = jnp.where(first_core, theirs_two, mine_two)
    low = jnp.where(first_y, jnp.stack([even[0], odd[0]]), jnp.stack([even[1], odd[1]]))
    high = jnp.where(first_y, jnp.stack([even[1], odd[1]]), jnp.stack([even[0], odd[0]]))
    return jnp.concatenate([low, high]).reshape(tokens, residual.shape[1])


def solution(mesh):
    fine = Mesh(mesh.devices.reshape(2, 8, 4, 2, 2), (*CONTEXT, *TENSOR))
    return jax.shard_map(
        on_device,
        mesh=fine,
        in_specs=(
            P(CONTEXT, TENSOR),
            P(CONTEXT, TENSOR),
            P(CONTEXT, TENSOR),
            P(CONTEXT, TENSOR),
            P(CONTEXT, TENSOR),
            P(TENSOR),
            P(TENSOR),
            P(TENSOR),
            P(TENSOR),
            P(TENSOR, None, None),
            P(TENSOR, CONTEXT),
            P((*CONTEXT, *TENSOR), None),
            P(),
        ),
        out_specs=P(CONTEXT, None),
        check_vma=False,
    )
```

```python
import functools

import jax
import jax.numpy as jnp
from jax import lax
from jax.experimental import pallas as pl
from jax.experimental.pallas import tpu as pltpu
from jax.sharding import Mesh, PartitionSpec as P

EPSILON = 1e-05
HIGHEST = lax.Precision.HIGHEST
SPAN = 128
STATE = 128
HEAD_DIM = 64
EXTRA = 8
BF16, F32 = jnp.bfloat16, jnp.float32
CONTEXT = ("yh", "z", "x")
TENSOR = ("yl", "core")
GROUPS = ("yh", "z")
VMEM_LIMIT = 14 * 2**20
VMEM_MOST = 61 * 2**20


def call(kernel, outs, *, scratch=(), flops=0, smem=0, vmem=0, hbm_outs=0, limit=VMEM_MOST, args=()):
    specs = [pl.BlockSpec(memory_space=pltpu.SMEM)] * smem
    specs += [pl.BlockSpec(memory_space=pltpu.VMEM)] * vmem
    specs += [pl.BlockSpec(memory_space=pltpu.HBM)] * (len(args) - smem - vmem)
    places = [pltpu.VMEM] * (len(outs) - hbm_outs) + [pltpu.HBM] * hbm_outs
    moved = sum(a.size * a.dtype.itemsize for a in (*args, *outs))
    return pl.pallas_call(
        kernel,
        out_shape=list(outs),
        in_specs=specs,
        out_specs=[pl.BlockSpec(memory_space=m) for m in places],
        scratch_shapes=scratch,
        compiler_params=pltpu.CompilerParams(
            vmem_limit_bytes=limit if len(args) > smem + vmem else VMEM_LIMIT
        ),
        cost_estimate=pl.CostEstimate(flops=flops, bytes_accessed=moved, transcendentals=0),
    )(*args)


def copies(pairs, semaphores, first=0):
    started = [pltpu.make_async_copy(a, b, semaphores.at[first + i]) for i, (a, b) in enumerate(pairs)]
    for copy in started:
        copy.start()
    return started


def dot(a, b, precision=None):
    return lax.dot_general(
        a, b, (((1,), (0,)), ((), ())), precision=precision, preferred_element_type=F32
    )


def as_column(row):
    square = (row.shape[1], row.shape[1])
    same = lax.broadcasted_iota(jnp.int32, square, 0) == lax.broadcasted_iota(jnp.int32, square, 1)
    return jnp.sum(jnp.where(same, jnp.broadcast_to(row, square), 0.0), axis=1, keepdims=True)


def steps_of(raw_t, bias, decay_log):
    v = raw_t.astype(F32) + as_column(bias)
    step = jnp.maximum(v, 0.0) + jnp.log1p(jnp.exp(-jnp.abs(v)))
    rows = lax.broadcasted_iota(jnp.int32, (SPAN, SPAN), 0)
    columns = lax.broadcasted_iota(jnp.int32, (SPAN, SPAN), 1)
    upper = jnp.where(rows <= columns, 1.0, 0.0).astype(F32)
    return step, dot(-jnp.exp(as_column(decay_log)) * step, upper, HIGHEST)


def split(a):
    high = a.astype(BF16)
    return high, (a - high.astype(F32)).astype(BF16)


def first_lanes(shape):
    return lax.broadcasted_iota(jnp.int32, shape, len(shape) - 1) < HEAD_DIM


def column(a, h):
    return jnp.broadcast_to(a[:, h : h + 1], (a.shape[0], 2 * HEAD_DIM))


def pair_row(a, pair):
    low = first_lanes((1, 2 * HEAD_DIM))
    return jnp.where(low, column(a[2 * pair : 2 * pair + 1], 0), column(a[2 * pair + 1 : 2 * pair + 2], 0))


def fresh_states(x_ref, b, step_t, cumulative_t, x_in=()):
    last = cumulative_t[:, SPAN - 1 : SPAN]
    weight = jnp.transpose(step_t * jnp.exp(last - cumulative_t))
    b_t = jnp.transpose(b)
    b_twice = jnp.concatenate([b_t, b_t], axis=1)
    low = first_lanes((SPAN, SPAN))
    pairs = x_ref.shape[1] // SPAN
    for pair in range(pairs):
        if x_in and pair % (pairs // len(x_in)) == 0:
            for copy in x_in[pair // (pairs // len(x_in))]:
                copy.wait()
        lanes = slice(pair * SPAN, (pair + 1) * SPAN)
        scale = jnp.where(low, column(weight, 2 * pair), column(weight, 2 * pair + 1))
        scaled = x_ref[:, lanes].astype(F32) * scale
        state = dot(b_twice, jnp.concatenate(split(scaled), axis=0))
        yield pair, state, pair_row(last, pair)


def states_kernel(x_hbm, gate_hbm, b_hbm, c_hbm, raw_hbm, bias_hbm, decay_hbm, out_ref, top_hbm, bottom_hbm, *scratch):
    packed_ref, bias_ref, decay_ref, semaphores = scratch
    inner, heads = x_hbm.shape[1], raw_hbm.shape[0]
    at = 2 * inner
    x_ref = packed_ref.at[:, :inner]
    gets = copies(
        [
            (raw_hbm, packed_ref.at[:heads, at + 2 * SPAN :]),
            (bias_hbm, bias_ref),
            (decay_hbm, decay_ref),
            (b_hbm, packed_ref.at[:, at : at + SPAN]),
            (x_hbm, x_ref),
            (c_hbm, packed_ref.at[:, at + SPAN : at + 2 * SPAN]),
            (gate_hbm, packed_ref.at[:, inner:at]),
        ],
        semaphores,
    )
    packed_ref[heads:, at + 2 * SPAN :] = jnp.zeros((SPAN - heads, SPAN), BF16)
    for copy in gets[:3]:
        copy.wait()
    step, cumulative = steps_of(packed_ref[:heads, at + 2 * SPAN :], bias_ref[...], decay_ref[...])
    for copy in gets[3:]:
        copy.wait()
    half = SPAN // 2
    puts = copies([(packed_ref.at[:half], top_hbm), (packed_ref.at[half:], bottom_hbm)], semaphores, len(gets))
    each = out_ref.shape[1] // SPAN
    for pair, state, log in fresh_states(x_ref, packed_ref[:, at : at + SPAN], step, cumulative):
        member, place = divmod(pair, each)
        out_ref[member, place * STATE : (place + 1) * STATE, :] = state
        out_ref[member, each * STATE + place : each * STATE + place + 1, :] = log
    for put in puts:
        put.wait()


def group_kernel(parts_ref, out_ref):
    members, rows, _ = parts_ref.shape
    pairs = rows // STATE
    slices, size = out_ref.shape[0], out_ref.shape[1] - EXTRA
    for pair in range(pairs):
        here = slice(pair * STATE, (pair + 1) * STATE)
        at = pairs * STATE + pair
        log = parts_ref[0, at : at + 1, :]
        state = parts_ref[0, here, :]
        for member in range(1, members):
            more = parts_ref[member, at : at + 1, :]
            state = jnp.exp(more) * state + parts_ref[member, here, :]
            log = log + more
        for i in range(STATE // size):
            out_ref[pair * (STATE // size) + i, :size, :] = state[i * size : (i + 1) * size]
            out_ref[pair * (STATE // size) + i, size:, :] = jnp.broadcast_to(log, (EXTRA, SPAN))


def enter_kernel(parts_ref, carry_ref, out_ref):
    size = out_ref.shape[1]
    run = carry_ref[...]
    for k in range(parts_ref.shape[0]):
        out_ref[k] = run
        run = jnp.exp(parts_ref[k, size : size + 1, :]) * run + parts_ref[k, :size, :]


def halves(pieces, columns, ref):
    half = SPAN // 2
    return [(pieces[0].at[:, columns], ref.at[:half]), (pieces[1].at[:, columns], ref.at[half:])]


def local_block(x_ref, coefs_ref, bias_ref, decay_ref, skip_ref, mixed_ref, state_ref, x_in=(), after=None):
    heads = bias_ref.shape[1]
    b, c = coefs_ref[:, :SPAN], coefs_ref[:, SPAN : 2 * SPAN]
    step_t, cumulative_t = steps_of(coefs_ref[:heads, 2 * SPAN :], bias_ref[...], decay_ref[...])
    cumulative = jnp.transpose(cumulative_t)
    scores = lax.dot_general(c, b, (((1,), (1,)), ((), ())), preferred_element_type=F32)
    rows = lax.broadcasted_iota(jnp.int32, (SPAN, SPAN), 0)
    columns = lax.broadcasted_iota(jnp.int32, (SPAN, SPAN), 1)
    causal = rows >= columns
    low = first_lanes((SPAN, SPAN))
    for pair, state, _ in fresh_states(x_ref, b, step_t, cumulative_t, x_in):
        lanes = slice(pair * SPAN, (pair + 1) * SPAN)
        state_ref[lanes, :] = state
        x = x_ref[:, lanes]
        weights = []
        for h in (2 * pair, 2 * pair + 1):
            gap = column(cumulative, h) - cumulative_t[h : h + 1, :]
            within = jnp.exp(jnp.where(causal, gap, -jnp.inf))
            weights.append(jnp.concatenate(split(scores * within * step_t[h : h + 1, :]), axis=1))
        both = dot(jnp.concatenate(weights, axis=0), jnp.concatenate([x, x], axis=0))
        mixed_ref[:, lanes] = jnp.where(low, both[:SPAN], both[SPAN:]) + skip_ref[:, lanes] * x.astype(F32)
        if after is not None:
            after(pair)
    return cumulative_t


def local_kernel(bias_ref, decay_ref, skip_ref, top_hbm, bottom_hbm, mixed_hbm, state_hbm, *scratch):
    x_ref, coefs_ref, mixed_ref, state_ref, gets, puts = scratch
    inner = x_ref.shape[1]
    step = inner // 4
    each = step // SPAN
    pieces = (top_hbm, bottom_hbm)
    coefs_in = copies(halves(pieces, slice(2 * inner, None), coefs_ref), gets)
    x_in = [
        copies(halves(pieces, pl.ds(i * step, step), x_ref.at[:, pl.ds(i * step, step)]), gets, 2 + 2 * i)
        for i in range(4)
    ]
    for copy in coefs_in:
        copy.wait()
    out = []

    def after(pair):
        if pair % each == each - 1:
            part = pl.ds(pair // each * step, step)
            moves = [(state_ref.at[part], state_hbm.at[part]), (mixed_ref.at[:, part], mixed_hbm.at[:, part])]
            out.extend(copies(moves, puts, len(out)))

    local_block(x_ref, coefs_ref, bias_ref, decay_ref, skip_ref, mixed_ref, state_ref, x_in, after)
    for copy in out:
        copy.wait()


def fold_kernel(n, place_ref, bias_ref, decay_ref, skip_ref, *refs):
    last = n - 1
    states, given, refs = refs[:last], refs[last : 2 * last], refs[2 * last :]
    blocks, out = refs[: 2 * n], refs[2 * n : 3 * n]
    x_ref, enter_ref, logs_ref, mixed_ref, coefs_ref, gets, puts = refs[3 * n :]
    inner, heads = mixed_ref.shape[2], bias_ref.shape[1]
    pairs = inner // SPAN
    coefs_in = [
        copies(halves(blocks[2 * i : 2 * i + 2], slice(2 * inner, None), coefs_ref.at[i]), gets, 2 * i)
        for i in reversed(range(n))
    ][::-1]
    x_in = copies(halves(blocks[2 * last :], slice(0, inner), x_ref), gets, 2 * n)
    state_in = copies([(states[i], enter_ref.at[place_ref[i]]) for i in range(last)], gets, 2 * n + 2)
    mixed_in = copies([(given[i], mixed_ref.at[i]) for i in range(last)], gets, 3 * n + 2)
    for i in reversed(range(n)):
        for copy in coefs_in[i]:
            copy.wait()
        place = place_ref[i]
        if i == last:
            state_ref = enter_ref.at[place]
            logs_ref[place] = local_block(
                x_ref, coefs_ref.at[i], bias_ref, decay_ref, skip_ref, mixed_ref.at[i], state_ref, [x_in]
            )
        else:
            logs_ref[place] = steps_of(coefs_ref[i, :heads, 2 * SPAN :], bias_ref[...], decay_ref[...])[1]
    for copy in state_in:
        copy.wait()
    for pair in range(pairs):
        lanes = slice(pair * SPAN, (pair + 1) * SPAN)
        run = jnp.zeros((SPAN, SPAN), F32)
        for p in range(n):
            fresh = enter_ref[p, lanes, :]
            enter_ref[p, lanes, :] = run
            run = jnp.exp(pair_row(logs_ref[p, :, SPAN - 1 :], pair)) * run + fresh
    low = first_lanes((SPAN, SPAN))
    out_copies = []
    for i in range(n):
        if i < last:
            mixed_in[i].wait()
        place = place_ref[i]
        cumulative = jnp.transpose(logs_ref[place])
        c = coefs_ref[i, :, SPAN : 2 * SPAN]
        c_twice = jnp.concatenate([c, c], axis=1)
        for pair in range(pairs):
            lanes = slice(pair * SPAN, (pair + 1) * SPAN)
            at = jnp.where(low, column(cumulative, 2 * pair), column(cumulative, 2 * pair + 1))
            carried = dot(c_twice, jnp.concatenate(split(enter_ref[place, lanes, :]), axis=0))
            mixed_ref[i, :, lanes] += carried * jnp.exp(at)
        out_copies += copies([(mixed_ref.at[i], out[i])], puts, i)
    for copy in out_copies:
        copy.wait()


def mix_kernel(n, place_ref, bias_ref, decay_ref, gain_ref, enter_ref, *refs):
    mixed, blocks, weight_hbm = refs[:n], refs[n : 3 * n], refs[3 * n]
    kept_ref, sent_ref, logs_ref, mixed_ref, block_ref, normed_ref, weight_ref, enter_two, semaphores = refs[3 * n + 1 :]
    inner, heads = mixed_ref.shape[2], bias_ref.shape[1]
    pairs = inner // SPAN
    coefs_in, gate_in, mixed_in = [], [], []
    for i in range(n):
        to = block_ref.at[i, :, pl.ds(inner, 3 * SPAN)]
        coefs_in += copies(halves(blocks[2 * i : 2 * i + 2], slice(2 * inner, None), to), semaphores, 2 * i)
    for i in range(n):
        to = block_ref.at[i, :, pl.ds(0, inner)]
        mixed_in += copies([(mixed[i], mixed_ref.at[i])], semaphores, 2 * n + i)
        gate_in.append(
            copies(halves(blocks[2 * i : 2 * i + 2], slice(inner, 2 * inner), to), semaphores, 3 * n + 2 * i)
        )
    (weight_in,) = copies([(weight_hbm, weight_ref)], semaphores, 5 * n)
    for copy in coefs_in:
        copy.wait()
    for i in range(n):
        raw_t = block_ref[i, :heads, inner + 2 * SPAN :]
        logs_ref[place_ref[i]] = steps_of(raw_t, bias_ref[...], decay_ref[...])[1]
    for pair in range(pairs):
        parts = split(enter_ref[pair * SPAN : (pair + 1) * SPAN, :])
        enter_two[2 * pair * SPAN : 2 * (pair + 1) * SPAN, :] = jnp.concatenate(parts, axis=0)
    before = jnp.zeros((heads, 1), F32)
    for p in range(n):
        here = logs_ref[p]
        logs_ref[p] = here + before
        before = before + here[:, SPAN - 1 :]
    low = first_lanes((SPAN, SPAN))
    for i in range(n):
        for copy in (mixed_in[i], *gate_in[i]):
            copy.wait()
        place = place_ref[i]
        cumulative = jnp.transpose(logs_ref[place])
        c = block_ref[i, :, inner + SPAN : inner + 2 * SPAN]
        c_twice = jnp.concatenate([c, c], axis=1)
        squares = jnp.zeros((SPAN, SPAN), F32)
        for pair in range(pairs):
            lanes = slice(pair * SPAN, (pair + 1) * SPAN)
            at = jnp.where(low, column(cumulative, 2 * pair), column(cumulative, 2 * pair + 1))
            carried = dot(c_twice, enter_two[2 * pair * SPAN : 2 * (pair + 1) * SPAN, :])
            mixer_out = mixed_ref[i, :, lanes] + carried * jnp.exp(at)
            gate = block_ref[i, :, lanes].astype(F32)
            gated = mixer_out * (gate / (1.0 + jnp.exp(-gate)))
            mixed_ref[i, :, lanes] = gated
            squares += gated * gated
        root = lax.rsqrt(jnp.sum(squares, axis=-1, keepdims=True) / inner + EPSILON)
        to = pl.ds(pl.multiple_of(place * SPAN, SPAN), SPAN)
        for pair in range(pairs):
            lanes = slice(pair * SPAN, (pair + 1) * SPAN)
            normed_ref[to, lanes] = (mixed_ref[i, :, lanes] * root * gain_ref[:, lanes]).astype(BF16)
    weight_in.wait()
    core, width = place_ref[n], kept_ref.shape[1]
    for ref, side in ((sent_ref, 1 - core), (kept_ref, core)):
        for tile in range(width // (2 * SPAN)):
            columns = slice(2 * tile * SPAN, 2 * (tile + 1) * SPAN)
            rows = pl.ds(pl.multiple_of(side * width + 2 * tile * SPAN, 2 * SPAN), 2 * SPAN)
            ref[:, columns] = lax.dot_general(
                normed_ref[...], weight_ref[rows, :], (((1,), (1,)), ((), ())), preferred_element_type=F32
            )


def finish_kernel(late_ref, parts_ref, residual_ref, gain_ref, out_ref, combined_ref, *, n_x, n_z):
    late = late_ref[0] > 0
    tokens = residual_ref.shape[0]
    sums = []
    for x in range(n_x):
        cores = []
        for core in range(parts_ref.shape[2]):
            total = parts_ref[x, 0, core].astype(F32)
            for y in range(1, parts_ref.shape[1]):
                total += parts_ref[x, y, core].astype(F32)
            cores.append(total)
        sums.append(jnp.concatenate(cores, axis=1))
    squares = jnp.zeros((tokens, 2 * HEAD_DIM), F32)
    for z in range(n_z):
        piece = slice(z * 2 * HEAD_DIM, (z + 1) * 2 * HEAD_DIM)
        own = [total[:, piece] for total in sums]
        swapped = [jnp.concatenate([a[:, HEAD_DIM:], a[:, :HEAD_DIM]], axis=1) for a in own]
        ordered = [jnp.where(late, b, a) for a, b in zip(own, swapped)]
        for yh in range(2):
            for x in range(0, n_x, 2):
                block = ((yh * n_z + z) * n_x + x) // 2
                lanes = slice(block * 2 * HEAD_DIM, (block + 1) * 2 * HEAD_DIM)
                half = slice(yh * HEAD_DIM, (yh + 1) * HEAD_DIM)
                both = jnp.concatenate([ordered[x][:, half], ordered[x + 1][:, half]], axis=1)
                combined = residual_ref[:, lanes].astype(F32) + both
                combined_ref[:, lanes] = combined
                squares += combined * combined
    root = lax.rsqrt(jnp.sum(squares, axis=-1, keepdims=True) / combined_ref.shape[1] + EPSILON)
    out_ref[...] = (combined_ref[...] * root * gain_ref[...]).astype(BF16)


def ring(n, by):
    return [(i, (i + by) % n) for i in range(n)]


def on_device(
    mixer_values,
    gate_values,
    input_coefs,
    output_coefs,
    step_raw,
    step_bias,
    decay_log,
    skip_gain,
    group_gain,
    carry_state,
    out_weight,
    residual,
    final_gain,
):
    tokens, inner = mixer_values.shape
    heads = step_raw.shape[1]
    n_z, n_x = lax.axis_size("z"), lax.axis_size("x")
    n_t = lax.axis_size("yl") * lax.axis_size("core")
    groups = 2 * n_z
    at_x = lax.axis_index("x")
    late = lax.axis_index("yh").astype(jnp.int32).reshape(1)
    bias, decay = step_bias.reshape(1, heads), decay_log.reshape(1, heads)
    skip = jnp.repeat(skip_gain, HEAD_DIM).reshape(1, inner)
    pairs = heads // 2
    quarter = inner // n_x
    size = quarter // groups
    packed = 2 * inner + 3 * SPAN

    half_block = jax.ShapeDtypeStruct((tokens // 2, packed), BF16)
    values = jax.ShapeDtypeStruct((tokens, inner), F32)

    weight = out_weight.T
    across = lax.ppermute(weight, "yh", ring(2, 1))

    states, top, bottom = call(
        states_kernel,
        [jax.ShapeDtypeStruct((n_x, quarter + EXTRA, SPAN), F32), half_block, half_block],
        scratch=[
            pltpu.VMEM((tokens, packed), BF16),
            pltpu.VMEM((1, heads), F32),
            pltpu.VMEM((1, heads), F32),
            pltpu.SemaphoreType.DMA((9,)),
        ],
        flops=2 * tokens * inner * STATE * 2,
        hbm_outs=2,
        args=(mixer_values, gate_values, input_coefs, output_coefs, step_raw.T, bias, decay),
    )
    parts = lax.all_to_all(states, "x", 0, 0, tiled=True)
    across, parts = lax.optimization_barrier((across, parts))
    weight = jnp.concatenate([weight, across], axis=0)
    weight = lax.all_gather(weight, "z", axis=0, tiled=True)

    parts, top, bottom = lax.optimization_barrier((parts, top, bottom))
    own = (top, bottom)
    left_top = lax.ppermute(top, "x", ring(n_x, 1))
    right_bottom = lax.ppermute(bottom, "x", ring(n_x, -1))
    place = (at_x + jnp.array([0, n_x - 1, 1, 2], jnp.int32)) % n_x
    place = jnp.concatenate([place, lax.axis_index("core").astype(jnp.int32).reshape(1)])

    def local(block):
        return call(
            local_kernel,
            [values, jax.ShapeDtypeStruct((inner, SPAN), F32)],
            scratch=[
                pltpu.VMEM((tokens, inner), BF16),
                pltpu.VMEM((tokens, 3 * SPAN), BF16),
                pltpu.VMEM((tokens, inner), F32),
                pltpu.VMEM((inner, SPAN), F32),
                pltpu.SemaphoreType.DMA((10,)),
                pltpu.SemaphoreType.DMA((8,)),
            ],
            flops=10**6,
            vmem=3,
            hbm_outs=2,
            args=(bias, decay, skip, *block),
        )

    (grouped,) = call(
        group_kernel,
        [jax.ShapeDtypeStruct((groups, size + EXTRA, SPAN), F32)],
        flops=10**6,
        vmem=1,
        args=(parts,),
    )
    parts = lax.all_to_all(grouped, GROUPS, 0, 0, tiled=True)
    own_local, top_later, bottom_later = lax.optimization_barrier((local(own), top, bottom))
    left_bottom = lax.ppermute(bottom_later, "x", ring(n_x, 1))
    right_top = lax.ppermute(top_later, "x", ring(n_x, -1))
    own_local, parts, left_top, right_bottom, place = lax.optimization_barrier(
        (own_local, parts, left_top, right_bottom, place)
    )
    left, right = (left_top, left_bottom), (right_top, right_bottom)
    mine = lax.axis_index(GROUPS)
    each = STATE // size
    carry = lax.dynamic_index_in_dim(
        carry_state.reshape(pairs, SPAN, STATE), at_x * (pairs // n_x) + mine // each, 0, False
    )
    carry = lax.dynamic_slice_in_dim(carry.T, (mine % each) * size, size, 0)
    (entering,) = call(
        enter_kernel,
        [jax.ShapeDtypeStruct((groups, size, SPAN), F32)],
        flops=10**6,
        vmem=2,
        args=(parts, carry),
    )
    entering, onward, back = lax.optimization_barrier((entering, left_top, right_bottom))
    far = (lax.ppermute(onward, "x", ring(n_x, 1)), lax.ppermute(back, "x", ring(n_x, -1)))
    entering = lax.all_to_all(entering, GROUPS, 0, 0, tiled=True).reshape(1, quarter, SPAN)
    entering, left_local, right_local, far = lax.optimization_barrier((entering, local(left), local(right), far))
    mixed, fresh = zip(own_local, left_local, right_local)
    entering = lax.all_to_all(jnp.broadcast_to(entering, (n_x, quarter, SPAN)), "x", 0, 0, tiled=True)

    blocks = (*own, *left, *right, *far)
    mixed = call(
        functools.partial(fold_kernel, n_x),
        [values] * n_x,
        scratch=[
            pltpu.VMEM((tokens, inner), BF16),
            pltpu.VMEM((n_x, inner, SPAN), F32),
            pltpu.VMEM((n_x, heads, SPAN), F32),
            pltpu.VMEM((n_x, tokens, inner), F32),
            pltpu.VMEM((n_x, tokens, 3 * SPAN), BF16),
            pltpu.SemaphoreType.DMA((4 * n_x + 2,)),
            pltpu.SemaphoreType.DMA((n_x,)),
        ],
        flops=2 * n_x * tokens * inner * STATE * 2,
        smem=1,
        vmem=3,
        hbm_outs=n_x,
        args=(place, bias, decay, skip, *fresh, *mixed, *blocks),
    )
    kept, sent = call(
        functools.partial(mix_kernel, n_x),
        [jax.ShapeDtypeStruct((n_x * tokens, weight.shape[0] // 2), F32)] * 2,
        scratch=[
            pltpu.VMEM((n_x, heads, SPAN), F32),
            pltpu.VMEM((n_x, tokens, inner), F32),
            pltpu.VMEM((n_x, tokens, packed - inner), BF16),
            pltpu.VMEM((n_x * tokens, inner), BF16),
            pltpu.VMEM(weight.shape, BF16),
            pltpu.VMEM((2 * inner, SPAN), BF16),
            pltpu.SemaphoreType.DMA((5 * n_x + 1,)),
        ],
        flops=2 * n_x * tokens * inner * (STATE * 2 + weight.shape[0]),
        smem=1,
        vmem=4,
        limit=57 * 2**20,
        args=(
            place,
            bias,
            decay,
            group_gain.reshape(1, inner),
            entering.reshape(inner, SPAN),
            *mixed,
            *blocks,
            weight,
        ),
    )
    partial = (kept + lax.ppermute(sent, "core", ring(2, 1))).astype(BF16)
    partial = lax.all_to_all(partial, ("x", *TENSOR), 0, 0, tiled=True)
    rows = residual.shape[0]
    (done,) = call(
        functools.partial(finish_kernel, n_x=n_x, n_z=n_z),
        [jax.ShapeDtypeStruct(residual.shape, BF16)],
        scratch=[pltpu.VMEM(residual.shape, F32)],
        flops=10**6,
        smem=1,
        vmem=3,
        args=(late, partial.reshape(n_x, n_t // 2, 2, rows, weight.shape[0] // 2), residual, final_gain.reshape(1, -1)),
    )
    across = lax.ppermute(done, "yl", ring(2, 1))
    mine_two = jnp.stack([done, across])
    theirs_two = lax.ppermute(mine_two, "core", ring(2, 1))
    first_y, first_core = lax.axis_index("yl") == 0, lax.axis_index("core") == 0
    even = jnp.where(first_core, mine_two, theirs_two)
    odd = jnp.where(first_core, theirs_two, mine_two)
    low = jnp.where(first_y, jnp.stack([even[0], odd[0]]), jnp.stack([even[1], odd[1]]))
    high = jnp.where(first_y, jnp.stack([even[1], odd[1]]), jnp.stack([even[0], odd[0]]))
    return jnp.concatenate([low, high]).reshape(tokens, residual.shape[1])


def solution(mesh):
    fine = Mesh(mesh.devices.reshape(2, 8, 4, 2, 2), (*CONTEXT, *TENSOR))
    return jax.shard_map(
        on_device,
        mesh=fine,
        in_specs=(
            P(CONTEXT, TENSOR),
            P(CONTEXT, TENSOR),
            P(CONTEXT, TENSOR),
            P(CONTEXT, TENSOR),
            P(CONTEXT, TENSOR),
            P(TENSOR),
            P(TENSOR),
            P(TENSOR),
            P(TENSOR),
            P(TENSOR, None, None),
            P(TENSOR, CONTEXT),
            P((*CONTEXT, *TENSOR), None),
            P(),
        ),
        out_specs=P(CONTEXT, None),
        check_vma=False,
    )
```

```python
import functools

import jax
import jax.numpy as jnp
from jax import lax
from jax.experimental import pallas as pl
from jax.experimental.pallas import tpu as pltpu
from jax.sharding import Mesh, PartitionSpec as P

EPSILON = 1e-05
HIGHEST = lax.Precision.HIGHEST
SPAN = 128
STATE = 128
HEAD_DIM = 64
EXTRA = 8
BF16, F32 = jnp.bfloat16, jnp.float32
CONTEXT = ("yh", "z", "x")
TENSOR = ("yl", "core")
GROUPS = ("yh", "z")
VMEM_LIMIT = 14 * 2**20
VMEM_MOST = 61 * 2**20


def call(kernel, outs, *, scratch=(), flops=0, smem=0, vmem=0, hbm_outs=0, limit=VMEM_MOST, args=()):
    specs = [pl.BlockSpec(memory_space=pltpu.SMEM)] * smem
    specs += [pl.BlockSpec(memory_space=pltpu.VMEM)] * vmem
    specs += [pl.BlockSpec(memory_space=pltpu.HBM)] * (len(args) - smem - vmem)
    places = [pltpu.VMEM] * (len(outs) - hbm_outs) + [pltpu.HBM] * hbm_outs
    moved = sum(a.size * a.dtype.itemsize for a in (*args, *outs))
    return pl.pallas_call(
        kernel,
        out_shape=list(outs),
        in_specs=specs,
        out_specs=[pl.BlockSpec(memory_space=m) for m in places],
        scratch_shapes=scratch,
        compiler_params=pltpu.CompilerParams(
            vmem_limit_bytes=limit if len(args) > smem + vmem else VMEM_LIMIT
        ),
        cost_estimate=pl.CostEstimate(flops=flops, bytes_accessed=moved, transcendentals=0),
    )(*args)


def copies(pairs, semaphores, first=0):
    started = [pltpu.make_async_copy(a, b, semaphores.at[first + i]) for i, (a, b) in enumerate(pairs)]
    for copy in started:
        copy.start()
    return started


def dot(a, b, precision=None):
    return lax.dot_general(
        a, b, (((1,), (0,)), ((), ())), precision=precision, preferred_element_type=F32
    )


def as_column(row):
    square = (row.shape[1], row.shape[1])
    same = lax.broadcasted_iota(jnp.int32, square, 0) == lax.broadcasted_iota(jnp.int32, square, 1)
    return jnp.sum(jnp.where(same, jnp.broadcast_to(row, square), 0.0), axis=1, keepdims=True)


def steps_of(raw_t, bias, decay_log):
    v = raw_t.astype(F32) + as_column(bias)
    step = jnp.maximum(v, 0.0) + jnp.log1p(jnp.exp(-jnp.abs(v)))
    rows = lax.broadcasted_iota(jnp.int32, (SPAN, SPAN), 0)
    columns = lax.broadcasted_iota(jnp.int32, (SPAN, SPAN), 1)
    upper = jnp.where(rows <= columns, 1.0, 0.0).astype(F32)
    return step, dot(-jnp.exp(as_column(decay_log)) * step, upper, HIGHEST)


def split(a):
    high = a.astype(BF16)
    return high, (a - high.astype(F32)).astype(BF16)


def first_lanes(shape):
    return lax.broadcasted_iota(jnp.int32, shape, len(shape) - 1) < HEAD_DIM


def column(a, h):
    return jnp.broadcast_to(a[:, h : h + 1], (a.shape[0], 2 * HEAD_DIM))


def pair_row(a, pair):
    low = first_lanes((1, 2 * HEAD_DIM))
    return jnp.where(low, column(a[2 * pair : 2 * pair + 1], 0), column(a[2 * pair + 1 : 2 * pair + 2], 0))


def fresh_states(x_ref, b, step_t, cumulative_t, x_in=()):
    last = cumulative_t[:, SPAN - 1 : SPAN]
    weight = jnp.transpose(step_t * jnp.exp(last - cumulative_t))
    b_t = jnp.transpose(b)
    b_twice = jnp.concatenate([b_t, b_t], axis=1)
    low = first_lanes((SPAN, SPAN))
    pairs = x_ref.shape[1] // SPAN
    for pair in range(pairs):
        if x_in and pair % (pairs // len(x_in)) == 0:
            for copy in x_in[pair // (pairs // len(x_in))]:
                copy.wait()
        lanes = slice(pair * SPAN, (pair + 1) * SPAN)
        scale = jnp.where(low, column(weight, 2 * pair), column(weight, 2 * pair + 1))
        scaled = x_ref[:, lanes].astype(F32) * scale
        state = dot(b_twice, jnp.concatenate(split(scaled), axis=0))
        yield pair, state, pair_row(last, pair)


def states_kernel(x_hbm, gate_hbm, b_hbm, c_hbm, raw_hbm, bias_hbm, decay_hbm, out_ref, top_hbm, bottom_hbm, *scratch):
    packed_ref, bias_ref, decay_ref, semaphores = scratch
    inner, heads = x_hbm.shape[1], raw_hbm.shape[0]
    at = 2 * inner
    x_ref = packed_ref.at[:, :inner]
    gets = copies(
        [
            (raw_hbm, packed_ref.at[:heads, at + 2 * SPAN :]),
            (bias_hbm, bias_ref),
            (decay_hbm, decay_ref),
            (b_hbm, packed_ref.at[:, at : at + SPAN]),
            (x_hbm, x_ref),
            (c_hbm, packed_ref.at[:, at + SPAN : at + 2 * SPAN]),
            (gate_hbm, packed_ref.at[:, inner:at]),
        ],
        semaphores,
    )
    packed_ref[heads:, at + 2 * SPAN :] = jnp.zeros((SPAN - heads, SPAN), BF16)
    for copy in gets[:3]:
        copy.wait()
    step, cumulative = steps_of(packed_ref[:heads, at + 2 * SPAN :], bias_ref[...], decay_ref[...])
    for copy in gets[3:]:
        copy.wait()
    half = SPAN // 2
    puts = copies([(packed_ref.at[:half], top_hbm), (packed_ref.at[half:], bottom_hbm)], semaphores, len(gets))
    each = out_ref.shape[1] // SPAN
    for pair, state, log in fresh_states(x_ref, packed_ref[:, at : at + SPAN], step, cumulative):
        member, place = divmod(pair, each)
        out_ref[member, place * STATE : (place + 1) * STATE, :] = state
        out_ref[member, each * STATE + place : each * STATE + place + 1, :] = log
    for put in puts:
        put.wait()


def group_kernel(parts_ref, out_ref):
    members, rows, _ = parts_ref.shape
    pairs = rows // STATE
    slices, size = out_ref.shape[0], out_ref.shape[1] - EXTRA
    for pair in range(pairs):
        here = slice(pair * STATE, (pair + 1) * STATE)
        at = pairs * STATE + pair
        log = parts_ref[0, at : at + 1, :]
        state = parts_ref[0, here, :]
        for member in range(1, members):
            more = parts_ref[member, at : at + 1, :]
            state = jnp.exp(more) * state + parts_ref[member, here, :]
            log = log + more
        for i in range(STATE // size):
            out_ref[pair * (STATE // size) + i, :size, :] = state[i * size : (i + 1) * size]
            out_ref[pair * (STATE // size) + i, size:, :] = jnp.broadcast_to(log, (EXTRA, SPAN))


def enter_kernel(parts_ref, carry_ref, out_ref):
    size = out_ref.shape[1]
    run = carry_ref[...]
    for k in range(parts_ref.shape[0]):
        out_ref[k] = run
        run = jnp.exp(parts_ref[k, size : size + 1, :]) * run + parts_ref[k, :size, :]


def halves(pieces, columns, ref):
    half = SPAN // 2
    return [(pieces[0].at[:, columns], ref.at[:half]), (pieces[1].at[:, columns], ref.at[half:])]


def local_block(x_ref, coefs_ref, bias_ref, decay_ref, skip_ref, mixed_ref, state_ref, x_in=(), after=None):
    heads = bias_ref.shape[1]
    b, c = coefs_ref[:, :SPAN], coefs_ref[:, SPAN : 2 * SPAN]
    step_t, cumulative_t = steps_of(coefs_ref[:heads, 2 * SPAN :], bias_ref[...], decay_ref[...])
    cumulative = jnp.transpose(cumulative_t)
    scores = lax.dot_general(c, b, (((1,), (1,)), ((), ())), preferred_element_type=F32)
    rows = lax.broadcasted_iota(jnp.int32, (SPAN, SPAN), 0)
    columns = lax.broadcasted_iota(jnp.int32, (SPAN, SPAN), 1)
    causal = rows >= columns
    low = first_lanes((SPAN, SPAN))
    for pair, state, _ in fresh_states(x_ref, b, step_t, cumulative_t, x_in):
        lanes = slice(pair * SPAN, (pair + 1) * SPAN)
        state_ref[lanes, :] = state
        x = x_ref[:, lanes]
        weights = []
        for h in (2 * pair, 2 * pair + 1):
            gap = column(cumulative, h) - cumulative_t[h : h + 1, :]
            within = jnp.exp(jnp.where(causal, gap, -jnp.inf))
            weights.append(jnp.concatenate(split(scores * within * step_t[h : h + 1, :]), axis=1))
        both = dot(jnp.concatenate(weights, axis=0), jnp.concatenate([x, x], axis=0))
        mixed_ref[:, lanes] = jnp.where(low, both[:SPAN], both[SPAN:]) + skip_ref[:, lanes] * x.astype(F32)
        if after is not None:
            after(pair)
    return cumulative_t


def local_kernel(bias_ref, decay_ref, skip_ref, top_hbm, bottom_hbm, mixed_hbm, state_hbm, *scratch):
    x_ref, coefs_ref, mixed_ref, state_ref, gets, puts = scratch
    inner = x_ref.shape[1]
    step = inner // 4
    each = step // SPAN
    pieces = (top_hbm, bottom_hbm)
    coefs_in = copies(halves(pieces, slice(2 * inner, None), coefs_ref), gets)
    x_in = [
        copies(halves(pieces, pl.ds(i * step, step), x_ref.at[:, pl.ds(i * step, step)]), gets, 2 + 2 * i)
        for i in range(4)
    ]
    for copy in coefs_in:
        copy.wait()
    out = []

    def after(pair):
        if pair % each == each - 1:
            part = pl.ds(pair // each * step, step)
            moves = [(state_ref.at[part], state_hbm.at[part]), (mixed_ref.at[:, part], mixed_hbm.at[:, part])]
            out.extend(copies(moves, puts, len(out)))

    local_block(x_ref, coefs_ref, bias_ref, decay_ref, skip_ref, mixed_ref, state_ref, x_in, after)
    for copy in out:
        copy.wait()


def fold_kernel(n, place_ref, bias_ref, decay_ref, skip_ref, *refs):
    last = n - 1
    states, given, refs = refs[:last], refs[last : 2 * last], refs[2 * last :]
    blocks, out = refs[: 2 * n], refs[2 * n : 3 * n]
    x_ref, enter_ref, logs_ref, mixed_ref, coefs_ref, gets, puts = refs[3 * n :]
    inner, heads = mixed_ref.shape[2], bias_ref.shape[1]
    pairs = inner // SPAN
    coefs_in = [
        copies(halves(blocks[2 * i : 2 * i + 2], slice(2 * inner, None), coefs_ref.at[i]), gets, 2 * i)
        for i in reversed(range(n))
    ][::-1]
    x_in = copies(halves(blocks[2 * last :], slice(0, inner), x_ref), gets, 2 * n)
    state_in = copies([(states[i], enter_ref.at[place_ref[i]]) for i in range(last)], gets, 2 * n + 2)
    mixed_in = copies([(given[i], mixed_ref.at[i]) for i in range(last)], gets, 3 * n + 2)
    for i in reversed(range(n)):
        for copy in coefs_in[i]:
            copy.wait()
        place = place_ref[i]
        if i == last:
            state_ref = enter_ref.at[place]
            logs_ref[place] = local_block(
                x_ref, coefs_ref.at[i], bias_ref, decay_ref, skip_ref, mixed_ref.at[i], state_ref, [x_in]
            )
        else:
            logs_ref[place] = steps_of(coefs_ref[i, :heads, 2 * SPAN :], bias_ref[...], decay_ref[...])[1]
    for copy in state_in:
        copy.wait()
    for pair in range(pairs):
        lanes = slice(pair * SPAN, (pair + 1) * SPAN)
        run = jnp.zeros((SPAN, SPAN), F32)
        for p in range(n):
            fresh = enter_ref[p, lanes, :]
            enter_ref[p, lanes, :] = run
            run = jnp.exp(pair_row(logs_ref[p, :, SPAN - 1 :], pair)) * run + fresh
    low = first_lanes((SPAN, SPAN))
    out_copies = []
    for i in range(n):
        if i < last:
            mixed_in[i].wait()
        place = place_ref[i]
        cumulative = jnp.transpose(logs_ref[place])
        c = coefs_ref[i, :, SPAN : 2 * SPAN]
        c_twice = jnp.concatenate([c, c], axis=1)
        for pair in range(pairs):
            lanes = slice(pair * SPAN, (pair + 1) * SPAN)
            at = jnp.where(low, column(cumulative, 2 * pair), column(cumulative, 2 * pair + 1))
            carried = dot(c_twice, jnp.concatenate(split(enter_ref[place, lanes, :]), axis=0))
            mixed_ref[i, :, lanes] += carried * jnp.exp(at)
        out_copies += copies([(mixed_ref.at[i], out[i])], puts, i)
    for copy in out_copies:
        copy.wait()


def mix_kernel(n, place_ref, bias_ref, decay_ref, gain_ref, enter_ref, *refs):
    mixed, blocks, weight_hbm = refs[:n], refs[n : 3 * n], refs[3 * n]
    kept_ref, sent_ref, logs_ref, mixed_ref, block_ref, normed_ref, weight_ref, enter_two, semaphores = refs[3 * n + 1 :]
    inner, heads = mixed_ref.shape[2], bias_ref.shape[1]
    pairs = inner // SPAN
    coefs_in, gate_in, mixed_in = [], [], []
    for i in range(n):
        to = block_ref.at[i, :, pl.ds(inner, 3 * SPAN)]
        coefs_in += copies(halves(blocks[2 * i : 2 * i + 2], slice(2 * inner, None), to), semaphores, 2 * i)
    for i in range(n):
        to = block_ref.at[i, :, pl.ds(0, inner)]
        mixed_in += copies([(mixed[i], mixed_ref.at[i])], semaphores, 2 * n + i)
        gate_in.append(
            copies(halves(blocks[2 * i : 2 * i + 2], slice(inner, 2 * inner), to), semaphores, 3 * n + 2 * i)
        )
    for copy in coefs_in:
        copy.wait()
    for i in range(n):
        raw_t = block_ref[i, :heads, inner + 2 * SPAN :]
        logs_ref[place_ref[i]] = steps_of(raw_t, bias_ref[...], decay_ref[...])[1]
    (weight_in,) = copies([(weight_hbm, weight_ref)], semaphores, 5 * n)
    for pair in range(pairs):
        parts = split(enter_ref[pair * SPAN : (pair + 1) * SPAN, :])
        enter_two[2 * pair * SPAN : 2 * (pair + 1) * SPAN, :] = jnp.concatenate(parts, axis=0)
    before = jnp.zeros((heads, 1), F32)
    for p in range(n):
        here = logs_ref[p]
        logs_ref[p] = here + before
        before = before + here[:, SPAN - 1 :]
    low = first_lanes((SPAN, SPAN))
    for i in range(n):
        for copy in (mixed_in[i], *gate_in[i]):
            copy.wait()
        place = place_ref[i]
        cumulative = jnp.transpose(logs_ref[place])
        c = block_ref[i, :, inner + SPAN : inner + 2 * SPAN]
        c_twice = jnp.concatenate([c, c], axis=1)
        squares = jnp.zeros((SPAN, SPAN), F32)
        for pair in range(pairs):
            lanes = slice(pair * SPAN, (pair + 1) * SPAN)
            at = jnp.where(low, column(cumulative, 2 * pair), column(cumulative, 2 * pair + 1))
            carried = dot(c_twice, enter_two[2 * pair * SPAN : 2 * (pair + 1) * SPAN, :])
            mixer_out = mixed_ref[i, :, lanes] + carried * jnp.exp(at)
            gate = block_ref[i, :, lanes].astype(F32)
            gated = mixer_out * (gate / (1.0 + jnp.exp(-gate)))
            mixed_ref[i, :, lanes] = gated
            squares += gated * gated
        root = lax.rsqrt(jnp.sum(squares, axis=-1, keepdims=True) / inner + EPSILON)
        to = pl.ds(pl.multiple_of(place * SPAN, SPAN), SPAN)
        for pair in range(pairs):
            lanes = slice(pair * SPAN, (pair + 1) * SPAN)
            normed_ref[to, lanes] = (mixed_ref[i, :, lanes] * root * gain_ref[:, lanes]).astype(BF16)
    weight_in.wait()
    core, width = place_ref[n], kept_ref.shape[1]
    for ref, side in ((sent_ref, 1 - core), (kept_ref, core)):
        for tile in range(width // (2 * SPAN)):
            columns = slice(2 * tile * SPAN, 2 * (tile + 1) * SPAN)
            rows = pl.ds(pl.multiple_of(side * width + 2 * tile * SPAN, 2 * SPAN), 2 * SPAN)
            ref[:, columns] = lax.dot_general(
                normed_ref[...], weight_ref[rows, :], (((1,), (1,)), ((), ())), preferred_element_type=F32
            )


def finish_kernel(late_ref, parts_ref, residual_ref, gain_ref, out_ref, combined_ref, *, n_x, n_z):
    late = late_ref[0] > 0
    tokens = residual_ref.shape[0]
    sums = []
    for x in range(n_x):
        cores = []
        for core in range(parts_ref.shape[2]):
            total = parts_ref[x, 0, core].astype(F32)
            for y in range(1, parts_ref.shape[1]):
                total += parts_ref[x, y, core].astype(F32)
            cores.append(total)
        sums.append(jnp.concatenate(cores, axis=1))
    squares = jnp.zeros((tokens, 2 * HEAD_DIM), F32)
    for z in range(n_z):
        piece = slice(z * 2 * HEAD_DIM, (z + 1) * 2 * HEAD_DIM)
        own = [total[:, piece] for total in sums]
        swapped = [jnp.concatenate([a[:, HEAD_DIM:], a[:, :HEAD_DIM]], axis=1) for a in own]
        ordered = [jnp.where(late, b, a) for a, b in zip(own, swapped)]
        for yh in range(2):
            for x in range(0, n_x, 2):
                block = ((yh * n_z + z) * n_x + x) // 2
                lanes = slice(block * 2 * HEAD_DIM, (block + 1) * 2 * HEAD_DIM)
                half = slice(yh * HEAD_DIM, (yh + 1) * HEAD_DIM)
                both = jnp.concatenate([ordered[x][:, half], ordered[x + 1][:, half]], axis=1)
                combined = residual_ref[:, lanes].astype(F32) + both
                combined_ref[:, lanes] = combined
                squares += combined * combined
    root = lax.rsqrt(jnp.sum(squares, axis=-1, keepdims=True) / combined_ref.shape[1] + EPSILON)
    out_ref[...] = (combined_ref[...] * root * gain_ref[...]).astype(BF16)


def ring(n, by):
    return [(i, (i + by) % n) for i in range(n)]


def on_device(
    mixer_values,
    gate_values,
    input_coefs,
    output_coefs,
    step_raw,
    step_bias,
    decay_log,
    skip_gain,
    group_gain,
    carry_state,
    out_weight,
    residual,
    final_gain,
):
    tokens, inner = mixer_values.shape
    heads = step_raw.shape[1]
    n_z, n_x = lax.axis_size("z"), lax.axis_size("x")
    n_t = lax.axis_size("yl") * lax.axis_size("core")
    groups = 2 * n_z
    at_x = lax.axis_index("x")
    late = lax.axis_index("yh").astype(jnp.int32).reshape(1)
    bias, decay = step_bias.reshape(1, heads), decay_log.reshape(1, heads)
    skip = jnp.repeat(skip_gain, HEAD_DIM).reshape(1, inner)
    pairs = heads // 2
    quarter = inner // n_x
    size = quarter // groups
    packed = 2 * inner + 3 * SPAN

    half_block = jax.ShapeDtypeStruct((tokens // 2, packed), BF16)
    values = jax.ShapeDtypeStruct((tokens, inner), F32)

    weight = out_weight.T
    across = lax.ppermute(weight, "yh", ring(2, 1))

    states, top, bottom = call(
        states_kernel,
        [jax.ShapeDtypeStruct((n_x, quarter + EXTRA, SPAN), F32), half_block, half_block],
        scratch=[
            pltpu.VMEM((tokens, packed), BF16),
            pltpu.VMEM((1, heads), F32),
            pltpu.VMEM((1, heads), F32),
            pltpu.SemaphoreType.DMA((9,)),
        ],
        flops=2 * tokens * inner * STATE * 2,
        hbm_outs=2,
        args=(mixer_values, gate_values, input_coefs, output_coefs, step_raw.T, bias, decay),
    )
    parts = lax.all_to_all(states, "x", 0, 0, tiled=True)
    across, parts = lax.optimization_barrier((across, parts))
    weight = jnp.concatenate([weight, across], axis=0)
    weight = lax.all_gather(weight, "z", axis=0, tiled=True)

    parts, top, bottom = lax.optimization_barrier((parts, top, bottom))
    own = (top, bottom)
    left_top = lax.ppermute(top, "x", ring(n_x, 1))
    right_bottom = lax.ppermute(bottom, "x", ring(n_x, -1))
    place = (at_x + jnp.array([0, n_x - 1, 1, 2], jnp.int32)) % n_x
    place = jnp.concatenate([place, lax.axis_index("core").astype(jnp.int32).reshape(1)])

    def local(block):
        return call(
            local_kernel,
            [values, jax.ShapeDtypeStruct((inner, SPAN), F32)],
            scratch=[
                pltpu.VMEM((tokens, inner), BF16),
                pltpu.VMEM((tokens, 3 * SPAN), BF16),
                pltpu.VMEM((tokens, inner), F32),
                pltpu.VMEM((inner, SPAN), F32),
                pltpu.SemaphoreType.DMA((10,)),
                pltpu.SemaphoreType.DMA((8,)),
            ],
            flops=10**6,
            vmem=3,
            hbm_outs=2,
            args=(bias, decay, skip, *block),
        )

    (grouped,) = call(
        group_kernel,
        [jax.ShapeDtypeStruct((groups, size + EXTRA, SPAN), F32)],
        flops=10**6,
        vmem=1,
        args=(parts,),
    )
    parts = lax.all_to_all(grouped, GROUPS, 0, 0, tiled=True)
    own_local, top_later, bottom_later = lax.optimization_barrier((local(own), top, bottom))
    left_bottom = lax.ppermute(bottom_later, "x", ring(n_x, 1))
    right_top = lax.ppermute(top_later, "x", ring(n_x, -1))
    own_local, parts, left_top, right_bottom, place = lax.optimization_barrier(
        (own_local, parts, left_top, right_bottom, place)
    )
    left, right = (left_top, left_bottom), (right_top, right_bottom)
    mine = lax.axis_index(GROUPS)
    each = STATE // size
    carry = lax.dynamic_index_in_dim(
        carry_state.reshape(pairs, SPAN, STATE), at_x * (pairs // n_x) + mine // each, 0, False
    )
    carry = lax.dynamic_slice_in_dim(carry.T, (mine % each) * size, size, 0)
    (entering,) = call(
        enter_kernel,
        [jax.ShapeDtypeStruct((groups, size, SPAN), F32)],
        flops=10**6,
        vmem=2,
        args=(parts, carry),
    )
    entering, onward, back = lax.optimization_barrier((entering, left_top, right_bottom))
    far = (lax.ppermute(onward, "x", ring(n_x, 1)), lax.ppermute(back, "x", ring(n_x, -1)))
    entering = lax.all_to_all(entering, GROUPS, 0, 0, tiled=True).reshape(1, quarter, SPAN)
    entering, left_local, right_local, far = lax.optimization_barrier((entering, local(left), local(right), far))
    mixed, fresh = zip(own_local, left_local, right_local)
    entering = lax.all_to_all(jnp.broadcast_to(entering, (n_x, quarter, SPAN)), "x", 0, 0, tiled=True)

    blocks = (*own, *left, *right, *far)
    mixed = call(
        functools.partial(fold_kernel, n_x),
        [values] * n_x,
        scratch=[
            pltpu.VMEM((tokens, inner), BF16),
            pltpu.VMEM((n_x, inner, SPAN), F32),
            pltpu.VMEM((n_x, heads, SPAN), F32),
            pltpu.VMEM((n_x, tokens, inner), F32),
            pltpu.VMEM((n_x, tokens, 3 * SPAN), BF16),
            pltpu.SemaphoreType.DMA((4 * n_x + 2,)),
            pltpu.SemaphoreType.DMA((n_x,)),
        ],
        flops=2 * n_x * tokens * inner * STATE * 2,
        smem=1,
        vmem=3,
        hbm_outs=n_x,
        args=(place, bias, decay, skip, *fresh, *mixed, *blocks),
    )
    kept, sent = call(
        functools.partial(mix_kernel, n_x),
        [jax.ShapeDtypeStruct((n_x * tokens, weight.shape[0] // 2), F32)] * 2,
        scratch=[
            pltpu.VMEM((n_x, heads, SPAN), F32),
            pltpu.VMEM((n_x, tokens, inner), F32),
            pltpu.VMEM((n_x, tokens, packed - inner), BF16),
            pltpu.VMEM((n_x * tokens, inner), BF16),
            pltpu.VMEM(weight.shape, BF16),
            pltpu.VMEM((2 * inner, SPAN), BF16),
            pltpu.SemaphoreType.DMA((5 * n_x + 1,)),
        ],
        flops=2 * n_x * tokens * inner * (STATE * 2 + weight.shape[0]),
        smem=1,
        vmem=4,
        limit=57 * 2**20,
        args=(
            place,
            bias,
            decay,
            group_gain.reshape(1, inner),
            entering.reshape(inner, SPAN),
            *mixed,
            *blocks,
            weight,
        ),
    )
    partial = (kept + lax.ppermute(sent, "core", ring(2, 1))).astype(BF16)
    partial = lax.all_to_all(partial, ("x", *TENSOR), 0, 0, tiled=True)
    rows = residual.shape[0]
    (done,) = call(
        functools.partial(finish_kernel, n_x=n_x, n_z=n_z),
        [jax.ShapeDtypeStruct(residual.shape, BF16)],
        scratch=[pltpu.VMEM(residual.shape, F32)],
        flops=10**6,
        smem=1,
        vmem=3,
        args=(late, partial.reshape(n_x, n_t // 2, 2, rows, weight.shape[0] // 2), residual, final_gain.reshape(1, -1)),
    )
    across = lax.ppermute(done, "yl", ring(2, 1))
    mine_two = jnp.stack([done, across])
    theirs_two = lax.ppermute(mine_two, "core", ring(2, 1))
    first_y, first_core = lax.axis_index("yl") == 0, lax.axis_index("core") == 0
    even = jnp.where(first_core, mine_two, theirs_two)
    odd = jnp.where(first_core, theirs_two, mine_two)
    low = jnp.where(first_y, jnp.stack([even[0], odd[0]]), jnp.stack([even[1], odd[1]]))
    high = jnp.where(first_y, jnp.stack([even[1], odd[1]]), jnp.stack([even[0], odd[0]]))
    return jnp.concatenate([low, high]).reshape(tokens, residual.shape[1])


def solution(mesh):
    fine = Mesh(mesh.devices.reshape(2, 8, 4, 2, 2), (*CONTEXT, *TENSOR))
    return jax.shard_map(
        on_device,
        mesh=fine,
        in_specs=(
            P(CONTEXT, TENSOR),
            P(CONTEXT, TENSOR),
            P(CONTEXT, TENSOR),
            P(CONTEXT, TENSOR),
            P(CONTEXT, TENSOR),
            P(TENSOR),
            P(TENSOR),
            P(TENSOR),
            P(TENSOR),
            P(TENSOR, None, None),
            P(TENSOR, CONTEXT),
            P((*CONTEXT, *TENSOR), None),
            P(),
        ),
        out_specs=P(CONTEXT, None),
        check_vma=False,
    )
```
